32 devices in a mesh: section: 2 (over core), dp: 16 (over z, y, x).
Axes of the slice: x: 2, y: 2, z: 4, core: 2. Of those that a mesh axis runs over, the one named last changes fastest.
Arguments:
- tokens: bfloat16 [64, 256, 1024], P('dp'), may hold values from -12 to 12
- clip_frames: int32 [64], P('dp'), may hold values from 4 to 16, as said below
- cotangent: bfloat16 [64, 256, 1024], P('dp'), may hold values from -12 to 12
- embed: bfloat16 [2, 256, 1024], P('section'), may hold values from -6 to 6
- norm_params: float32 [2, 6, 1024], P('section'), may hold values from -1.2 to 1.6
- w_qkv: bfloat16 [2, 1024, 3072], P('section'), may hold values from -0.1875 to 0.1875
- w_out: bfloat16 [2, 1024, 1024], P('section'), may hold values from -0.75 to 0.75
- w_up: bfloat16 [2, 1024, 4096], P('section'), may hold values from -0.1875 to 0.1875
- w_down: bfloat16 [2, 4096, 1024], P('section'), may hold values from -0.09375 to 0.09375
Outputs:
- section_out: float32 [2, 64, 256, 1024], P('section', 'dp')
- section_grad: float32 [2, 64, 256, 1024], P('section', 'dp')
- grad_qkv: float32 [2, 1024, 3072], P('section')
- grad_out: float32 [2, 1024, 1024], P('section')
- grad_up: float32 [2, 1024, 4096], P('section')
- grad_down: float32 [2, 4096, 1024], P('section')
- grad_norm_params: float32 [2, 6, 1024], P('section')
- grad_embed: float32 [2, 256, 1024], P('section')
- norms: float32 [2, 64], P('section', 'dp')
The draws below stay inside these ranges and needn't reach their ends.
Inputs may be any that keep to these rules, and one draw needn't show every extreme that they name: `clip_frames`: each entry is 4 or 16.
All inputs are finite; a program needn't handle non-finite values.
Results may differ from the reference program's by a relative error of at most 0.015.
Values may be sent and summed in bfloat16 or wider, within the bound.
A program may use at most 320 MiB of HBM per device.

```python
import jax
import jax.numpy as jnp
from jax import lax

D = 1024
HEADS = 8
HEAD = 128
FF = 4096
SLOTS = 256
GROUPS = 64


def draw_tokens(key, part):
    key = jax.random.fold_in(key, 11)
    noise_key = jax.random.fold_in(key, 0)
    ramp_up = 1.0 + 2.0 * jnp.arange(GROUPS, dtype=jnp.float32) / max(GROUPS - 1, 1)
    noise = jnp.clip(jax.random.normal(noise_key, (GROUPS, SLOTS, D), jnp.float32), -4.0, 4.0)
    return (noise * ramp_up[:, None, None]).astype(jnp.bfloat16)


def draw_cotangent(key, part):
    key = jax.random.fold_in(key, 14)
    noise_key = jax.random.fold_in(key, 0)
    position = jnp.arange(GROUPS, dtype=jnp.float32) / max(GROUPS - 1, 1)
    noise = jnp.clip(jax.random.normal(noise_key, (GROUPS, SLOTS, D), jnp.float32), -4.0, 4.0)
    ramp_up = 1.0 + 2.0 * position
    return (noise * ramp_up[:, None, None]).astype(jnp.bfloat16)


def draw_clip_frames(key, part):
    key = jax.random.fold_in(key, 12)
    scores = jax.random.randint(key, (GROUPS,), 0, GROUPS)
    longer = scores < jnp.arange(GROUPS, dtype=jnp.int32)
    frames = jnp.where(longer, 16, 4).astype(jnp.int32)
    frames = frames.at[0].set(4)
    return frames.at[GROUPS - 1].set(16)


def draw_norm_params(key, part):
    key = jax.random.fold_in(key, 13)
    noise = jnp.clip(jax.random.normal(key, (2, 6, D), jnp.float32), -4.0, 4.0)
    even_rows = (jnp.arange(6) % 2 == 0)[None, :, None]
    return jnp.where(even_rows, 1.0 + 0.15 * noise, 0.3 * noise).astype(jnp.float32)


def block_levels(rng, extent, pieces, smallest, high):
    loudness, own = 1.0, jax.random.fold_in(rng, 6)
    for dim, shards_of in pieces:
        steps = jnp.exp(jax.random.uniform(jax.random.fold_in(own, dim), (shards_of,), jnp.float32, smallest / len(pieces), high / len(pieces)))
        loudness = loudness * jnp.repeat(steps, extent[dim] // shards_of).reshape([-1 if axis == dim else 1 for axis in range(len(extent))])
    return loudness


def scatter_about(own_key, dims, deviation, most, cuts=(), held_as=jnp.bfloat16):
    entries = jax.random.normal(own_key, dims, jnp.float32) * deviation
    if len(cuts) > 0:
        entries = block_levels(own_key, dims, cuts, -0.22, 0.18) * entries
    return jnp.clip(entries, min=-most, max=most).astype(held_as)


def setup_inputs(seed: int = 0) -> dict:
    key_list = jax.random.split(jax.random.key(seed), 10)
    tokens = draw_tokens(jax.random.fold_in(key_list[9], 71), 0)
    clip_frames = draw_clip_frames(jax.random.fold_in(key_list[9], 71), 0)
    cotangent = draw_cotangent(jax.random.fold_in(key_list[9], 71), 0)
    embed = scatter_about(key_list[3], (2, SLOTS, D), 1.0, 6.0, ((0, 2),))
    norm_params = draw_norm_params(jax.random.fold_in(key_list[9], 71), 0)
    w_qkv = scatter_about(key_list[5], (2, D, 3 * D), D ** -0.5, 0.1875, ((0, 2),))
    w_out = scatter_about(key_list[6], (2, D, D), (D // 16) ** -0.5, 0.75, ((0, 2),))
    w_up = scatter_about(key_list[7], (2, D, FF), D ** -0.5, 0.1875, ((0, 2),))
    w_down = scatter_about(key_list[8], (2, FF, D), FF ** -0.5, 0.09375, ((0, 2),))
    return {"tokens": tokens, "clip_frames": clip_frames, "cotangent": cotangent, "embed": embed, "norm_params": norm_params, "w_qkv": w_qkv, "w_out": w_out, "w_up": w_up, "w_down": w_down}


@jax.custom_vjp
def low(v):
    return lax.optimization_barrier(v.astype(jnp.bfloat16)).astype(jnp.float32)

@jax.custom_vjp
def low_back(v):
    return v

def low_keep(v):
    return (low(v), None)

def low_pass(kept, grad):
    return (grad,)

def back_keep(v):
    return (v, None)

def back_low(kept, grad):
    return (low(grad),)
low.defvjp(low_keep, low_pass)
low_back.defvjp(back_keep, back_low)

def layer_norm(values, gain_row, shift_row):
    center = values - lax.optimization_barrier(jnp.mean(values, -1, keepdims=True))
    spread = lax.optimization_barrier(jnp.mean(center * center, -1, keepdims=True))
    return center * lax.rsqrt(spread + 1e-05) * gain_row + shift_row

def project(values, matrix):
    return jnp.einsum('gld,de->gle', values, matrix, precision=lax.Precision.HIGHEST)

def attend(inputs):
    queries, key_rows, values, visible = inputs
    heads_q = queries.reshape(SLOTS, HEADS, HEAD)
    heads_k = key_rows.reshape(SLOTS, HEADS, HEAD)
    heads_v = values.reshape(SLOTS, HEADS, HEAD)
    scores = jnp.einsum('qhd,khd->hqk', heads_q, heads_k, precision=lax.Precision.HIGHEST) * HEAD ** (-0.5)
    scores = low_back(scores)
    scores = jnp.where(visible[None, None, :], scores, -1e+30)
    weights_soft = jax.nn.softmax(scores, axis=-1)
    mixed_out = jnp.einsum('hqk,khd->qhd', low(weights_soft), heads_v, precision=lax.Precision.HIGHEST)
    return mixed_out.reshape(SLOTS, D)

def block(base_in, source, visible, qkv_w, out_w, up_w, down_w, params):
    query_in = low(layer_norm(base_in, params[0], params[1]))
    key_in = low(layer_norm(source, params[2], params[3]))
    queries = low_back(low(project(query_in, qkv_w[:, :D])))
    key_rows = low_back(low(project(key_in, qkv_w[:, D:2 * D])))
    values = low_back(low(project(key_in, qkv_w[:, 2 * D:])))
    mixed_out = lax.map(jax.checkpoint(attend), (queries, key_rows, values, visible))
    mixed_out = low_back(low(mixed_out))
    hidden = base_in + low_back(project(mixed_out, out_w))
    normed = low(layer_norm(hidden, params[4], params[5]))
    upward = low_back(project(normed, up_w))
    return hidden + low_back(project(low(jax.nn.gelu(upward)), down_w))

def reference(tokens, clip_frames, cotangent, embed, norm_params, w_qkv, w_out, w_up, w_down):
    slot_ids = jnp.arange(SLOTS, dtype=jnp.int32)
    visible = slot_ids[None, :] < clip_frames[:, None] * (SLOTS // 16)
    everyone = jnp.ones_like(visible)

    def forward(inputs, embeds, params, qkv_w, out_w, up_w, down_w, probe_zero):
        first_base = jnp.broadcast_to(embeds[0], inputs.shape)
        first_out = block(first_base, inputs, visible, qkv_w[0], out_w[0], up_w[0], down_w[0], params[0])
        passed = low_back(low(first_out) + probe_zero)
        second = block(passed + embeds[1], passed, everyone, qkv_w[1], out_w[1], up_w[1], down_w[1], params[1])
        return (second, first_out)
    probe_zero = jnp.zeros((GROUPS, SLOTS, D), jnp.float32)
    second, backward, first_out = jax.vjp(forward, tokens.astype(jnp.float32), embed.astype(jnp.float32), norm_params.astype(jnp.float32), w_qkv.astype(jnp.float32), w_out.astype(jnp.float32), w_up.astype(jnp.float32), w_down.astype(jnp.float32), probe_zero, has_aux=True)
    gradients = backward(cotangent.astype(jnp.float32))
    section_out = jnp.stack([first_out, second])
    section_grad = jnp.stack([gradients[0], gradients[7]])
    magnitude = jnp.sqrt(lax.optimization_barrier(jnp.mean(section_grad * section_grad, axis=(2, 3))) + 1e-06)
    norms = magnitude / lax.optimization_barrier(jnp.mean(magnitude, axis=1, keepdims=True))
    return (section_out, section_grad, gradients[3], gradients[4], gradients[5], gradients[6], gradients[2], gradients[1], norms)
```

```python
import functools
import jax
import jax.numpy as jnp
from jax import lax
from jax.experimental import pallas as pl
from jax.experimental.pallas import tpu as pltpu
from jax.sharding import PartitionSpec as P

HEADS = 8
MESH = pl.DeviceIdType.MESH
TILE = 256
RING = 8
WIDTH = 1024
SPLIT = (80, 64, 48, 64)
ORDERS = ((2, 1, 0), (1, 2, 0), (0, 2, 1), (0, 1, 2))


def lines_of(size):
    short = 1
    while 2 * short**3 < size:
        short += 1
    assert 2 * short**3 == size
    return (2 * short, short, short)


class Plan:
    def __init__(self, dims):
        d = lax.axis_index("dp")
        self.d = d
        self.dims = dims
        self.strides = (dims[1] * dims[2], dims[2], 1)
        self.coords = tuple(lax.rem(lax.div(d, s), n) for s, n in zip(self.strides, dims))
        self.depth = 2 * (sum(dims) - 3)


def stages(plan):
    found = []
    row = 0
    for kind, order in enumerate(ORDERS):
        delay = 0
        left, free = 0, 0
        active = None
        bases = []
        for phase, axis in enumerate(order):
            n, c = plan.dims[axis], plan.coords[axis]
            w = WIDTH >> (phase + 1)
            bases.append((delay, left, free, active, axis, w))
            delay += n - 1
            top = c == n - 1
            left = left + jnp.where(top, w, 0)
            free = free + jnp.where(top, 0, w)
            if n > 2:
                end = (c == 0) | top
                active = end if active is None else active & end
        for phase in range(3):
            found.append(("sum", kind, phase, row) + tuple(bases[phase]))
        for phase in (2, 1, 0):
            _, left, free, active, axis, w = bases[phase]
            found.append(("spread", kind, phase, row, delay, left, free, active, axis, w))
            delay += plan.dims[axis] - 1
        row += SPLIT[kind]
    return found


def both(*terms):
    out = None
    for t in terms:
        if t is None:
            continue
        out = t if out is None else out & t
    return out


def copies(plan, stage, up, tick, total, held, landing, result, send_sem, recv_sem):
    what, kind, phase, row, delay, left, free, active, axis, w = stage
    n, c, stride = plan.dims[axis], plan.coords[axis], plan.strides[axis]
    toward_top = up if what == "sum" else not up
    hops = c if toward_top else n - 1 - c
    job = tick - delay - hops
    ok = both(job >= 0, job < total, active)
    job = jnp.clip(job, 0, total - 1)
    rows = pl.ds(row, SPLIT[kind])
    col = pl.ds(pl.multiple_of(left + (w if up else 0), 128), w)
    stream = (kind * 6 + (phase if what == "sum" else 3 + phase)) * 2 + int(up)
    if what == "sum":
        land = pl.ds(pl.multiple_of(free + (w if up else 0), 128), w)
        src = held.at[job, rows, col]
        dst = landing.at[job, rows, land]
    else:
        src = result.at[job, rows, col]
        dst = result.at[job, rows, col]
    step = stride if toward_top else -stride
    def make(source):
        return pltpu.make_async_remote_copy(
            src_ref=source, dst_ref=dst,
            send_sem=send_sem.at[stream, lax.rem(job, RING)], recv_sem=recv_sem.at[stream, job],
            device_id={"dp": plan.d + step}, device_id_type=MESH)
    def send(source):
        copy = make(source)
        @pl.when(job >= RING)
        def _():
            copy.wait_send()
        copy.start()
    return make, send, src, dst, ok, hops, n, job, rows, col


def comm_tick(plan, table, kinds, tick, total, held, landing, result, send_sem, recv_sem, own_sem):
    for stage in table:
        what, kind, phase = stage[:3]
        if kind not in kinds:
            continue
        for up in (True, False):
            make, send, src, dst, ok, hops, n, job, rows, col = copies(
                plan, stage, up, tick, total, held, landing, result, send_sem, recv_sem)
            if what == "sum":
                @pl.when(ok & (hops > 0))
                def _():
                    make(src).wait_recv()
                    held[job, rows, col] = held[job, rows, col] + dst[...]
                @pl.when(ok & (hops < n - 1))
                def _():
                    send(src)
            else:
                if phase == 2:
                    @pl.when(ok & (hops == 0))
                    def _():
                        mine = held.at[job, rows, col]
                        send(mine)
                        pltpu.make_async_copy(mine, dst, own_sem.at[kind, job]).start()
                    @pl.when(ok & (hops > 0))
                    def _():
                        make(src).wait_recv()
                    if n > 2:
                        @pl.when(ok & (hops > 0) & (hops < n - 1))
                        def _():
                            send(src)
                else:
                    if phase == 1:
                        last = [s for s in table if s[1] == kind and s[0] == "spread" and s[2] == 2][0]
                        _, _, _, _, _, left3, _, active3, axis3, w3 = last
                        c3, n3 = plan.coords[axis3], plan.dims[axis3]
                        top3 = c3 == n3 - 1
                        own = held.at[job, rows, pl.ds(pl.multiple_of(left3 + jnp.where(top3, w3, 0), 128), w3)]
                        own_dst = result.at[job, rows, pl.ds(pl.multiple_of(left3 + jnp.where(top3, w3, 0), 128), w3)]
                        @pl.when(both(ok, hops == 0, (c3 == 0) | top3 if n3 > 2 else None))
                        def _():
                            pltpu.make_async_copy(own, own_dst, own_sem.at[kind, job]).wait()
                    @pl.when(ok & (hops > 0))
                    def _():
                        make(src).wait_recv()
                    @pl.when(ok & (hops < n - 1))
                    def _():
                        send(src)


def drain(plan, table, tick, total, held, landing, result, send_sem, recv_sem):
    for stage in table:
        what, kind, phase = stage[:3]
        for up in (True, False):
            make, send, src, dst, ok, hops, n, job, rows, col = copies(
                plan, stage, up, tick, total, held, landing, result, send_sem, recv_sem)
            @pl.when(ok & (hops < n - 1) & (job >= total - RING))
            def _():
                make(src).wait_send()


def greet(plan):
    barrier = pltpu.get_barrier_semaphore()
    count = 0
    for n, c, s in zip(plan.dims, plan.coords, plan.strides):
        for inside, step in ((c > 0, -s), (c < n - 1, s)):
            @pl.when(inside)
            def _():
                pl.semaphore_signal(barrier, inc=1, device_id={"dp": plan.d + step}, device_id_type=MESH)
            count = count + inside.astype(jnp.int32)
    pl.semaphore_wait(barrier, count)


def weights_kernel(dims, jobs, extra, left_ref, right_ref, extra_ref, result, held, landing,
                   left_buf, right_buf, load_sem, send_sem, recv_sem, own_sem):
    plan = Plan(dims)
    table = stages(plan)
    total = 4 * jobs + extra
    greet(plan)

    def left_copy(s):
        job, part, slot = lax.div(s, 4), lax.rem(s, 4), lax.rem(s, 2)
        slab = jnp.where(job < 4, job, jnp.where(job < 8, 4, jnp.minimum(job - 3, 7)))
        return pltpu.make_async_copy(
            left_ref.at[:, pl.ds(pl.multiple_of(slab * WIDTH + part * TILE, TILE), TILE)],
            left_buf.at[slot], load_sem.at[slot])

    def right_copy(job):
        slot = lax.rem(job, 2)
        slab = jnp.where(job < 4, 0, job - 3)
        return pltpu.make_async_copy(
            right_ref.at[:, pl.ds(pl.multiple_of(slab * WIDTH, WIDTH), WIDTH)],
            right_buf.at[slot], load_sem.at[2 + slot])

    def product(s):
        job = lax.div(s, 4)
        left_copy(s).wait()
        @pl.when(lax.rem(s, 4) == 0)
        def _():
            right_copy(job).wait()
            @pl.when(job + 1 < jobs)
            def _():
                right_copy(job + 1).start()
        @pl.when(s + 1 < 4 * jobs)
        def _():
            left_copy(s + 1).start()
        a = left_buf[lax.rem(s, 2)]
        b = right_buf[lax.rem(job, 2)]
        held[s] = lax.dot_general(a, b, (((0,), (0,)), ((), ())), preferred_element_type=jnp.float32).astype(jnp.bfloat16)

    extras = pltpu.make_async_copy(extra_ref, held.at[pl.ds(4 * jobs, extra)], load_sem.at[4])
    extras.start()
    left_copy(0).start()
    right_copy(0).start()
    product(0)
    extras.wait()

    args = (total, held, landing, result, send_sem, recv_sem)

    def tick(t, _):
        comm_tick(plan, table, (0, 2), t, *args, own_sem)
        @pl.when(t + 1 < 4 * jobs)
        def _():
            product(t + 1)
        comm_tick(plan, table, (1, 3), t, *args, own_sem)
        return 0

    lax.fori_loop(0, total + plan.depth, tick, 0)

    def finish(t, _):
        drain(plan, table, t, *args)
        return 0

    lax.fori_loop(0, total + plan.depth, finish, 0)


def weight_sums(dims, lefts, rights, extras, cid):
    jobs, extra = 12, extras.shape[0]
    total = 4 * jobs + extra
    rows = lefts.shape[0]
    any_space = pl.BlockSpec(memory_space=pl.ANY)
    return pl.pallas_call(
        functools.partial(weights_kernel, dims, jobs, extra),
        out_shape=jax.ShapeDtypeStruct((total, TILE, WIDTH), jnp.bfloat16),
        in_specs=[any_space] * 3,
        out_specs=any_space,
        scratch_shapes=[
            pltpu.VMEM((total, TILE, WIDTH), jnp.bfloat16),
            pltpu.VMEM((total, TILE, WIDTH), jnp.bfloat16),
            pltpu.VMEM((2, rows, TILE), jnp.bfloat16),
            pltpu.VMEM((2, rows, WIDTH), jnp.bfloat16),
            pltpu.SemaphoreType.DMA((5,)),
            pltpu.SemaphoreType.DMA((48, RING)),
            pltpu.SemaphoreType.DMA((48, total)),
            pltpu.SemaphoreType.DMA((4, total)),
        ],
        compiler_params=pltpu.CompilerParams(collective_id=cid, has_side_effects=True, vmem_limit_bytes=62 * 2**20),
        cost_estimate=pl.CostEstimate(flops=2 * 12 * rows * WIDTH * WIDTH, bytes_accessed=100 * 2**20, transcendentals=0),
    )(lefts, rights, extras)


def layer_norm(values, gain_row, shift_row):
    center = values - jnp.mean(values, -1, keepdims=True)
    spread = jnp.mean(center * center, -1, keepdims=True)
    return center * lax.rsqrt(spread + 1e-05) * gain_row + shift_row


def matmul(left, right, form):
    return jnp.einsum(form, left, right, preferred_element_type=jnp.float32)


def advance(base_in, source, visible, w_qkv, w_out, w_up, w_down, params):
    query_in, query_back = jax.vjp(layer_norm, base_in, params[0], params[1])
    key_in, key_back = jax.vjp(layer_norm, source, params[2], params[3])
    query_low = query_in.astype(jnp.bfloat16)
    key_low = key_in.astype(jnp.bfloat16)
    features = query_low.shape[-1]
    queries = matmul(query_low, w_qkv[:, :features], "gld,de->gle").astype(jnp.bfloat16)
    key_vals = matmul(key_low, w_qkv[:, features:], "gld,de->gle").astype(jnp.bfloat16)
    groups, positions = (queries.shape[0], queries.shape[1])
    head_shape = (groups, positions, HEADS, features // HEADS)
    head_scale = (features // HEADS) ** (-0.5)
    heads_q = queries.reshape(head_shape)
    heads_k = key_vals[..., :features].reshape(head_shape)
    heads_v = key_vals[..., features:].reshape(head_shape)
    scores = matmul(heads_q, heads_k, "gqhd,gkhd->ghqk") * head_scale
    scores = jnp.where(visible[:, None, None, :], scores, -1e30)
    row_max = jnp.max(scores, -1, keepdims=True)
    exponent = jnp.exp(scores - row_max)
    weights_soft = exponent / jnp.sum(exponent, -1, keepdims=True)
    weights_low = weights_soft.astype(jnp.bfloat16)
    mixed_out = (
        matmul(weights_low, heads_v, "ghqk,gkhd->gqhd")
        .reshape(groups, positions, features)
        .astype(jnp.bfloat16)
    )
    hidden = base_in + matmul(mixed_out, w_out, "gld,de->gle")
    normed, normed_back = jax.vjp(layer_norm, hidden, params[4], params[5])
    normed_low = normed.astype(jnp.bfloat16)
    upward = matmul(normed_low, w_up, "gld,df->glf")
    active, active_back = jax.vjp(jax.nn.gelu, upward)
    active_low = active.astype(jnp.bfloat16)
    outcome = hidden + matmul(active_low, w_down, "glf,fd->gld")
    stored_parts = (
        query_back,
        key_back,
        query_low,
        key_low,
        heads_q,
        heads_k,
        heads_v,
        weights_soft,
        weights_low,
        mixed_out,
        normed_back,
        normed_low,
        active_back,
        active_low,
    )
    return (outcome, stored_parts)


def retreat(stored_parts, w_qkv, w_out, w_up, w_down, grad_outcome):
    (
        query_back,
        key_back,
        query_low,
        key_low,
        heads_q,
        heads_k,
        heads_v,
        weights_soft,
        weights_low,
        mixed_out,
        normed_back,
        normed_low,
        active_back,
        active_low,
    ) = stored_parts
    features = query_low.shape[-1]
    groups, positions = (query_low.shape[0], query_low.shape[1])
    head_scale = (features // HEADS) ** (-0.5)
    outcome_low = grad_outcome.astype(jnp.bfloat16)
    grad_active = matmul(outcome_low, w_down, "gld,fd->glf")
    (grad_upward,) = active_back(grad_active)
    upward_low = grad_upward.astype(jnp.bfloat16)
    grad_normed = matmul(upward_low, w_up, "glf,df->gld")
    grad_from_norm, grad_gain_mlp, grad_shift_mlp = normed_back(grad_normed)
    grad_hidden = grad_outcome + grad_from_norm
    hidden_low = grad_hidden.astype(jnp.bfloat16)
    grad_mixed = (
        matmul(hidden_low, w_out, "gle,de->gld").astype(jnp.bfloat16).reshape(heads_q.shape)
    )
    grad_weights = matmul(grad_mixed, heads_v, "gqhd,gkhd->ghqk")
    grad_values = matmul(weights_low, grad_mixed, "ghqk,gqhd->gkhd").astype(jnp.bfloat16)
    grad_scores = weights_soft * (
        grad_weights - jnp.sum(grad_weights * weights_soft, -1, keepdims=True)
    )
    scores_low = grad_scores.astype(jnp.bfloat16)
    grad_queries = (matmul(scores_low, heads_k, "ghqk,gkhd->gqhd") * head_scale).astype(
        jnp.bfloat16
    )
    grad_keys = (matmul(scores_low, heads_q, "ghqk,gqhd->gkhd") * head_scale).astype(jnp.bfloat16)
    grad_queries = grad_queries.reshape(groups, positions, features)
    grad_keys = grad_keys.reshape(groups, positions, features)
    grad_values = grad_values.reshape(groups, positions, features)
    grad_query_in = matmul(grad_queries, w_qkv[:, :features], "gle,de->gld")
    grad_key_in = matmul(grad_keys, w_qkv[:, features : 2 * features], "gle,de->gld") + matmul(
        grad_values, w_qkv[:, 2 * features :], "gle,de->gld"
    )
    grad_base_norm, grad_gain_q, grad_shift_q = query_back(grad_query_in)
    grad_source, grad_gain_k, grad_shift_k = key_back(grad_key_in)
    grad_base = grad_hidden + grad_base_norm
    grad_params = jnp.stack(
        [grad_gain_q, grad_shift_q, grad_gain_k, grad_shift_k, grad_gain_mlp, grad_shift_mlp]
    )
    rights = (outcome_low, upward_low, hidden_low, grad_queries, grad_keys, grad_values)
    return rights, grad_params, grad_base, grad_source


def body(tokens, clip_frames, cotangent, embed, norm_params, w_qkv, w_out, w_up, w_down):
    is_first = lax.axis_index("section") == 0
    matrices = (w_qkv[0], w_out[0], w_up[0], w_down[0])
    params = norm_params[0]
    embed_row = embed[0].astype(jnp.float32)
    groups, positions, features = tokens.shape
    slot_ids = jnp.arange(positions, dtype=jnp.int32)
    visible = (slot_ids[None, :] < clip_frames[:, None] * (positions // 16)) | jnp.logical_not(
        is_first
    )

    def forward(source):
        source_wide = source.astype(jnp.float32)
        base_in = jnp.where(is_first, 0.0, source_wide) + embed_row
        return advance(base_in, source_wide, visible, *matrices, params)

    early, _ = forward(tokens)
    received = lax.ppermute(early.astype(jnp.bfloat16), "section", [(0, 1)])
    outcome, stored = forward(jnp.where(is_first, tokens, received))

    def backward(upstream):
        rights, grad_params, grad_base, grad_source = retreat(
            stored, *matrices, upstream.astype(jnp.float32)
        )
        sent = (grad_source + grad_base).astype(jnp.bfloat16)
        return rights, grad_params, grad_base, grad_source, sent

    sent_early = backward(cotangent)[-1]
    arriving = lax.ppermute(sent_early, "section", [(1, 0)])
    rights, grad_params, grad_base, grad_source, sent = backward(
        jnp.where(is_first, arriving, cotangent)
    )
    grad_inputs = jnp.where(is_first, grad_source, sent.astype(jnp.float32))
    rows = groups * positions
    flat = lambda parts: jnp.concatenate([p.reshape(rows, -1) for p in parts], axis=1)
    (_, _, query_low, key_low, _, _, _, _, _, mixed_low, _, normed_low, _, active_low) = stored
    lefts = flat((active_low, normed_low, mixed_low, query_low, key_low))
    rights = flat(rights)
    magnitude = jnp.sqrt(jnp.mean(grad_inputs * grad_inputs, axis=(1, 2)) + 1e-06)
    overall = lax.psum(jnp.sum(magnitude), "dp")
    norms = magnitude / (overall / (groups * lax.axis_size("dp")))
    extras = jnp.stack(
        [jnp.sum(grad_base, axis=0), jnp.pad(grad_params, ((0, TILE - 6), (0, 0)))]
    ).astype(jnp.bfloat16)
    sums = weight_sums(lines_of(lax.axis_size("dp")), lefts, rights, extras, 1)
    blocks = sums[:48].reshape(12, 1024, 1024)
    beside = lambda first, last: (
        blocks[first:last].transpose(1, 0, 2).reshape(1024, -1).astype(jnp.float32)
    )
    return (
        outcome[None],
        grad_inputs[None],
        beside(9, 12)[None],
        beside(8, 9)[None],
        beside(4, 8)[None],
        blocks[0:4].reshape(4096, 1024).astype(jnp.float32)[None],
        sums[49, :6].astype(jnp.float32)[None],
        sums[48].astype(jnp.float32)[None],
        norms[None],
    )


def solution(mesh):
    placed = (
        P("dp", None, None),
        P("dp"),
        P("dp", None, None),
        P("section", None, None),
        P("section", None, None),
        P("section", None, None),
        P("section", None, None),
        P("section", None, None),
        P("section", None, None),
    )
    return jax.shard_map(
        body,
        mesh=mesh,
        in_specs=placed,
        out_specs=(
            P("section", "dp", None, None),
            P("section", "dp", None, None),
            P("section", None, None),
            P("section", None, None),
            P("section", None, None),
            P("section", None, None),
            P("section", None, None),
            P("section", None, None),
            P("section", "dp"),
        ),
        check_vma=False,
    )
```

```python
import functools

import jax
import jax.numpy as jnp
from jax import lax
from jax.experimental import pallas as pl
from jax.experimental.pallas import tpu as pltpu
from jax.sharding import PartitionSpec as P

MESH = pl.DeviceIdType.MESH
TILE = 256
RING = 8
WIDTH = 1024
SPLIT = (80, 64, 48, 64)
ORDERS = ((2, 1, 0), (1, 2, 0), (0, 2, 1), (0, 1, 2))


def lines_of(size):
    short = 1
    while 2 * short**3 < size:
        short += 1
    assert 2 * short**3 == size
    return (2 * short, short, short)


class Plan:
    def __init__(self, dims):
        d = lax.axis_index("dp")
        self.d = d
        self.dims = dims
        self.strides = (dims[1] * dims[2], dims[2], 1)
        self.coords = tuple(lax.rem(lax.div(d, s), n) for s, n in zip(self.strides, dims))
        self.depth = 2 * (sum(dims) - 3)


def stages(plan):
    found = []
    row = 0
    for kind, order in enumerate(ORDERS):
        delay = 0
        left, free = 0, 0
        active = None
        bases = []
        for phase, axis in enumerate(order):
            n, c = plan.dims[axis], plan.coords[axis]
            w = WIDTH >> (phase + 1)
            bases.append((delay, left, free, active, axis, w))
            delay += n - 1
            top = c == n - 1
            left = left + jnp.where(top, w, 0)
            free = free + jnp.where(top, 0, w)
            if n > 2:
                end = (c == 0) | top
                active = end if active is None else active & end
        for phase in range(3):
            found.append(("sum", kind, phase, row) + tuple(bases[phase]))
        for phase in (2, 1, 0):
            _, left, free, active, axis, w = bases[phase]
            found.append(("spread", kind, phase, row, delay, left, free, active, axis, w))
            delay += plan.dims[axis] - 1
        row += SPLIT[kind]
    return found


def both(*terms):
    out = None
    for t in terms:
        if t is None:
            continue
        out = t if out is None else out & t
    return out


def copies(plan, stage, up, tick, total, held, landing, result, send_sem, recv_sem):
    what, kind, phase, row, delay, left, free, active, axis, w = stage
    n, c, stride = plan.dims[axis], plan.coords[axis], plan.strides[axis]
    toward_top = up if what == "sum" else not up
    hops = c if toward_top else n - 1 - c
    job = tick - delay - hops
    ok = both(job >= 0, job < total, active)
    job = jnp.clip(job, 0, total - 1)
    rows = pl.ds(row, SPLIT[kind])
    col = pl.ds(pl.multiple_of(left + (w if up else 0), 128), w)
    stream = (kind * 6 + (phase if what == "sum" else 3 + phase)) * 2 + int(up)
    if what == "sum":
        land = pl.ds(pl.multiple_of(free + (w if up else 0), 128), w)
        src = held.at[job, rows, col]
        dst = landing.at[job, rows, land]
    else:
        src = result.at[job, rows, col]
        dst = result.at[job, rows, col]
    step = stride if toward_top else -stride
    def make(source):
        return pltpu.make_async_remote_copy(
            src_ref=source, dst_ref=dst,
            send_sem=send_sem.at[stream, lax.rem(job, RING)], recv_sem=recv_sem.at[stream, job],
            device_id={"dp": plan.d + step}, device_id_type=MESH)
    def send(source):
        copy = make(source)
        @pl.when(job >= RING)
        def _():
            copy.wait_send()
        copy.start()
    return make, send, src, dst, ok, hops, n, job, rows, col


def comm_tick(plan, table, kinds, tick, total, held, landing, result, send_sem, recv_sem, own_sem):
    for stage in table:
        what, kind, phase = stage[:3]
        if kind not in kinds:
            continue
        for up in (True, False):
            make, send, src, dst, ok, hops, n, job, rows, col = copies(
                plan, stage, up, tick, total, held, landing, result, send_sem, recv_sem)
            if what == "sum":
                @pl.when(ok & (hops > 0))
                def _():
                    make(src).wait_recv()
                    held[job, rows, col] = held[job, rows, col] + dst[...]
                @pl.when(ok & (hops < n - 1))
                def _():
                    send(src)
            else:
                if phase == 2:
                    @pl.when(ok & (hops == 0))
                    def _():
                        mine = held.at[job, rows, col]
                        send(mine)
                        pltpu.make_async_copy(mine, dst, own_sem.at[kind, job]).start()
                    @pl.when(ok & (hops > 0))
                    def _():
                        make(src).wait_recv()
                    if n > 2:
                        @pl.when(ok & (hops > 0) & (hops < n - 1))
                        def _():
                            send(src)
                else:
                    if phase == 1:
                        last = [s for s in table if s[1] == kind and s[0] == "spread" and s[2] == 2][0]
                        _, _, _, _, _, left3, _, active3, axis3, w3 = last
                        c3, n3 = plan.coords[axis3], plan.dims[axis3]
                        top3 = c3 == n3 - 1
                        own = held.at[job, rows, pl.ds(pl.multiple_of(left3 + jnp.where(top3, w3, 0), 128), w3)]
                        own_dst = result.at[job, rows, pl.ds(pl.multiple_of(left3 + jnp.where(top3, w3, 0), 128), w3)]
                        @pl.when(both(ok, hops == 0, (c3 == 0) | top3 if n3 > 2 else None))
                        def _():
                            pltpu.make_async_copy(own, own_dst, own_sem.at[kind, job]).wait()
                    @pl.when(ok & (hops > 0))
                    def _():
                        make(src).wait_recv()
                    @pl.when(ok & (hops < n - 1))
                    def _():
                        send(src)


def drain(plan, table, tick, total, held, landing, result, send_sem, recv_sem):
    for stage in table:
        what, kind, phase = stage[:3]
        for up in (True, False):
            make, send, src, dst, ok, hops, n, job, rows, col = copies(
                plan, stage, up, tick, total, held, landing, result, send_sem, recv_sem)
            @pl.when(ok & (hops < n - 1) & (job >= total - RING))
            def _():
                make(src).wait_send()


def greet(plan):
    barrier = pltpu.get_barrier_semaphore()
    count = 0
    for n, c, s in zip(plan.dims, plan.coords, plan.strides):
        for inside, step in ((c > 0, -s), (c < n - 1, s)):
            @pl.when(inside)
            def _():
                pl.semaphore_signal(barrier, inc=1, device_id={"dp": plan.d + step}, device_id_type=MESH)
            count = count + inside.astype(jnp.int32)
    pl.semaphore_wait(barrier, count)


def weights_kernel(dims, jobs, extra, left_ref, right_ref, extra_ref, result, held, landing,
                   left_buf, right_buf, load_sem, send_sem, recv_sem, own_sem):
    plan = Plan(dims)
    table = stages(plan)
    total = 4 * jobs + extra
    greet(plan)

    def left_copy(s):
        job, part, slot = lax.div(s, 4), lax.rem(s, 4), lax.rem(s, 2)
        slab = jnp.where(job < 4, job, jnp.where(job < 8, 4, jnp.minimum(job - 3, 7)))
        return pltpu.make_async_copy(
            left_ref.at[:, pl.ds(pl.multiple_of(slab * WIDTH + part * TILE, TILE), TILE)],
            left_buf.at[slot], load_sem.at[slot])

    def right_copy(job):
        slot = lax.rem(job, 2)
        slab = jnp.where(job < 4, 0, job - 3)
        return pltpu.make_async_copy(
            right_ref.at[:, pl.ds(pl.multiple_of(slab * WIDTH, WIDTH), WIDTH)],
            right_buf.at[slot], load_sem.at[2 + slot])

    def product(s):
        job = lax.div(s, 4)
        left_copy(s).wait()
        @pl.when(lax.rem(s, 4) == 0)
        def _():
            right_copy(job).wait()
            @pl.when(job + 1 < jobs)
            def _():
                right_copy(job + 1).start()
        @pl.when(s + 1 < 4 * jobs)
        def _():
            left_copy(s + 1).start()
        a = left_buf[lax.rem(s, 2)]
        b = right_buf[lax.rem(job, 2)]
        held[s] = lax.dot_general(a, b, (((0,), (0,)), ((), ())), preferred_element_type=jnp.float32).astype(jnp.bfloat16)

    extras = pltpu.make_async_copy(extra_ref, held.at[pl.ds(4 * jobs, extra)], load_sem.at[4])
    extras.start()
    left_copy(0).start()
    right_copy(0).start()
    product(0)
    extras.wait()

    args = (total, held, landing, result, send_sem, recv_sem)

    def tick(t, _):
        comm_tick(plan, table, (0, 2), t, *args, own_sem)
        @pl.when(t + 1 < 4 * jobs)
        def _():
            product(t + 1)
        comm_tick(plan, table, (1, 3), t, *args, own_sem)
        return 0

    lax.fori_loop(0, total + plan.depth, tick, 0)

    def finish(t, _):
        drain(plan, table, t, *args)
        return 0

    lax.fori_loop(0, total + plan.depth, finish, 0)


def weight_sums(dims, lefts, rights, extras, cid):
    jobs, extra = 12, extras.shape[0]
    total = 4 * jobs + extra
    rows = lefts.shape[0]
    any_space = pl.BlockSpec(memory_space=pl.ANY)
    return pl.pallas_call(
        functools.partial(weights_kernel, dims, jobs, extra),
        out_shape=jax.ShapeDtypeStruct((total, TILE, WIDTH), jnp.bfloat16),
        in_specs=[any_space] * 3,
        out_specs=any_space,
        scratch_shapes=[
            pltpu.VMEM((total, TILE, WIDTH), jnp.bfloat16),
            pltpu.VMEM((total, TILE, WIDTH), jnp.bfloat16),
            pltpu.VMEM((2, rows, TILE), jnp.bfloat16),
            pltpu.VMEM((2, rows, WIDTH), jnp.bfloat16),
            pltpu.SemaphoreType.DMA((5,)),
            pltpu.SemaphoreType.DMA((48, RING)),
            pltpu.SemaphoreType.DMA((48, total)),
            pltpu.SemaphoreType.DMA((4, total)),
        ],
        compiler_params=pltpu.CompilerParams(collective_id=cid, has_side_effects=True, vmem_limit_bytes=62 * 2**20),
        cost_estimate=pl.CostEstimate(flops=2 * 12 * rows * WIDTH * WIDTH, bytes_accessed=100 * 2**20, transcendentals=0),
    )(lefts, rights, extras)


HEADS = 8
CHUNK = 512
LOW = jnp.bfloat16
WIDE = jnp.float32
NN = (((1,), (0,)), ((), ()))
NT = (((1,), (1,)), ((), ()))
TN = (((0,), (0,)), ((), ()))


def dot(a, b, form):
    return lax.dot_general(a, b, form, preferred_element_type=WIDE)


def normalize(values):
    center = values - jnp.mean(values, -1, keepdims=True)
    inverse = lax.rsqrt(jnp.mean(center * center, -1, keepdims=True) + 1e-05)
    return center * inverse, inverse


def norm_back(upstream, gain, xhat, inverse):
    scaled = upstream * gain
    return inverse * (scaled - jnp.mean(scaled, -1, keepdims=True)
                      - xhat * jnp.mean(scaled * xhat, -1, keepdims=True))


def gelu_pair(u):
    c = 0.7978845608028654
    square = u * u
    t = jnp.tanh(u * (c + (c * 0.044715) * square))
    half = 0.5 * (1.0 + t)
    slope = half + (0.5 * u) * (1.0 - t * t) * (c + (3.0 * c * 0.044715) * square)
    return u * half, slope


def layers_kernel(groups, tokens, cotangent, mask, embed, params, w_qkv, w_out, w_up, w_down,
                  lefts, rights, sec_out, sec_grad, g_params, g_embed, squares,
                  qkv_w, out_w, up_w, down_w, emb, src, upstream, qkv, probs, slopes, xhat_f, stats,
                  active, keep, passed, acc, hid, wide, u_buf,
                  w_sem, in_sem, left_sem, right_sem, wide_sem, send_sem, recv_sem):
    section = lax.axis_index("section")
    first = section == 0
    other = 1 - section
    slots, width = emb.shape
    units = up_w.shape[1]
    steps = units // CHUNK
    head = width // HEADS
    scale = head ** -0.5

    loads = [pltpu.make_async_copy(a, b, w_sem.at[k]) for k, (a, b) in enumerate(
        ((w_qkv, qkv_w), (w_out, out_w), (w_up, up_w), (w_down, down_w), (embed, emb)))]
    loads[4].start()
    loads[0].start()

    def token_load(g):
        return pltpu.make_async_copy(tokens.at[g], src.at[g], in_sem.at[g])

    def cot_load(g):
        return pltpu.make_async_copy(cotangent.at[g], upstream.at[g], in_sem.at[groups + g])

    @pl.when(first)
    def _():
        for g in range(groups):
            token_load(g).start()
    for k in (1, 2, 3):
        loads[k].start()

    @pl.when(section == 1)
    def _():
        for g in range(groups):
            cot_load(g).start()

    barrier = pltpu.get_barrier_semaphore()
    pl.semaphore_signal(barrier, inc=1, device_id={"section": other}, device_id_type=MESH)
    pl.semaphore_wait(barrier, 1)

    def relay(g):
        return pltpu.make_async_remote_copy(
            src_ref=passed, dst_ref=src.at[g], send_sem=send_sem.at[g], recv_sem=recv_sem.at[g],
            device_id={"section": other}, device_id_type=MESH)

    def relay_back(g):
        return pltpu.make_async_remote_copy(
            src_ref=passed, dst_ref=upstream.at[g], send_sem=send_sem.at[groups + g],
            recv_sem=recv_sem.at[groups + g], device_id={"section": other}, device_id_type=MESH)

    def rows_of(g):
        return pl.ds(pl.multiple_of(g * slots, slots), slots)

    def cols(i, w=CHUNK):
        return pl.ds(pl.multiple_of(i * w, w), w)

    def left_store(g, k):
        if k == 0:
            return pltpu.make_async_copy(active, lefts.at[rows_of(g), pl.ds(0, units)], left_sem.at[0])
        return pltpu.make_async_copy(
            keep.at[:, pl.ds((k - 1) * width, width)], lefts.at[rows_of(g), pl.ds(units + (k - 1) * width, width)], left_sem.at[k])

    def right_store(g, k):
        if k == 0:
            return pltpu.make_async_copy(upstream.at[g], rights.at[rows_of(g), pl.ds(0, width)], right_sem.at[0])
        if k == 1:
            return pltpu.make_async_copy(active, rights.at[rows_of(g), pl.ds(width, units)], right_sem.at[1])
        return pltpu.make_async_copy(
            keep.at[:, pl.ds((k - 2) * width, width)],
            rights.at[rows_of(g), pl.ds(width + units + (k - 2) * width, width)], right_sem.at[k])

    def out_store(g):
        return pltpu.make_async_copy(wide, sec_out.at[g], wide_sem.at[0])

    def grad_store(g):
        return pltpu.make_async_copy(wide, sec_grad.at[g], wide_sem.at[1])

    def base_of(g):
        return jnp.where(first, 0.0, src[g].astype(WIDE)) + emb[...].astype(WIDE)

    def forward(g, _):
        @pl.when(first)
        def _():
            token_load(g).wait()
        @pl.when(section == 1)
        def _():
            relay(g).wait_recv()
        @pl.when(g == 0)
        def _():
            loads[4].wait()

        @pl.when(g > 0)
        def _():
            for k in (3, 4):
                left_store(g - 1, k).wait()
        source = src[g].astype(WIDE)
        xhat, inverse = normalize(source)
        stats[g, :, 0:1] = inverse
        stats[g, :, 3:4] = jnp.mean(source, -1, keepdims=True)
        keep[:, 3 * width:4 * width] = (xhat * params[2:3] + params[3:4]).astype(LOW)
        base = base_of(g)
        xhat, inverse = normalize(base)
        stats[g, :, 1:2] = inverse
        stats[g, :, 4:5] = jnp.mean(base, -1, keepdims=True)
        keep[:, 2 * width:3 * width] = (xhat * params[0:1] + params[1:2]).astype(LOW)
        left_store(g, 3).start()
        left_store(g, 4).start()

        @pl.when(g == 0)
        def _():
            loads[0].wait()

        def project(k, a):
            def step(i, _):
                qkv[g, :, cols(i)] = dot(a[...], qkv_w[:, cols(i)], NN).astype(LOW)
                return 0
            lax.fori_loop(*k, step, 0)
        per = width // CHUNK
        project((0, per), keep.at[:, 2 * width:3 * width])
        project((per, 3 * per), keep.at[:, 3 * width:4 * width])

        @pl.when(g > 0)
        def _():
            for k in (0, 1, 2):
                left_store(g - 1, k).wait()
        seen = mask[g, 0:1, :] > 0
        for h in range(HEADS):
            q = qkv[g, :, h * head:(h + 1) * head]
            k = qkv[g, :, width + h * head:width + (h + 1) * head]
            v = qkv[g, :, 2 * width + h * head:2 * width + (h + 1) * head]
            s = jnp.where(seen, dot(q, k, NT) * scale, -1e30)
            e = jnp.exp(s - jnp.max(s, -1, keepdims=True))
            p = (e / jnp.sum(e, -1, keepdims=True)).astype(LOW)
            probs[g, h] = p
            keep[:, width + h * head:width + (h + 1) * head] = dot(p, v, NN).astype(LOW)
        left_store(g, 2).start()

        @pl.when(g == 0)
        def _():
            loads[1].wait()

        def mix(i, _):
            hid[:, cols(i)] = dot(keep[:, width:2 * width], out_w[:, cols(i)], NN)
            return 0
        lax.fori_loop(0, width // CHUNK, mix, 0)
        hidden = base_of(g) + hid[...]
        hid[...] = hidden
        xhat, inverse = normalize(hidden)
        stats[g, :, 2:3] = inverse
        xhat_f[g] = xhat.astype(LOW)
        keep[:, 0:width] = (xhat * params[4:5] + params[5:6]).astype(LOW)
        left_store(g, 1).start()

        @pl.when(g == 0)
        def _():
            loads[2].wait()
            loads[3].wait()

        acc[...] = hid[...]
        u_buf[0] = dot(keep[:, 0:width], up_w[:, cols(0)], NN)

        def feed(i, _):
            ahead = jnp.minimum(i + 1, steps - 1)
            u_buf[lax.rem(i + 1, 2)] = dot(keep[:, 0:width], up_w[:, cols(ahead)], NN)
            value, slope = gelu_pair(u_buf[lax.rem(i, 2)])
            slopes[g, :, cols(i)] = slope.astype(LOW)
            value = value.astype(LOW)
            active[:, cols(i)] = value
            acc[...] += dot(value, down_w[cols(i), :], NN)
            return 0
        lax.fori_loop(0, steps, feed, 0)
        left_store(g, 0).start()

        @pl.when(g > 0)
        def _():
            out_store(g - 1).wait()
        wide[...] = acc[...]
        out_store(g).start()

        @pl.when(first)
        def _():
            @pl.when(g > 0)
            def _():
                relay(g - 1).wait_send()
            passed[...] = acc[...].astype(LOW)
            relay(g).start()
        return 0

    lax.fori_loop(0, groups, forward, 0)
    for k in range(5):
        left_store(groups - 1, k).wait()
    out_store(groups - 1).wait()

    @pl.when(first)
    def _():
        relay(groups - 1).wait_send()

    g_params[...] = jnp.zeros_like(g_params)
    g_embed[...] = jnp.zeros_like(g_embed)
    squares[...] = jnp.zeros_like(squares)

    def gains(row, e, xhat):
        g_params[row:row + 1] += jnp.sum(e * xhat, axis=0, keepdims=True)
        g_params[row + 1:row + 2] += jnp.sum(e, axis=0, keepdims=True)

    def backward(g, _):
        @pl.when(first)
        def _():
            relay_back(g).wait_recv()
        @pl.when(section == 1)
        def _():
            cot_load(g).wait()
        @pl.when(g > 0)
        def _():
            for k in (0, 1):
                right_store(g - 1, k).wait()
        right_store(g, 0).start()

        acc[...] = jnp.zeros_like(acc)
        u_buf[0] = dot(upstream[g], down_w[cols(0), :], NT)

        def feed(i, _):
            ahead = jnp.minimum(i + 1, steps - 1)
            u_buf[lax.rem(i + 1, 2)] = dot(upstream[g], down_w[cols(ahead), :], NT)
            value = (u_buf[lax.rem(i, 2)] * slopes[g, :, cols(i)].astype(WIDE)).astype(LOW)
            active[:, cols(i)] = value
            acc[...] += dot(value, up_w[:, cols(i)], NT)
            return 0
        lax.fori_loop(0, steps, feed, 0)
        right_store(g, 1).start()

        e = acc[...]
        xhat = xhat_f[g].astype(WIDE)
        gains(4, e, xhat)
        grad_hidden = upstream[g].astype(WIDE) + norm_back(e, params[4:5], xhat, stats[g, :, 2:3])
        hid[...] = grad_hidden

        @pl.when(g > 0)
        def _():
            for k in (2, 3, 4, 5):
                right_store(g - 1, k).wait()
        keep[:, 0:width] = grad_hidden.astype(LOW)
        right_store(g, 2).start()

        def mixed_back(i, _):
            xhat_f[g, :, cols(i)] = dot(keep[:, 0:width], out_w[cols(i), :], NT).astype(LOW)
            return 0
        lax.fori_loop(0, width // CHUNK, mixed_back, 0)

        for h in range(HEADS):
            q = qkv[g, :, h * head:(h + 1) * head]
            k = qkv[g, :, width + h * head:width + (h + 1) * head]
            v = qkv[g, :, 2 * width + h * head:2 * width + (h + 1) * head]
            m = xhat_f[g, :, h * head:(h + 1) * head]
            low = probs[g, h]
            p = low.astype(WIDE)
            gp = dot(m, v, NT)
            ds = (p * (gp - jnp.sum(gp * p, -1, keepdims=True))).astype(LOW)
            keep[:, width + h * head:width + (h + 1) * head] = (dot(ds, k, NN) * scale).astype(LOW)
            keep[:, 2 * width + h * head:2 * width + (h + 1) * head] = (dot(ds, q, TN) * scale).astype(LOW)
            keep[:, 3 * width + h * head:3 * width + (h + 1) * head] = dot(low, m, TN).astype(LOW)
        for k in (3, 4, 5):
            right_store(g, k).start()

        def query_back(i, _):
            acc[:, cols(i)] = dot(keep[:, width:2 * width], qkv_w[cols(i), 0:width], NT)
            return 0
        lax.fori_loop(0, width // CHUNK, query_back, 0)
        e = acc[...]
        xhat = (base_of(g) - stats[g, :, 4:5]) * stats[g, :, 1:2]
        gains(0, e, xhat)
        grad_base = hid[...] + norm_back(e, params[0:1], xhat, stats[g, :, 1:2])
        g_embed[...] += grad_base
        hid[...] = grad_base

        def key_back(i, _):
            acc[:, cols(i)] = dot(keep[:, 2 * width:4 * width], qkv_w[cols(i), width:3 * width], NT)
            return 0
        lax.fori_loop(0, width // CHUNK, key_back, 0)
        e = acc[...]
        xhat = (src[g].astype(WIDE) - stats[g, :, 3:4]) * stats[g, :, 0:1]
        gains(2, e, xhat)
        grad_source = norm_back(e, params[2:3], xhat, stats[g, :, 0:1])

        @pl.when(g > 0)
        def _():
            grad_store(g - 1).wait()
        wide[...] = grad_source

        @pl.when(section == 1)
        def _():
            @pl.when(g > 0)
            def _():
                relay_back(g - 1).wait_send()
            low = (wide[...] + hid[...]).astype(LOW)
            passed[...] = low
            relay_back(g).start()
            wide[...] = low.astype(WIDE)
        grad_store(g).start()
        total = wide[...]
        squares[pl.ds(g, 1), :] = jnp.broadcast_to(
            jnp.sum(jnp.sum(total * total, axis=0, keepdims=True), axis=1, keepdims=True), (1, squares.shape[1]))
        return 0

    lax.fori_loop(0, groups, backward, 0)
    for k in range(6):
        right_store(groups - 1, k).wait()
    grad_store(groups - 1).wait()

    @pl.when(section == 1)
    def _():
        relay_back(groups - 1).wait_send()


def layers(tokens, cotangent, mask, embed, params, w_qkv, w_out, w_up, w_down, cid):
    groups, slots, width = tokens.shape
    units = w_up.shape[1]
    rows = groups * slots
    hbm = pl.BlockSpec(memory_space=pl.ANY)
    vmem = pl.BlockSpec(memory_space=pltpu.VMEM)
    shape = jax.ShapeDtypeStruct
    return pl.pallas_call(
        functools.partial(layers_kernel, groups),
        out_shape=(
            shape((rows, units + 4 * width), LOW),
            shape((rows, units + 5 * width), LOW),
            shape((groups, slots, width), WIDE),
            shape((groups, slots, width), WIDE),
            shape((8, width), WIDE),
            shape((slots, width), WIDE),
            shape((groups, 128), WIDE),
        ),
        in_specs=[hbm, hbm, vmem, hbm, vmem, hbm, hbm, hbm, hbm],
        out_specs=(hbm, hbm, hbm, hbm, vmem, vmem, vmem),
        scratch_shapes=[
            pltpu.VMEM(w_qkv.shape, LOW),
            pltpu.VMEM(w_out.shape, LOW),
            pltpu.VMEM(w_up.shape, LOW),
            pltpu.VMEM(w_down.shape, LOW),
            pltpu.VMEM((slots, width), LOW),
            pltpu.VMEM((groups, slots, width), LOW),
            pltpu.VMEM((groups, slots, width), LOW),
            pltpu.VMEM((groups, slots, 3 * width), LOW),
            pltpu.VMEM((groups, HEADS, slots, slots), LOW),
            pltpu.VMEM((groups, slots, units), LOW),
            pltpu.VMEM((groups, slots, width), LOW),
            pltpu.VMEM((groups, slots, 128), WIDE),
            pltpu.VMEM((slots, units), LOW),
            pltpu.VMEM((slots, 4 * width), LOW),
            pltpu.VMEM((slots, width), LOW),
            pltpu.VMEM((slots, width), WIDE),
            pltpu.VMEM((slots, width), WIDE),
            pltpu.VMEM((slots, width), WIDE),
            pltpu.VMEM((2, slots, CHUNK), WIDE),
            pltpu.SemaphoreType.DMA((5,)),
            pltpu.SemaphoreType.DMA((2 * groups,)),
            pltpu.SemaphoreType.DMA((5,)),
            pltpu.SemaphoreType.DMA((6,)),
            pltpu.SemaphoreType.DMA((2,)),
            pltpu.SemaphoreType.DMA((2 * groups,)),
            pltpu.SemaphoreType.DMA((2 * groups,)),
        ],
        compiler_params=pltpu.CompilerParams(
            collective_id=cid, has_side_effects=True, vmem_limit_bytes=63 * 2**20),
        cost_estimate=pl.CostEstimate(flops=54 * 10**9, bytes_accessed=120 * 2**20, transcendentals=10**7),
    )(tokens, cotangent, mask, embed, params, w_qkv, w_out, w_up, w_down)


def body(tokens, clip_frames, cotangent, embed, norm_params, w_qkv, w_out, w_up, w_down):
    is_first = lax.axis_index("section") == 0
    groups, slots, width = tokens.shape
    units = w_up.shape[-1]
    slot_ids = jnp.arange(slots, dtype=jnp.int32)
    visible = (slot_ids[None, :] < clip_frames[:, None] * (slots // 16)) | jnp.logical_not(is_first)
    mask = jnp.broadcast_to(visible[:, None, :].astype(WIDE), (groups, 8, slots))
    lefts, rights, outcome, grad_inputs, g_params, g_embed, squares = layers(
        tokens, cotangent, mask, embed[0], norm_params[0], w_qkv[0], w_out[0], w_up[0], w_down[0], 2
    )
    magnitude = jnp.sqrt(squares[:, 0] / (slots * width) + 1e-06)
    factors = 1.0 + jnp.arange(width, dtype=WIDE) / width
    row = (jnp.sum(magnitude) * factors)[None]
    extras = jnp.stack(
        [g_embed, jnp.concatenate([g_params[:6], row, jnp.zeros((TILE - 7, width), WIDE)])]
    ).astype(LOW)
    sums = weight_sums(lines_of(lax.axis_size("dp")), lefts, rights, extras, 1)
    overall = jnp.sum(sums[49, 6].astype(WIDE)) / jnp.sum(factors)
    norms = magnitude / (overall / (groups * lax.axis_size("dp")))
    blocks = sums[:48].reshape(12, width, width)
    beside = lambda first, last: (
        blocks[first:last].transpose(1, 0, 2).reshape(width, -1).astype(WIDE)
    )
    return (
        outcome[None],
        grad_inputs[None],
        beside(9, 12)[None],
        beside(8, 9)[None],
        beside(4, 8)[None],
        blocks[0:4].reshape(units, width).astype(WIDE)[None],
        sums[49, :6].astype(WIDE)[None],
        sums[48].astype(WIDE)[None],
        norms[None],
    )


def solution(mesh):
    placed = (
        P("dp", None, None),
        P("dp"),
        P("dp", None, None),
        P("section", None, None),
        P("section", None, None),
        P("section", None, None),
        P("section", None, None),
        P("section", None, None),
        P("section", None, None),
    )
    return jax.shard_map(
        body,
        mesh=mesh,
        in_specs=placed,
        out_specs=(
            P("section", "dp", None, None),
            P("section", "dp", None, None),
            P("section", None, None),
            P("section", None, None),
            P("section", None, None),
            P("section", None, None),
            P("section", None, None),
            P("section", None, None),
            P("section", "dp"),
        ),
        check_vma=False,
    )
```

```python
import functools

import jax
import jax.numpy as jnp
from jax import lax
from jax.experimental import pallas as pl
from jax.experimental.pallas import tpu as pltpu
from jax.sharding import PartitionSpec as P

MESH = pl.DeviceIdType.MESH
TILE = 256
RING = 8
WIDTH = 1024
SPLIT = (80, 64, 48, 64)
ORDERS = ((2, 1, 0), (1, 2, 0), (0, 2, 1), (0, 1, 2))


def lines_of(size):
    short = 1
    while 2 * short**3 < size:
        short += 1
    assert 2 * short**3 == size
    return (2 * short, short, short)


class Plan:
    def __init__(self, dims):
        d = lax.axis_index("dp")
        self.d = d
        self.dims = dims
        self.strides = (dims[1] * dims[2], dims[2], 1)
        self.coords = tuple(lax.rem(lax.div(d, s), n) for s, n in zip(self.strides, dims))
        self.depth = 2 * (sum(dims) - 3)


def stages(plan):
    found = []
    row = 0
    for kind, order in enumerate(ORDERS):
        delay = 0
        left, free = 0, 0
        active = None
        bases = []
        for phase, axis in enumerate(order):
            n, c = plan.dims[axis], plan.coords[axis]
            w = WIDTH >> (phase + 1)
            bases.append((delay, left, free, active, axis, w))
            delay += n - 1
            top = c == n - 1
            left = left + jnp.where(top, w, 0)
            free = free + jnp.where(top, 0, w)
            if n > 2:
                end = (c == 0) | top
                active = end if active is None else active & end
        for phase in range(3):
            found.append(("sum", kind, phase, row) + tuple(bases[phase]))
        for phase in (2, 1, 0):
            _, left, free, active, axis, w = bases[phase]
            found.append(("spread", kind, phase, row, delay, left, free, active, axis, w))
            delay += plan.dims[axis] - 1
        row += SPLIT[kind]
    return found


def both(*terms):
    out = None
    for t in terms:
        if t is None:
            continue
        out = t if out is None else out & t
    return out


def copies(plan, stage, up, tick, total, held, landing, result, send_sem, recv_sem):
    what, kind, phase, row, delay, left, free, active, axis, w = stage
    n, c, stride = plan.dims[axis], plan.coords[axis], plan.strides[axis]
    toward_top = up if what == "sum" else not up
    hops = c if toward_top else n - 1 - c
    job = tick - delay - hops
    ok = both(job >= 0, job < total, active)
    job = jnp.clip(job, 0, total - 1)
    rows = pl.ds(row, SPLIT[kind])
    col = pl.ds(pl.multiple_of(left + (w if up else 0), 128), w)
    stream = (kind * 6 + (phase if what == "sum" else 3 + phase)) * 2 + int(up)
    if what == "sum":
        land = pl.ds(pl.multiple_of(free + (w if up else 0), 128), w)
        src = held.at[job, rows, col]
        dst = landing.at[job, rows, land]
    else:
        src = result.at[job, rows, col]
        dst = result.at[job, rows, col]
    step = stride if toward_top else -stride
    def make(source):
        return pltpu.make_async_remote_copy(
            src_ref=source, dst_ref=dst,
            send_sem=send_sem.at[stream, lax.rem(job, RING)], recv_sem=recv_sem.at[stream, job],
            device_id={"dp": plan.d + step}, device_id_type=MESH)
    def send(source):
        copy = make(source)
        @pl.when(job >= RING)
        def _():
            copy.wait_send()
        copy.start()
    return make, send, src, dst, ok, hops, n, job, rows, col


def comm_tick(plan, table, kinds, tick, total, held, landing, result, send_sem, recv_sem, own_sem):
    for stage in table:
        what, kind, phase = stage[:3]
        if kind not in kinds:
            continue
        for up in (True, False):
            make, send, src, dst, ok, hops, n, job, rows, col = copies(
                plan, stage, up, tick, total, held, landing, result, send_sem, recv_sem)
            if what == "sum":
                @pl.when(ok & (hops > 0))
                def _():
                    make(src).wait_recv()
                    held[job, rows, col] = held[job, rows, col] + dst[...]
                @pl.when(ok & (hops < n - 1))
                def _():
                    send(src)
            else:
                if phase == 2:
                    @pl.when(ok & (hops == 0))
                    def _():
                        mine = held.at[job, rows, col]
                        send(mine)
                        pltpu.make_async_copy(mine, dst, own_sem.at[kind, job]).start()
                    @pl.when(ok & (hops > 0))
                    def _():
                        make(src).wait_recv()
                    if n > 2:
                        @pl.when(ok & (hops > 0) & (hops < n - 1))
                        def _():
                            send(src)
                else:
                    if phase == 1:
                        last = [s for s in table if s[1] == kind and s[0] == "spread" and s[2] == 2][0]
                        _, _, _, _, _, left3, _, active3, axis3, w3 = last
                        c3, n3 = plan.coords[axis3], plan.dims[axis3]
                        top3 = c3 == n3 - 1
                        own = held.at[job, rows, pl.ds(pl.multiple_of(left3 + jnp.where(top3, w3, 0), 128), w3)]
                        own_dst = result.at[job, rows, pl.ds(pl.multiple_of(left3 + jnp.where(top3, w3, 0), 128), w3)]
                        @pl.when(both(ok, hops == 0, (c3 == 0) | top3 if n3 > 2 else None))
                        def _():
                            pltpu.make_async_copy(own, own_dst, own_sem.at[kind, job]).wait()
                    @pl.when(ok & (hops > 0))
                    def _():
                        make(src).wait_recv()
                    @pl.when(ok & (hops < n - 1))
                    def _():
                        send(src)


def drain(plan, table, tick, total, held, landing, result, send_sem, recv_sem):
    for stage in table:
        what, kind, phase = stage[:3]
        for up in (True, False):
            make, send, src, dst, ok, hops, n, job, rows, col = copies(
                plan, stage, up, tick, total, held, landing, result, send_sem, recv_sem)
            @pl.when(ok & (hops < n - 1) & (job >= total - RING))
            def _():
                make(src).wait_send()


def greet(plan):
    barrier = pltpu.get_barrier_semaphore()
    count = 0
    for n, c, s in zip(plan.dims, plan.coords, plan.strides):
        for inside, step in ((c > 0, -s), (c < n - 1, s)):
            @pl.when(inside)
            def _():
                pl.semaphore_signal(barrier, inc=1, device_id={"dp": plan.d + step}, device_id_type=MESH)
            count = count + inside.astype(jnp.int32)
    pl.semaphore_wait(barrier, count)


def weights_kernel(dims, jobs, extra, left_ref, right_ref, extra_ref, result, held, landing,
                   left_buf, right_buf, load_sem, send_sem, recv_sem, own_sem):
    plan = Plan(dims)
    table = stages(plan)
    total = 4 * jobs + extra
    greet(plan)

    def left_copy(s):
        job, part, slot = lax.div(s, 4), lax.rem(s, 4), lax.rem(s, 2)
        slab = jnp.where(job < 4, job, jnp.where(job < 8, 4, jnp.minimum(job - 3, 7)))
        return pltpu.make_async_copy(
            left_ref.at[:, pl.ds(pl.multiple_of(slab * WIDTH + part * TILE, TILE), TILE)],
            left_buf.at[slot], load_sem.at[slot])

    def right_copy(job):
        slot = lax.rem(job, 2)
        slab = jnp.where(job < 4, 0, job - 3)
        return pltpu.make_async_copy(
            right_ref.at[:, pl.ds(pl.multiple_of(slab * WIDTH, WIDTH), WIDTH)],
            right_buf.at[slot], load_sem.at[2 + slot])

    def product(s):
        job = lax.div(s, 4)
        left_copy(s).wait()
        @pl.when(lax.rem(s, 4) == 0)
        def _():
            right_copy(job).wait()
            @pl.when(job + 1 < jobs)
            def _():
                right_copy(job + 1).start()
        @pl.when(s + 1 < 4 * jobs)
        def _():
            left_copy(s + 1).start()
        a = left_buf[lax.rem(s, 2)]
        b = right_buf[lax.rem(job, 2)]
        held[s] = lax.dot_general(a, b, (((0,), (0,)), ((), ())), preferred_element_type=jnp.float32).astype(jnp.bfloat16)

    extras = pltpu.make_async_copy(extra_ref, held.at[pl.ds(4 * jobs, extra)], load_sem.at[4])
    extras.start()
    left_copy(0).start()
    right_copy(0).start()
    product(0)
    extras.wait()

    args = (total, held, landing, result, send_sem, recv_sem)

    def tick(t, _):
        comm_tick(plan, table, (0, 2), t, *args, own_sem)
        @pl.when(t + 1 < 4 * jobs)
        def _():
            product(t + 1)
        comm_tick(plan, table, (1, 3), t, *args, own_sem)
        return 0

    lax.fori_loop(0, total + plan.depth, tick, 0)

    def finish(t, _):
        drain(plan, table, t, *args)
        return 0

    lax.fori_loop(0, total + plan.depth, finish, 0)


def weight_sums(dims, lefts, rights, extras, cid):
    jobs, extra = 12, extras.shape[0]
    total = 4 * jobs + extra
    rows = lefts.shape[0]
    any_space = pl.BlockSpec(memory_space=pl.ANY)
    return pl.pallas_call(
        functools.partial(weights_kernel, dims, jobs, extra),
        out_shape=jax.ShapeDtypeStruct((total, TILE, WIDTH), jnp.bfloat16),
        in_specs=[any_space] * 3,
        out_specs=any_space,
        scratch_shapes=[
            pltpu.VMEM((total, TILE, WIDTH), jnp.bfloat16),
            pltpu.VMEM((total, TILE, WIDTH), jnp.bfloat16),
            pltpu.VMEM((2, rows, TILE), jnp.bfloat16),
            pltpu.VMEM((2, rows, WIDTH), jnp.bfloat16),
            pltpu.SemaphoreType.DMA((5,)),
            pltpu.SemaphoreType.DMA((48, RING)),
            pltpu.SemaphoreType.DMA((48, total)),
            pltpu.SemaphoreType.DMA((4, total)),
        ],
        compiler_params=pltpu.CompilerParams(collective_id=cid, has_side_effects=True, vmem_limit_bytes=62 * 2**20),
        cost_estimate=pl.CostEstimate(flops=2 * 12 * rows * WIDTH * WIDTH, bytes_accessed=100 * 2**20, transcendentals=0),
    )(lefts, rights, extras)


HEADS = 8
CHUNK = 1024
LOW = jnp.bfloat16
WIDE = jnp.float32
NN = (((1,), (0,)), ((), ()))
NT = (((1,), (1,)), ((), ()))
TN = (((0,), (0,)), ((), ()))


def dot(a, b, form):
    return lax.dot_general(a, b, form, preferred_element_type=WIDE)


def normalize(values):
    center = values - jnp.mean(values, -1, keepdims=True)
    inverse = lax.rsqrt(jnp.mean(center * center, -1, keepdims=True) + 1e-05)
    return center * inverse, inverse


def norm_back(upstream, gain, xhat, inverse):
    scaled = upstream * gain
    return inverse * (scaled - jnp.mean(scaled, -1, keepdims=True)
                      - xhat * jnp.mean(scaled * xhat, -1, keepdims=True))


def gelu_pair(u):
    c = 0.7978845608028654
    square = u * u
    t = jnp.tanh(u * (c + (c * 0.044715) * square))
    half = 0.5 * (1.0 + t)
    slope = half + (0.5 * u) * (1.0 - t * t) * (c + (3.0 * c * 0.044715) * square)
    return u * half, slope


def layers_kernel(groups, tokens, cotangent, mask, embed, params, w_qkv, w_out, w_up, w_down,
                  lefts, rights, sec_out, sec_grad, g_params, g_embed, squares,
                  qkv_w, out_w, up_w, down_w, emb, src, upstream, qkv, probs, slopes, xhat_f, stats,
                  keep, passed, acc, hid, u_buf,
                  w_sem, in_sem, left_sem, right_sem, wide_sem, send_sem, recv_sem):
    section = lax.axis_index("section")
    first = section == 0
    other = 1 - section
    slots, width = emb.shape
    units = up_w.shape[1]
    steps = units // CHUNK
    head = width // HEADS
    scale = head ** -0.5

    loads = [pltpu.make_async_copy(a, b, w_sem.at[k]) for k, (a, b) in enumerate(
        ((w_qkv, qkv_w), (w_out, out_w), (w_up, up_w), (w_down, down_w), (embed, emb)))]
    loads[4].start()
    loads[0].start()

    def token_load(g):
        return pltpu.make_async_copy(tokens.at[g], src.at[g], in_sem.at[g])

    def cot_load(g):
        return pltpu.make_async_copy(cotangent.at[g], upstream.at[g], in_sem.at[groups + g])

    @pl.when(first)
    def _():
        for g in range(groups):
            token_load(g).start()
    for k in (1, 2, 3):
        loads[k].start()

    barrier = pltpu.get_barrier_semaphore()
    pl.semaphore_signal(barrier, inc=1, device_id={"section": other}, device_id_type=MESH)
    pl.semaphore_wait(barrier, 1)

    def relay(g):
        return pltpu.make_async_remote_copy(
            src_ref=passed, dst_ref=src.at[g], send_sem=send_sem.at[g], recv_sem=recv_sem.at[g],
            device_id={"section": other}, device_id_type=MESH)

    def relay_back(g):
        return pltpu.make_async_remote_copy(
            src_ref=passed, dst_ref=upstream.at[g], send_sem=send_sem.at[groups + g],
            recv_sem=recv_sem.at[groups + g], device_id={"section": other}, device_id_type=MESH)

    def rows_of(g):
        return pl.ds(pl.multiple_of(g * slots, slots), slots)

    def cols(i, w=CHUNK):
        return pl.ds(pl.multiple_of(i * w, w), w)

    def left_store(g, k):
        return pltpu.make_async_copy(
            keep.at[:, pl.ds((k - 1) * width, width)], lefts.at[rows_of(g), pl.ds(units + (k - 1) * width, width)], left_sem.at[k])

    def right_store(g, k):
        if k == 0:
            return pltpu.make_async_copy(upstream.at[g], rights.at[rows_of(g), pl.ds(0, width)], right_sem.at[0])
        return pltpu.make_async_copy(
            keep.at[:, pl.ds((k - 2) * width, width)],
            rights.at[rows_of(g), pl.ds(width + units + (k - 2) * width, width)], right_sem.at[k])

    def left_chunk(g, i):
        return pltpu.make_async_copy(
            upstream.at[i], lefts.at[rows_of(g), pl.ds(i * CHUNK, CHUNK)], left_sem.at[5 + i])

    def right_chunk(g, i):
        return pltpu.make_async_copy(
            slopes.at[g, :, pl.ds(i * CHUNK, CHUNK)],
            rights.at[rows_of(g), pl.ds(width + i * CHUNK, CHUNK)], right_sem.at[6 + i])

    def out_store(g):
        return pltpu.make_async_copy(acc, sec_out.at[g], wide_sem.at[0])

    def grad_store(g):
        return pltpu.make_async_copy(acc, sec_grad.at[g], wide_sem.at[1])

    def base_of(g):
        return jnp.where(first, 0.0, src[g].astype(WIDE)) + emb[...].astype(WIDE)

    stage = pl.when(section >= 0)

    def heads_of(g, h):
        return tuple(qkv[g, :, k * width + h * head:k * width + (h + 1) * head] for k in range(3))

    def forward(g):
        @pl.when(first)
        def _():
            token_load(g).wait()
        @pl.when(section == 1)
        def _():
            relay(g).wait_recv()

        @stage
        def _():
            @pl.when(g == 0)
            def _():
                loads[4].wait()

            @pl.when(g > 0)
            def _():
                for k in (3, 4):
                    left_store(g - 1, k).wait()
            source = src[g].astype(WIDE)
            xhat, inverse = normalize(source)
            stats[g, :, 0:1] = inverse
            stats[g, :, 3:4] = jnp.mean(source, -1, keepdims=True)
            keep[:, 3 * width:4 * width] = (xhat * params[2:3] + params[3:4]).astype(LOW)
            @pl.when(g == 0)
            def _():
                loads[0].wait()
            for k, rows in ((1, 3), (2, 3)):
                part = slice(k * width, (k + 1) * width)
                qkv[g, :, part] = dot(keep[:, rows * width:(rows + 1) * width], qkv_w[:, part], NN).astype(LOW)
            base = base_of(g)
            xhat, inverse = normalize(base)
            stats[g, :, 1:2] = inverse
            stats[g, :, 4:5] = jnp.mean(base, -1, keepdims=True)
            keep[:, 2 * width:3 * width] = (xhat * params[0:1] + params[1:2]).astype(LOW)
            qkv[g, :, 0:width] = dot(keep[:, 2 * width:3 * width], qkv_w[:, 0:width], NN).astype(LOW)
            left_store(g, 3).start()
            left_store(g, 4).start()

        @stage
        def _():
            @pl.when(g > 0)
            def _():
                for k in (1, 2):
                    left_store(g - 1, k).wait()
            seen = mask[g, 0:1, :] > 0
            for h in range(HEADS):
                q, k, v = heads_of(g, h)
                s = jnp.where(seen, dot(q, k, NT) * scale, -1e30)
                e = jnp.exp(s - jnp.max(s, -1, keepdims=True))
                p = (e / jnp.sum(e, -1, keepdims=True)).astype(LOW)
                probs[g, h] = p
                keep[:, width + h * head:width + (h + 1) * head] = dot(p, v, NN).astype(LOW)
            left_store(g, 2).start()
            @pl.when(g == 0)
            def _():
                loads[1].wait()

        @stage
        def _():
            hid[...] = dot(keep[:, width:2 * width], out_w[...], NN)
            hidden = base_of(g) + hid[...]
            hid[...] = hidden
            xhat, inverse = normalize(hidden)
            stats[g, :, 2:3] = inverse
            xhat_f[g] = xhat.astype(LOW)
            keep[:, 0:width] = (xhat * params[4:5] + params[5:6]).astype(LOW)
            left_store(g, 1).start()
            @pl.when(g == 0)
            def _():
                loads[2].wait()
                loads[3].wait()

            @pl.when(g > 0)
            def _():
                out_store(g - 1).wait()
                for i in range(steps):
                    left_chunk(g - 1, i).wait()

        @stage
        def _():
            chunks = [slice(i * CHUNK, (i + 1) * CHUNK) for i in range(steps)]
            u_buf[0] = dot(keep[:, 0:width], up_w[:, chunks[0]], NN)
            for i, part in enumerate(chunks):
                if i + 1 < steps:
                    u_buf[(i + 1) % 2] = dot(keep[:, 0:width], up_w[:, chunks[i + 1]], NN)
                value, slope = gelu_pair(u_buf[i % 2])
                slopes[g, :, part] = slope.astype(LOW)
                value = value.astype(LOW)
                upstream[i] = value
                term = dot(value, down_w[part, :], NN)
                if i == 0:
                    acc[...] = hid[...] + term
                else:
                    acc[...] += term
            for i in range(steps):
                left_chunk(g, i).start()
            out_store(g).start()

        @pl.when(first)
        def _():
            @pl.when(g > 0)
            def _():
                relay(g - 1).wait_send()
                @pl.when(g == groups - 1)
                def _():
                    for i in range(steps):
                        left_chunk(g, i).wait()
            passed[...] = acc[...].astype(LOW)
            relay(g).start()

    pl.loop(0, groups)(forward)

    for k in range(1, 5):
        left_store(groups - 1, k).wait()
    out_store(groups - 1).wait()

    @pl.when(first)
    def _():
        relay(groups - 1).wait_send()

    @pl.when(section == 1)
    def _():
        for i in range(steps):
            left_chunk(groups - 1, i).wait()
        for g in range(groups):
            cot_load(g).start()

    g_params[...] = jnp.zeros_like(g_params)
    g_embed[...] = jnp.zeros_like(g_embed)
    squares[...] = jnp.zeros_like(squares)

    def gains(row, e, xhat):
        g_params[row:row + 1] += jnp.sum(e * xhat, axis=0, keepdims=True)
        g_params[row + 1:row + 2] += jnp.sum(e, axis=0, keepdims=True)

    def backward(g):
        @pl.when(first)
        def _():
            relay_back(g).wait_recv()
        @pl.when(section == 1)
        def _():
            cot_load(g).wait()

        @stage
        def _():
            @pl.when(g > 0)
            def _():
                for k in (2, 3, 4, 5):
                    right_store(g - 1, k).wait()
                right_store(g - 1, 0).wait()
                for i in range(steps):
                    right_chunk(g - 1, i).wait()
                grad_store(g - 1).wait()
            right_store(g, 0).start()
            chunks = [slice(i * CHUNK, (i + 1) * CHUNK) for i in range(steps)]
            u_buf[0] = dot(upstream[g], down_w[chunks[0], :], NT)
            for i, part in enumerate(chunks):
                if i + 1 < steps:
                    u_buf[(i + 1) % 2] = dot(upstream[g], down_w[chunks[i + 1], :], NT)
                value = (u_buf[i % 2] * slopes[g, :, part].astype(WIDE)).astype(LOW)
                slopes[g, :, part] = value
                term = dot(value, up_w[:, part], NT)
                if i == 0:
                    acc[...] = term
                else:
                    acc[...] += term

        @stage
        def _():
            for i in range(steps):
                right_chunk(g, i).start()
            e = acc[...]
            xhat = xhat_f[g].astype(WIDE)
            gains(4, e, xhat)
            grad_hidden = upstream[g].astype(WIDE) + norm_back(e, params[4:5], xhat, stats[g, :, 2:3])
            hid[...] = grad_hidden
            keep[:, 0:width] = grad_hidden.astype(LOW)
            xhat_f[g] = dot(keep[:, 0:width], out_w[...], NT).astype(LOW)

        @stage
        def _():
            for h in range(HEADS):
                q, k, v = heads_of(g, h)
                m = xhat_f[g, :, h * head:(h + 1) * head]
                low = probs[g, h]
                p = low.astype(WIDE)
                gp = dot(m, v, NT)
                ds = (p * (gp - jnp.sum(gp * p, -1, keepdims=True))).astype(LOW)
                keep[:, width + h * head:width + (h + 1) * head] = (dot(ds, k, NN) * scale).astype(LOW)
                keep[:, 2 * width + h * head:2 * width + (h + 1) * head] = (dot(ds, q, TN) * scale).astype(LOW)
                keep[:, 3 * width + h * head:3 * width + (h + 1) * head] = dot(low, m, TN).astype(LOW)
            for k in (2, 3, 4, 5):
                right_store(g, k).start()

        @stage
        def _():
            acc[...] = dot(keep[:, width:2 * width], qkv_w[:, 0:width], NT)
            u_buf[0] = dot(keep[:, 2 * width:4 * width], qkv_w[:, width:3 * width], NT)
            e = acc[...]
            xhat = (base_of(g) - stats[g, :, 4:5]) * stats[g, :, 1:2]
            gains(0, e, xhat)
            grad_base = hid[...] + norm_back(e, params[0:1], xhat, stats[g, :, 1:2])
            g_embed[...] += grad_base
            hid[...] = grad_base

        @stage
        def _():
            e = u_buf[0]
            xhat = (src[g].astype(WIDE) - stats[g, :, 3:4]) * stats[g, :, 0:1]
            gains(2, e, xhat)
            acc[...] = norm_back(e, params[2:3], xhat, stats[g, :, 0:1])

        @pl.when(section == 1)
        def _():
            @pl.when(g > 0)
            def _():
                relay_back(g - 1).wait_send()
            low = (acc[...] + hid[...]).astype(LOW)
            passed[...] = low
            relay_back(g).start()
            acc[...] = low.astype(WIDE)
        grad_store(g).start()
        total = acc[...]
        squares[pl.ds(g, 1), :] = jnp.broadcast_to(
            jnp.sum(jnp.sum(total * total, axis=0, keepdims=True), axis=1, keepdims=True), (1, squares.shape[1]))

    pl.loop(0, groups)(backward)

    for k in (0, 2, 3, 4, 5):
        right_store(groups - 1, k).wait()
    for i in range(steps):
        right_chunk(groups - 1, i).wait()
    grad_store(groups - 1).wait()

    @pl.when(section == 1)
    def _():
        relay_back(groups - 1).wait_send()


def layers(tokens, cotangent, mask, embed, params, w_qkv, w_out, w_up, w_down, cid):
    groups, slots, width = tokens.shape
    units = w_up.shape[1]
    rows = groups * slots
    hbm = pl.BlockSpec(memory_space=pl.ANY)
    vmem = pl.BlockSpec(memory_space=pltpu.VMEM)
    shape = jax.ShapeDtypeStruct
    return pl.pallas_call(
        functools.partial(layers_kernel, groups),
        out_shape=(
            shape((rows, units + 4 * width), LOW),
            shape((rows, units + 5 * width), LOW),
            shape((groups, slots, width), WIDE),
            shape((groups, slots, width), WIDE),
            shape((8, width), WIDE),
            shape((slots, width), WIDE),
            shape((groups, 128), WIDE),
        ),
        in_specs=[hbm, hbm, vmem, hbm, vmem, hbm, hbm, hbm, hbm],
        out_specs=(hbm, hbm, hbm, hbm, vmem, vmem, vmem),
        scratch_shapes=[
            pltpu.VMEM(w_qkv.shape, LOW),
            pltpu.VMEM(w_out.shape, LOW),
            pltpu.VMEM(w_up.shape, LOW),
            pltpu.VMEM(w_down.shape, LOW),
            pltpu.VMEM((slots, width), LOW),
            pltpu.VMEM((groups, slots, width), LOW),
            pltpu.VMEM((max(groups, units // CHUNK), slots, width), LOW),
            pltpu.VMEM((groups, slots, 3 * width), LOW),
            pltpu.VMEM((groups, HEADS, slots, slots), LOW),
            pltpu.VMEM((groups, slots, units), LOW),
            pltpu.VMEM((groups, slots, width), LOW),
            pltpu.VMEM((groups, slots, 128), WIDE),
            pltpu.VMEM((slots, 4 * width), LOW),
            pltpu.VMEM((slots, width), LOW),
            pltpu.VMEM((slots, width), WIDE),
            pltpu.VMEM((slots, width), WIDE),
            pltpu.VMEM((2, slots, CHUNK), WIDE),
            pltpu.SemaphoreType.DMA((5,)),
            pltpu.SemaphoreType.DMA((2 * groups,)),
            pltpu.SemaphoreType.DMA((5 + units // CHUNK,)),
            pltpu.SemaphoreType.DMA((6 + units // CHUNK,)),
            pltpu.SemaphoreType.DMA((2,)),
            pltpu.SemaphoreType.DMA((2 * groups,)),
            pltpu.SemaphoreType.DMA((2 * groups,)),
        ],
        compiler_params=pltpu.CompilerParams(
            collective_id=cid, has_side_effects=True, vmem_limit_bytes=63 * 2**20),
        cost_estimate=pl.CostEstimate(flops=54 * 10**9, bytes_accessed=120 * 2**20, transcendentals=10**7),
    )(tokens, cotangent, mask, embed, params, w_qkv, w_out, w_up, w_down)


def widen_kernel(ranges, block, *outs):
    step = pl.program_id(0)
    for (first, last), out in zip(ranges, outs):
        @pl.when((step >= first) & (step < last))
        def _():
            out[...] = block[0].astype(out.dtype)


def widen(sums, places):
    tile, width = sums.shape[1:]
    steps = sum(p[1] for p in places)

    def place(first, count, tall, wide):
        def index(step):
            k = jnp.clip(step - first, 0, count - 1)
            if wide == 1:
                return k, 0
            return lax.rem(k, tall), lax.div(k, tall)
        return pl.BlockSpec((tile, width), index)

    return pl.pallas_call(
        lambda *refs: widen_kernel(tuple((p[0], p[0] + p[1]) for p in places), *refs),
        grid=(steps,),
        out_shape=tuple(jax.ShapeDtypeStruct((p[2] * tile, p[3] * width), jnp.float32) for p in places),
        in_specs=[pl.BlockSpec((1, tile, width), lambda step: (step, 0, 0))],
        out_specs=tuple(place(*p) for p in places),
        compiler_params=pltpu.CompilerParams(vmem_limit_bytes=32 * 2**20),
        cost_estimate=pl.CostEstimate(flops=0, bytes_accessed=6 * steps * tile * width, transcendentals=0),
    )(sums)


def body(tokens, clip_frames, cotangent, embed, norm_params, w_qkv, w_out, w_up, w_down):
    is_first = lax.axis_index("section") == 0
    groups, slots, width = tokens.shape
    units = w_up.shape[-1]
    slot_ids = jnp.arange(slots, dtype=jnp.int32)
    visible = (slot_ids[None, :] < clip_frames[:, None] * (slots // 16)) | jnp.logical_not(is_first)
    mask = jnp.broadcast_to(visible[:, None, :].astype(WIDE), (groups, 8, slots))
    lefts, rights, outcome, grad_inputs, g_params, g_embed, squares = layers(
        tokens, cotangent, mask, embed[0], norm_params[0], w_qkv[0], w_out[0], w_up[0], w_down[0], 2
    )
    magnitude = jnp.sqrt(squares[:, 0] / (slots * width) + 1e-06)
    factors = 1.0 + jnp.arange(width, dtype=WIDE) / width
    row = (jnp.sum(magnitude) * factors)[None]
    extras = jnp.stack(
        [g_embed, jnp.concatenate([g_params[:6], row, jnp.zeros((TILE - 7, width), WIDE)])]
    ).astype(LOW)
    sums = weight_sums(lines_of(lax.axis_size("dp")), lefts, rights, extras, 1)
    overall = jnp.sum(sums[49, 6].astype(WIDE)) / jnp.sum(factors)
    norms = magnitude / (overall / (groups * lax.axis_size("dp")))
    down, up, out, qkv = widen(sums, ((0, 16, 16, 1), (16, 16, 4, 4), (32, 4, 4, 1), (36, 12, 4, 3)))
    return (
        outcome[None],
        grad_inputs[None],
        qkv[None],
        out[None],
        up[None],
        down[None],
        sums[49, :6].astype(WIDE)[None],
        sums[48].astype(WIDE)[None],
        norms[None],
    )


def solution(mesh):
    placed = (
        P("dp", None, None),
        P("dp"),
        P("dp", None, None),
        P("section", None, None),
        P("section", None, None),
        P("section", None, None),
        P("section", None, None),
        P("section", None, None),
        P("section", None, None),
    )
    return jax.shard_map(
        body,
        mesh=mesh,
        in_specs=placed,
        out_specs=(
            P("section", "dp", None, None),
            P("section", "dp", None, None),
            P("section", None, None),
            P("section", None, None),
            P("section", None, None),
            P("section", None, None),
            P("section", None, None),
            P("section", None, None),
            P("section", "dp"),
        ),
        check_vma=False,
    )
```

```python
import functools

import jax
import jax.numpy as jnp
from jax import lax
from jax.experimental import pallas as pl
from jax.experimental.pallas import tpu as pltpu
from jax.sharding import PartitionSpec as P

MESH = pl.DeviceIdType.MESH
TILE = 256
WIDTH = 1024
RING = 8
SHARES = (
    (0, 80, 2, ((1, 0),), False),
    (160, 48, 0, ((2, 1), (1, 2)), False),
    (208, 48, 0, ((1, 2), (2, 1)), True),
    (80, 80, 1, ((2, 0),), False),
)
MIDDLE_ROWS = 48


def lines_of(size):
    short = 1
    while 2 * short**3 < size:
        short += 1
    assert 2 * short**3 == size
    return (2 * short, short, short)


def both(*terms):
    out = None
    for t in terms:
        if t is not None:
            out = t if out is None else out & t
    return out


def lanes_of(n, wide):
    return 1 if n == 2 else 4 if wide else 2


class Flow:
    def __init__(self, row, count, middle, phase, axis, n, c, w, owners, left, free, active, parity, lag, summing):
        self.row, self.count, self.middle, self.phase, self.axis = row, count, middle, phase, axis
        self.n, self.c, self.w, self.owners, self.left, self.free = n, c, w, owners, left, free
        self.active, self.parity, self.lag, self.summing = active, parity, lag, summing


class Own:
    def __init__(self, row, count, left, active, parity, sem, turns):
        self.row, self.count, self.left, self.active = row, count, left, active
        self.parity, self.sem, self.turns = parity, sem, turns


class Plan:
    def __init__(self, dims, total):
        self.d = lax.axis_index("dp")
        self.dims = dims
        self.total = total
        self.strides = (dims[1] * dims[2], dims[2], 1)
        self.coords = tuple(lax.rem(lax.div(self.d, s), n) for s, n in zip(self.strides, dims))
        self.depth = self.streams = self.arrivals = self.owns = 0
        self.shares = [self.lay_out(*share) for share in SHARES]

    def flow(self, **fields):
        f = Flow(**fields)
        f.turns = self.total if f.parity is None else (self.total + 1 - f.parity) // 2
        f.wide = f.middle and f.phase == 0 and f.n > 2
        f.lanes = lanes_of(f.n, f.wide)
        f.stream, f.arrival = self.streams, self.arrivals
        self.streams += f.lanes
        self.arrivals += f.lanes * f.turns
        return f

    def lay_out(self, row, count, axis, orders, middle):
        share = dict(row=row, count=count, middle=middle)

        def phase(p, axis, lag, left, free, active, parity):
            n, c = self.dims[axis], self.coords[axis]
            w = WIDTH >> (p + 1)
            inner = middle and p == 0 and n > 2
            owners = (n // 2 - 1, n // 2) if inner else (0, n - 1)
            top = c == owners[1]
            half = jnp.where(top, w, 0)
            used = 0 if middle and p == 0 else w - half
            now = both(active, (c == owners[0]) | top) if n > 2 else active
            fields = dict(share, phase=p, axis=axis, n=n, c=c, w=w, owners=owners, left=left, free=free,
                          active=active, parity=parity)
            hops = (n // 2 if inner else n - 1, max(owners[1], n - 1 - owners[0]))
            return fields, hops, left + half, free + used, now

        free = 512 if middle else 0
        first, hops, left, free, gate = phase(0, axis, 0, 0, free, None, None)
        start = hops[0]
        inner = []
        for parity, order in enumerate(orders):
            key = None if len(orders) == 1 else parity
            lag = start
            second, hops2, left2, free2, gate2 = phase(1, order[0], lag, left, free, gate, key)
            third, hops3, left3, _, gate3 = phase(2, order[1], lag, left2, free2, gate2, key)
            own = Own(row=row, count=count, left=left3, active=gate3, parity=key, sem=self.owns,
                       turns=self.total if key is None else (self.total + 1 - key) // 2)
            self.owns += own.turns
            flows = [self.flow(**second, lag=lag, summing=True)]
            lag += hops2[0]
            flows.append(self.flow(**third, lag=lag, summing=True))
            lag += hops3[0]
            own.start = lag
            flows.append(self.flow(**third, lag=lag, summing=False))
            lag += hops3[1]
            own.end = lag
            flows.append(self.flow(**second, lag=lag, summing=False))
            lag += hops2[1]
            inner.append((key, flows, own))
        before = self.flow(**first, lag=0, summing=True)
        after = self.flow(**first, lag=lag, summing=False)
        self.depth = max(self.depth, lag + hops[1])
        return before, gate, inner, after


def due(plan, job, steady, parity, *terms):
    return both(None if steady else (job >= 0) & (job < plan.total),
                None if parity is None else lax.rem(job, 2) == parity, *terms)


def when(ok):
    return (lambda f: f()) if ok is None else pl.when(ok)


def move(plan, flow, refs, job, cols, spot, step, lane, short=False):
    held, landing, side, result, send_sem, recv_sem = refs
    turn = job if flow.parity is None else lax.div(job, 2)
    rows = pl.ds(flow.row, flow.count)
    at = lambda first: pl.ds(first if isinstance(first, int) else pl.multiple_of(first, 128), flow.w)
    if not flow.summing:
        src = dst = result.at[job, rows, at(cols)]
    else:
        src = held.at[job, rows, at(cols)]
        if short or (flow.middle and flow.phase > 0):
            dst = side.at[job, pl.ds(0, flow.count), at(spot)]
        else:
            dst = landing.at[job, rows, at(spot)]

    def make(source):
        return pltpu.make_async_remote_copy(
            src_ref=source, dst_ref=dst, send_sem=send_sem.at[flow.stream + lane, lax.rem(turn, RING)],
            recv_sem=recv_sem.at[flow.arrival + lane * flow.turns + turn],
            device_id={"dp": plan.d + step}, device_id_type=MESH)

    def send(first_owner=False):
        copy = make(held.at[job, rows, at(cols)] if first_owner else src)
        @pl.when(turn >= RING)
        def _():
            copy.wait_send()
        copy.start()

    def receive():
        make(src).wait_recv()
        if flow.summing:
            place = (job, rows, at(cols))
            held[place] = held[place] + dst[...]

    def finish():
        @pl.when(turn >= flow.turns - RING)
        def _():
            make(src).wait_send()

    return send, receive, finish


def run_flow(plan, flow, tick, refs, steady, ending=False):
    n, c, w, left = flow.n, flow.c, flow.w, flow.left
    stride = plan.strides[flow.axis]
    from_held = not flow.summing and flow.phase == 2
    if n == 2:
        own, other = jnp.where(c == 1, w, 0), jnp.where(c == 1, 0, w)
        out, back = (other, own) if flow.summing else (own, other)
        step = jnp.where(c == 1, -stride, stride)
        job = tick - flow.lag
        send, _, finish = move(plan, flow, refs, job, left + out, flow.free + out, step, 0)
        @when(due(plan, job, steady, flow.parity))
        def _():
            finish() if ending else send(from_held)
        if not ending:
            job = job - 1
            _, receive, _ = move(plan, flow, refs, job, left + back, flow.free + back, step, 0)
            @when(due(plan, job, steady, flow.parity))
            def _():
                receive()
        return
    for up in (True, False):
        owner = flow.owners[int(up)]
        for below in (True, False):
            if (owner if below else n - 1 - owner) == 0:
                continue
            place = c <= owner if below else c >= owner
            if flow.summing:
                hops = c if below else n - 1 - c
                sends = c < owner if below else c > owner
                step = stride if below else -stride
            else:
                hops = owner - c if below else c - owner
                sends = c > 0 if below else c < n - 1
                step = -stride if below else stride
            job = tick - flow.lag - hops
            lower = w if up else 0
            short = flow.summing and flow.middle and flow.phase == 0 and up != below
            if short:
                spot = 0
            elif flow.middle and flow.phase == 0:
                spot = lower
            else:
                spot = flow.free + lower
            send, receive, finish = move(
                plan, flow, refs, job, left + lower, spot, step, 2 * int(up) + int(below) if flow.wide else int(up), short)
            @when(due(plan, job, steady, flow.parity, place, flow.active if flow.phase == 2 else None))
            def _():
                if ending:
                    pl.when(sends)(finish)
                    return
                pl.when(hops > 0)(receive)
                if from_held:
                    pl.when(sends & (hops == 0))(functools.partial(send, True))
                    pl.when(sends & (hops > 0))(send)
                else:
                    pl.when(sends)(send)


def own_copy(plan, own, refs, job, own_sem):
    turn = job if own.parity is None else lax.div(job, 2)
    part = (job, pl.ds(own.row, own.count), pl.ds(pl.multiple_of(own.left, 128), WIDTH >> 3))
    return pltpu.make_async_copy(refs[0].at[part], refs[3].at[part], own_sem.at[own.sem + turn])


def serve(plan, shares, tick, refs, own_sem, steady, ending=False):
    for k in shares:
        before, gate, inner, after = plan.shares[k]
        run_flow(plan, before, tick, refs, steady, ending)

        @when(gate)
        def _():
            for parity, flows, own in inner:
                for flow in flows:
                    if not flow.summing and not ending:
                        opens = flow.phase == 2
                        job = tick - (own.start if opens else own.end)
                        @when(due(plan, job, steady, parity, own.active))
                        def _():
                            copy = own_copy(plan, own, refs, job, own_sem)
                            copy.start() if opens else copy.wait()
                    run_flow(plan, flow, tick, refs, steady, ending)
        run_flow(plan, after, tick, refs, steady, ending)


def greet(plan):
    barrier = pltpu.get_barrier_semaphore()
    count = 0
    for n, c, s in zip(plan.dims, plan.coords, plan.strides):
        for inside, step in ((c > 0, -s), (c < n - 1, s)):
            @pl.when(inside)
            def _():
                pl.semaphore_signal(barrier, inc=1, device_id={"dp": plan.d + step}, device_id_type=MESH)
            count = count + inside.astype(jnp.int32)
    pl.semaphore_wait(barrier, count)


def weights_kernel(dims, tiles, total, left_ref, right_ref, extra_ref, result, held, landing, side,
                   left_buf, right_buf, load_sem, send_sem, recv_sem, own_sem):
    plan = Plan(dims, total)
    per = WIDTH // TILE
    greet(plan)

    def left_copy(s):
        job, part = lax.div(s, per), lax.rem(s, per)
        slab = jnp.where(job < 4, job, jnp.where(job < 8, 4, jnp.minimum(job - 3, 7)))
        return pltpu.make_async_copy(
            left_ref.at[:, pl.ds(pl.multiple_of(slab * WIDTH + part * TILE, TILE), TILE)],
            left_buf, load_sem.at[0])

    def right_copy(job):
        slab = jnp.where(job < 4, 0, job - 3)
        return pltpu.make_async_copy(
            right_ref.at[:, pl.ds(pl.multiple_of(slab * WIDTH, WIDTH), WIDTH)],
            right_buf, load_sem.at[1])

    def product(s):
        left_copy(s).wait()
        @pl.when(lax.rem(s, per) == 0)
        def _():
            right_copy(lax.div(s, per)).wait()
        held[s] = lax.dot_general(
            left_buf[...], right_buf[...], (((0,), (0,)), ((), ())),
            preferred_element_type=jnp.float32).astype(jnp.bfloat16)
        @pl.when(s + 1 < tiles)
        def _():
            left_copy(s + 1).start()
            @pl.when(lax.rem(s + 1, per) == 0)
            def _():
                right_copy(lax.div(s + 1, per)).start()

    extras = pltpu.make_async_copy(extra_ref, held.at[pl.ds(tiles, total - tiles)], load_sem.at[2])
    left_copy(0).start()
    right_copy(0).start()
    extras.start()
    product(0)
    extras.wait()
    refs = (held, landing, side, result, send_sem, recv_sem)

    def tick(steady, t, _):
        serve(plan, (0, 1), t, refs, own_sem, steady)
        @pl.when(t + 1 < tiles)
        def _():
            product(t + 1)
        serve(plan, (2, 3), t, refs, own_sem, steady)
        return 0

    lax.fori_loop(0, plan.depth, functools.partial(tick, False), 0)
    lax.fori_loop(plan.depth, total, functools.partial(tick, True), 0)
    lax.fori_loop(total, total + plan.depth, functools.partial(tick, False), 0)

    def finish(t, _):
        serve(plan, range(len(SHARES)), t, refs, own_sem, False, True)
        return 0

    lax.fori_loop(0, total + plan.depth, finish, 0)


def semaphores(dims, total):
    streams = arrivals = owns = 0
    for _, _, axis, orders, middle in SHARES:
        for parity, order in enumerate(orders):
            turns = total if len(orders) == 1 else (total + 1 - parity) // 2
            owns += turns
            for line in order:
                lanes = lanes_of(dims[line], False)
                streams, arrivals = streams + 2 * lanes, arrivals + 2 * lanes * turns
        lanes = lanes_of(dims[axis], middle and dims[axis] > 2)
        streams, arrivals = streams + 2 * lanes, arrivals + 2 * lanes * total
    return streams, arrivals, owns


def weight_sums(dims, lefts, rights, extras, cid):
    tiles = 12 * (WIDTH // TILE)
    total = tiles + extras.shape[0]
    rows = lefts.shape[0]
    streams, arrivals, owns = semaphores(dims, total)
    any_space = pl.BlockSpec(memory_space=pl.ANY)
    return pl.pallas_call(
        functools.partial(weights_kernel, dims, tiles, total),
        out_shape=jax.ShapeDtypeStruct((total, TILE, WIDTH), jnp.bfloat16),
        in_specs=[any_space] * 3,
        out_specs=any_space,
        scratch_shapes=[
            pltpu.VMEM((total, TILE, WIDTH), jnp.bfloat16),
            pltpu.VMEM((total, TILE, WIDTH), jnp.bfloat16),
            pltpu.VMEM((total, MIDDLE_ROWS, WIDTH), jnp.bfloat16),
            pltpu.VMEM((rows, TILE), jnp.bfloat16),
            pltpu.VMEM((rows, WIDTH), jnp.bfloat16),
            pltpu.SemaphoreType.DMA((3,)),
            pltpu.SemaphoreType.DMA((streams, RING)),
            pltpu.SemaphoreType.DMA((arrivals,)),
            pltpu.SemaphoreType.DMA((owns,)),
        ],
        compiler_params=pltpu.CompilerParams(collective_id=cid, has_side_effects=True, vmem_limit_bytes=63 * 2**20),
        cost_estimate=pl.CostEstimate(flops=2 * 12 * rows * WIDTH * WIDTH, bytes_accessed=100 * 2**20, transcendentals=0),
    )(lefts, rights, extras)


HEADS = 8
CHUNK = 1024
LOW = jnp.bfloat16
WIDE = jnp.float32
NN = (((1,), (0,)), ((), ()))
NT = (((1,), (1,)), ((), ()))
TN = (((0,), (0,)), ((), ()))


def dot(a, b, form):
    return lax.dot_general(a, b, form, preferred_element_type=WIDE)


def normalize(values):
    center = values - jnp.mean(values, -1, keepdims=True)
    inverse = lax.rsqrt(jnp.mean(center * center, -1, keepdims=True) + 1e-05)
    return center * inverse, inverse


def norm_back(upstream, gain, xhat, inverse):
    scaled = upstream * gain
    return inverse * (scaled - jnp.mean(scaled, -1, keepdims=True)
                      - xhat * jnp.mean(scaled * xhat, -1, keepdims=True))


def gelu_pair(u):
    c = 0.7978845608028654
    square = u * u
    t = jnp.tanh(u * (c + (c * 0.044715) * square))
    half = 0.5 * (1.0 + t)
    slope = half + (0.5 * u) * (1.0 - t * t) * (c + (3.0 * c * 0.044715) * square)
    return u * half, slope


def layers_kernel(groups, tokens, cotangent, mask, embed, params, w_qkv, w_out, w_up, w_down,
                  lefts, rights, sec_out, sec_grad, g_params, g_embed, squares,
                  qkv_w, out_w, up_w, down_w, emb, src, upstream, qkv, probs, slopes, xhat_f, stats,
                  keep, passed, acc, hid, u_buf,
                  w_sem, in_sem, left_sem, right_sem, wide_sem, send_sem, recv_sem):
    section = lax.axis_index("section")
    first = section == 0
    other = 1 - section
    slots, width = emb.shape
    units = up_w.shape[1]
    steps = units // CHUNK
    head = width // HEADS
    scale = head ** -0.5

    loads = [pltpu.make_async_copy(a, b, w_sem.at[k]) for k, (a, b) in enumerate(
        ((w_qkv, qkv_w), (w_out, out_w), (w_up, up_w), (w_down, down_w), (embed, emb)))]
    loads[4].start()
    loads[0].start()

    def token_load(g):
        return pltpu.make_async_copy(tokens.at[g], src.at[g], in_sem.at[g])

    def cot_load(g):
        return pltpu.make_async_copy(cotangent.at[g], upstream.at[g], in_sem.at[groups + g])

    @pl.when(first)
    def _():
        for g in range(groups):
            token_load(g).start()
    for k in (1, 2, 3):
        loads[k].start()

    barrier = pltpu.get_barrier_semaphore()
    pl.semaphore_signal(barrier, inc=1, device_id={"section": other}, device_id_type=MESH)
    pl.semaphore_wait(barrier, 1)

    def relay(g):
        return pltpu.make_async_remote_copy(
            src_ref=passed, dst_ref=src.at[g], send_sem=send_sem.at[g], recv_sem=recv_sem.at[g],
            device_id={"section": other}, device_id_type=MESH)

    def relay_back(g):
        return pltpu.make_async_remote_copy(
            src_ref=passed, dst_ref=upstream.at[g], send_sem=send_sem.at[groups + g],
            recv_sem=recv_sem.at[groups + g], device_id={"section": other}, device_id_type=MESH)

    def rows_of(g):
        return pl.ds(pl.multiple_of(g * slots, slots), slots)

    def cols(i, w=CHUNK):
        return pl.ds(pl.multiple_of(i * w, w), w)

    def left_store(g, k):
        return pltpu.make_async_copy(
            keep.at[:, pl.ds((k - 1) * width, width)], lefts.at[rows_of(g), pl.ds(units + (k - 1) * width, width)], left_sem.at[k])

    def right_store(g, k):
        if k == 0:
            return pltpu.make_async_copy(upstream.at[g], rights.at[rows_of(g), pl.ds(0, width)], right_sem.at[0])
        return pltpu.make_async_copy(
            keep.at[:, pl.ds((k - 2) * width, width)],
            rights.at[rows_of(g), pl.ds(width + units + (k - 2) * width, width)], right_sem.at[k])

    def left_chunk(g, i):
        return pltpu.make_async_copy(
            upstream.at[i], lefts.at[rows_of(g), pl.ds(i * CHUNK, CHUNK)], left_sem.at[5 + i])

    def right_chunk(g, i):
        return pltpu.make_async_copy(
            slopes.at[g, :, pl.ds(i * CHUNK, CHUNK)],
            rights.at[rows_of(g), pl.ds(width + i * CHUNK, CHUNK)], right_sem.at[6 + i])

    def out_store(g):
        return pltpu.make_async_copy(acc, sec_out.at[g], wide_sem.at[0])

    def grad_store(g):
        return pltpu.make_async_copy(acc, sec_grad.at[g], wide_sem.at[1])

    def base_of(g):
        return jnp.where(first, 0.0, src[g].astype(WIDE)) + emb[...].astype(WIDE)

    stage = pl.when(section >= 0)

    def heads_of(g, h):
        return tuple(qkv[g, :, k * width + h * head:k * width + (h + 1) * head] for k in range(3))

    def forward(g):
        @pl.when(first)
        def _():
            token_load(g).wait()
        @pl.when(section == 1)
        def _():
            relay(g).wait_recv()

        @stage
        def _():
            @pl.when(g == 0)
            def _():
                loads[4].wait()

            @pl.when(g > 0)
            def _():
                for k in (3, 4):
                    left_store(g - 1, k).wait()
            source = src[g].astype(WIDE)
            xhat, inverse = normalize(source)
            stats[g, :, 0:1] = inverse
            stats[g, :, 3:4] = jnp.mean(source, -1, keepdims=True)
            keep[:, 3 * width:4 * width] = (xhat * params[2:3] + params[3:4]).astype(LOW)
            @pl.when(g == 0)
            def _():
                loads[0].wait()
            for k, rows in ((1, 3), (2, 3)):
                part = slice(k * width, (k + 1) * width)
                qkv[g, :, part] = dot(keep[:, rows * width:(rows + 1) * width], qkv_w[:, part], NN).astype(LOW)
            base = base_of(g)
            xhat, inverse = normalize(base)
            stats[g, :, 1:2] = inverse
            stats[g, :, 4:5] = jnp.mean(base, -1, keepdims=True)
            keep[:, 2 * width:3 * width] = (xhat * params[0:1] + params[1:2]).astype(LOW)
            qkv[g, :, 0:width] = dot(keep[:, 2 * width:3 * width], qkv_w[:, 0:width], NN).astype(LOW)
            left_store(g, 3).start()
            left_store(g, 4).start()

        @stage
        def _():
            @pl.when(g > 0)
            def _():
                for k in (1, 2):
                    left_store(g - 1, k).wait()
            seen = mask[g, 0:1, :] > 0
            for h in range(HEADS):
                q, k, v = heads_of(g, h)
                s = jnp.where(seen, dot(q, k, NT) * scale, -1e30)
                e = jnp.exp(s - jnp.max(s, -1, keepdims=True))
                p = (e / jnp.sum(e, -1, keepdims=True)).astype(LOW)
                probs[g, h] = p
                keep[:, width + h * head:width + (h + 1) * head] = dot(p, v, NN).astype(LOW)
            left_store(g, 2).start()
            @pl.when(g == 0)
            def _():
                loads[1].wait()

        @stage
        def _():
            hid[...] = dot(keep[:, width:2 * width], out_w[...], NN)
            hidden = base_of(g) + hid[...]
            hid[...] = hidden
            xhat, inverse = normalize(hidden)
            stats[g, :, 2:3] = inverse
            xhat_f[g] = xhat.astype(LOW)
            keep[:, 0:width] = (xhat * params[4:5] + params[5:6]).astype(LOW)
            left_store(g, 1).start()
            @pl.when(g == 0)
            def _():
                loads[2].wait()
                loads[3].wait()

            @pl.when(g > 0)
            def _():
                out_store(g - 1).wait()
                for i in range(steps):
                    left_chunk(g - 1, i).wait()

        @stage
        def _():
            chunks = [slice(i * CHUNK, (i + 1) * CHUNK) for i in range(steps)]
            u_buf[0] = dot(keep[:, 0:width], up_w[:, chunks[0]], NN)
            for i, part in enumerate(chunks):
                if i + 1 < steps:
                    u_buf[(i + 1) % 2] = dot(keep[:, 0:width], up_w[:, chunks[i + 1]], NN)
                value, slope = gelu_pair(u_buf[i % 2])
                slopes[g, :, part] = slope.astype(LOW)
                value = value.astype(LOW)
                upstream[i] = value
                term = dot(value, down_w[part, :], NN)
                if i == 0:
                    acc[...] = hid[...] + term
                else:
                    acc[...] += term
            for i in range(steps):
                left_chunk(g, i).start()
            out_store(g).start()

        @pl.when(first)
        def _():
            @pl.when(g > 0)
            def _():
                relay(g - 1).wait_send()
                @pl.when(g == groups - 1)
                def _():
                    for i in range(steps):
                        left_chunk(g, i).wait()
            passed[...] = acc[...].astype(LOW)
            relay(g).start()

    pl.loop(0, groups)(forward)

    for k in range(1, 5):
        left_store(groups - 1, k).wait()
    out_store(groups - 1).wait()

    @pl.when(first)
    def _():
        relay(groups - 1).wait_send()

    @pl.when(section == 1)
    def _():
        for i in range(steps):
            left_chunk(groups - 1, i).wait()
        for g in range(groups):
            cot_load(g).start()

    g_params[...] = jnp.zeros_like(g_params)
    g_embed[...] = jnp.zeros_like(g_embed)
    squares[...] = jnp.zeros_like(squares)

    def gains(row, e, xhat):
        g_params[row:row + 1] += jnp.sum(e * xhat, axis=0, keepdims=True)
        g_params[row + 1:row + 2] += jnp.sum(e, axis=0, keepdims=True)

    def backward(g):
        @pl.when(first)
        def _():
            relay_back(g).wait_recv()
        @pl.when(section == 1)
        def _():
            cot_load(g).wait()

        @stage
        def _():
            @pl.when(g > 0)
            def _():
                for k in (2, 3, 4, 5):
                    right_store(g - 1, k).wait()
                right_store(g - 1, 0).wait()
                for i in range(steps):
                    right_chunk(g - 1, i).wait()
                grad_store(g - 1).wait()
            right_store(g, 0).start()
            chunks = [slice(i * CHUNK, (i + 1) * CHUNK) for i in range(steps)]
            u_buf[0] = dot(upstream[g], down_w[chunks[0], :], NT)
            for i, part in enumerate(chunks):
                if i + 1 < steps:
                    u_buf[(i + 1) % 2] = dot(upstream[g], down_w[chunks[i + 1], :], NT)
                value = (u_buf[i % 2] * slopes[g, :, part].astype(WIDE)).astype(LOW)
                slopes[g, :, part] = value
                term = dot(value, up_w[:, part], NT)
                if i == 0:
                    acc[...] = term
                else:
                    acc[...] += term

        @stage
        def _():
            for i in range(steps):
                right_chunk(g, i).start()
            e = acc[...]
            xhat = xhat_f[g].astype(WIDE)
            gains(4, e, xhat)
            grad_hidden = upstream[g].astype(WIDE) + norm_back(e, params[4:5], xhat, stats[g, :, 2:3])
            hid[...] = grad_hidden
            keep[:, 0:width] = grad_hidden.astype(LOW)
            xhat_f[g] = dot(keep[:, 0:width], out_w[...], NT).astype(LOW)

        @stage
        def _():
            for h in range(HEADS):
                q, k, v = heads_of(g, h)
                m = xhat_f[g, :, h * head:(h + 1) * head]
                low = probs[g, h]
                p = low.astype(WIDE)
                gp = dot(m, v, NT)
                ds = (p * (gp - jnp.sum(gp * p, -1, keepdims=True))).astype(LOW)
                keep[:, width + h * head:width + (h + 1) * head] = (dot(ds, k, NN) * scale).astype(LOW)
                keep[:, 2 * width + h * head:2 * width + (h + 1) * head] = (dot(ds, q, TN) * scale).astype(LOW)
                keep[:, 3 * width + h * head:3 * width + (h + 1) * head] = dot(low, m, TN).astype(LOW)
            for k in (2, 3, 4, 5):
                right_store(g, k).start()

        @stage
        def _():
            acc[...] = dot(keep[:, width:2 * width], qkv_w[:, 0:width], NT)
            u_buf[0] = dot(keep[:, 2 * width:4 * width], qkv_w[:, width:3 * width], NT)
            e = acc[...]
            xhat = (base_of(g) - stats[g, :, 4:5]) * stats[g, :, 1:2]
            gains(0, e, xhat)
            grad_base = hid[...] + norm_back(e, params[0:1], xhat, stats[g, :, 1:2])
            g_embed[...] += grad_base
            hid[...] = grad_base

        @stage
        def _():
            e = u_buf[0]
            xhat = (src[g].astype(WIDE) - stats[g, :, 3:4]) * stats[g, :, 0:1]
            gains(2, e, xhat)
            acc[...] = norm_back(e, params[2:3], xhat, stats[g, :, 0:1])

        @pl.when(section == 1)
        def _():
            @pl.when(g > 0)
            def _():
                relay_back(g - 1).wait_send()
            low = (acc[...] + hid[...]).astype(LOW)
            passed[...] = low
            relay_back(g).start()
            acc[...] = low.astype(WIDE)
        grad_store(g).start()
        total = acc[...]
        squares[pl.ds(g, 1), :] = jnp.broadcast_to(
            jnp.sum(jnp.sum(total * total, axis=0, keepdims=True), axis=1, keepdims=True), (1, squares.shape[1]))

    pl.loop(0, groups)(backward)

    for k in (0, 2, 3, 4, 5):
        right_store(groups - 1, k).wait()
    for i in range(steps):
        right_chunk(groups - 1, i).wait()
    grad_store(groups - 1).wait()

    @pl.when(section == 1)
    def _():
        relay_back(groups - 1).wait_send()


def layers(tokens, cotangent, mask, embed, params, w_qkv, w_out, w_up, w_down, cid):
    groups, slots, width = tokens.shape
    units = w_up.shape[1]
    rows = groups * slots
    hbm = pl.BlockSpec(memory_space=pl.ANY)
    vmem = pl.BlockSpec(memory_space=pltpu.VMEM)
    shape = jax.ShapeDtypeStruct
    return pl.pallas_call(
        functools.partial(layers_kernel, groups),
        out_shape=(
            shape((rows, units + 4 * width), LOW),
            shape((rows, units + 5 * width), LOW),
            shape((groups, slots, width), WIDE),
            shape((groups, slots, width), WIDE),
            shape((8, width), WIDE),
            shape((slots, width), WIDE),
            shape((groups, 128), WIDE),
        ),
        in_specs=[hbm, hbm, vmem, hbm, vmem, hbm, hbm, hbm, hbm],
        out_specs=(hbm, hbm, hbm, hbm, vmem, vmem, vmem),
        scratch_shapes=[
            pltpu.VMEM(w_qkv.shape, LOW),
            pltpu.VMEM(w_out.shape, LOW),
            pltpu.VMEM(w_up.shape, LOW),
            pltpu.VMEM(w_down.shape, LOW),
            pltpu.VMEM((slots, width), LOW),
            pltpu.VMEM((groups, slots, width), LOW),
            pltpu.VMEM((max(groups, units // CHUNK), slots, width), LOW),
            pltpu.VMEM((groups, slots, 3 * width), LOW),
            pltpu.VMEM((groups, HEADS, slots, slots), LOW),
            pltpu.VMEM((groups, slots, units), LOW),
            pltpu.VMEM((groups, slots, width), LOW),
            pltpu.VMEM((groups, slots, 128), WIDE),
            pltpu.VMEM((slots, 4 * width), LOW),
            pltpu.VMEM((slots, width), LOW),
            pltpu.VMEM((slots, width), WIDE),
            pltpu.VMEM((slots, width), WIDE),
            pltpu.VMEM((2, slots, CHUNK), WIDE),
            pltpu.SemaphoreType.DMA((5,)),
            pltpu.SemaphoreType.DMA((2 * groups,)),
            pltpu.SemaphoreType.DMA((5 + units // CHUNK,)),
            pltpu.SemaphoreType.DMA((6 + units // CHUNK,)),
            pltpu.SemaphoreType.DMA((2,)),
            pltpu.SemaphoreType.DMA((2 * groups,)),
            pltpu.SemaphoreType.DMA((2 * groups,)),
        ],
        compiler_params=pltpu.CompilerParams(
            collective_id=cid, has_side_effects=True, vmem_limit_bytes=63 * 2**20),
        cost_estimate=pl.CostEstimate(flops=54 * 10**9, bytes_accessed=120 * 2**20, transcendentals=10**7),
    )(tokens, cotangent, mask, embed, params, w_qkv, w_out, w_up, w_down)


def widen_kernel(ranges, block, *outs):
    step = pl.program_id(0)
    for (first, last), out in zip(ranges, outs):
        @pl.when((step >= first) & (step < last))
        def _():
            out[...] = block[0].astype(out.dtype)


def widen(sums, places):
    tile, width = sums.shape[1:]
    steps = sum(p[1] for p in places)

    def place(first, count, tall, wide):
        def index(step):
            k = jnp.clip(step - first, 0, count - 1)
            if wide == 1:
                return k, 0
            return lax.rem(k, tall), lax.div(k, tall)
        return pl.BlockSpec((tile, width), index)

    return pl.pallas_call(
        lambda *refs: widen_kernel(tuple((p[0], p[0] + p[1]) for p in places), *refs),
        grid=(steps,),
        out_shape=tuple(jax.ShapeDtypeStruct((p[2] * tile, p[3] * width), jnp.float32) for p in places),
        in_specs=[pl.BlockSpec((1, tile, width), lambda step: (step, 0, 0))],
        out_specs=tuple(place(*p) for p in places),
        compiler_params=pltpu.CompilerParams(vmem_limit_bytes=32 * 2**20),
        cost_estimate=pl.CostEstimate(flops=0, bytes_accessed=6 * steps * tile * width, transcendentals=0),
    )(sums)


def body(tokens, clip_frames, cotangent, embed, norm_params, w_qkv, w_out, w_up, w_down):
    is_first = lax.axis_index("section") == 0
    groups, slots, width = tokens.shape
    units = w_up.shape[-1]
    slot_ids = jnp.arange(slots, dtype=jnp.int32)
    visible = (slot_ids[None, :] < clip_frames[:, None] * (slots // 16)) | jnp.logical_not(is_first)
    mask = jnp.broadcast_to(visible[:, None, :].astype(WIDE), (groups, 8, slots))
    lefts, rights, outcome, grad_inputs, g_params, g_embed, squares = layers(
        tokens, cotangent, mask, embed[0], norm_params[0], w_qkv[0], w_out[0], w_up[0], w_down[0], 2
    )
    magnitude = jnp.sqrt(squares[:, 0] / (slots * width) + 1e-06)
    factors = 1.0 + jnp.arange(width, dtype=WIDE) / width
    row = (jnp.sum(magnitude) * factors)[None]
    extras = jnp.stack(
        [g_embed, jnp.concatenate([g_params[:6], row, jnp.zeros((TILE - 7, width), WIDE)])]
    ).astype(LOW)
    sums = weight_sums(lines_of(lax.axis_size("dp")), lefts, rights, extras, 1)
    overall = jnp.sum(sums[49, 6].astype(WIDE)) / jnp.sum(factors)
    norms = magnitude / (overall / (groups * lax.axis_size("dp")))
    down, up, out, qkv = widen(sums, ((0, 16, 16, 1), (16, 16, 4, 4), (32, 4, 4, 1), (36, 12, 4, 3)))
    return (
        outcome[None],
        grad_inputs[None],
        qkv[None],
        out[None],
        up[None],
        down[None],
        sums[49, :6].astype(WIDE)[None],
        sums[48].astype(WIDE)[None],
        norms[None],
    )


def solution(mesh):
    placed = (
        P("dp", None, None),
        P("dp"),
        P("dp", None, None),
        P("section", None, None),
        P("section", None, None),
        P("section", None, None),
        P("section", None, None),
        P("section", None, None),
        P("section", None, None),
    )
    return jax.shard_map(
        body,
        mesh=mesh,
        in_specs=placed,
        out_specs=(
            P("section", "dp", None, None),
            P("section", "dp", None, None),
            P("section", None, None),
            P("section", None, None),
            P("section", None, None),
            P("section", None, None),
            P("section", None, None),
            P("section", None, None),
            P("section", "dp"),
        ),
        check_vma=False,
    )
```

```python
import functools

import jax
import jax.numpy as jnp
from jax import lax
from jax.experimental import pallas as pl
from jax.experimental.pallas import tpu as pltpu
from jax.sharding import PartitionSpec as P

MESH = pl.DeviceIdType.MESH
TILE = 256
WIDTH = 1024
RING = 8
SHARES = (
    (0, 80, 2, ((1, 0),), False),
    (160, 48, 0, ((2, 1), (1, 2)), False),
    (208, 48, 0, ((1, 2), (2, 1)), True),
    (80, 80, 1, ((2, 0),), False),
)
MIDDLE_ROWS = 48


def lines_of(size):
    short = 1
    while 2 * short**3 < size:
        short += 1
    assert 2 * short**3 == size
    return (2 * short, short, short)


def both(*terms):
    out = None
    for t in terms:
        if t is not None:
            out = t if out is None else out & t
    return out


def lanes_of(n, wide):
    return 1 if n == 2 else 4 if wide else 2


class Flow:
    def __init__(self, row, count, middle, phase, axis, n, c, w, owners, left, free, active, parity, lag, summing):
        self.row, self.count, self.middle, self.phase, self.axis = row, count, middle, phase, axis
        self.n, self.c, self.w, self.owners, self.left, self.free = n, c, w, owners, left, free
        self.active, self.parity, self.lag, self.summing = active, parity, lag, summing


class Own:
    def __init__(self, row, count, left, active, parity, sem, turns):
        self.row, self.count, self.left, self.active = row, count, left, active
        self.parity, self.sem, self.turns = parity, sem, turns


class Plan:
    def __init__(self, dims, total):
        self.d = lax.axis_index("dp")
        self.dims = dims
        self.total = total
        self.strides = (dims[1] * dims[2], dims[2], 1)
        self.coords = tuple(lax.rem(lax.div(self.d, s), n) for s, n in zip(self.strides, dims))
        self.depth = self.streams = self.arrivals = self.owns = 0
        self.shares = [self.lay_out(*share) for share in SHARES]

    def flow(self, **fields):
        f = Flow(**fields)
        f.turns = self.total if f.parity is None else (self.total + 1 - f.parity) // 2
        f.wide = f.middle and f.phase == 0 and f.n > 2
        f.lanes = lanes_of(f.n, f.wide)
        f.stream, f.arrival = self.streams, self.arrivals
        self.streams += f.lanes
        self.arrivals += f.lanes * f.turns
        return f

    def lay_out(self, row, count, axis, orders, middle):
        share = dict(row=row, count=count, middle=middle)

        def phase(p, axis, lag, left, free, active, parity):
            n, c = self.dims[axis], self.coords[axis]
            w = WIDTH >> (p + 1)
            inner = middle and p == 0 and n > 2
            owners = (n // 2 - 1, n // 2) if inner else (0, n - 1)
            top = c == owners[1]
            half = jnp.where(top, w, 0)
            used = 0 if middle and p == 0 else w - half
            now = both(active, (c == owners[0]) | top) if n > 2 else active
            fields = dict(share, phase=p, axis=axis, n=n, c=c, w=w, owners=owners, left=left, free=free,
                          active=active, parity=parity)
            hops = (n // 2 if inner else n - 1, max(owners[1], n - 1 - owners[0]))
            return fields, hops, left + half, free + used, now

        free = 512 if middle else 0
        first, hops, left, free, gate = phase(0, axis, 0, 0, free, None, None)
        start = hops[0]
        inner = []
        for parity, order in enumerate(orders):
            key = None if len(orders) == 1 else parity
            lag = start
            second, hops2, left2, free2, gate2 = phase(1, order[0], lag, left, free, gate, key)
            third, hops3, left3, _, gate3 = phase(2, order[1], lag, left2, free2, gate2, key)
            own = Own(row=row, count=count, left=left3, active=gate3, parity=key, sem=self.owns,
                       turns=self.total if key is None else (self.total + 1 - key) // 2)
            self.owns += own.turns
            flows = [self.flow(**second, lag=lag, summing=True)]
            lag += hops2[0]
            flows.append(self.flow(**third, lag=lag, summing=True))
            lag += hops3[0]
            own.start = lag
            flows.append(self.flow(**third, lag=lag, summing=False))
            lag += hops3[1]
            own.end = lag
            flows.append(self.flow(**second, lag=lag, summing=False))
            lag += hops2[1]
            inner.append((key, flows, own))
        before = self.flow(**first, lag=0, summing=True)
        after = self.flow(**first, lag=lag, summing=False)
        self.depth = max(self.depth, lag + hops[1])
        return before, gate, inner, after


def due(plan, job, steady, parity, *terms):
    return both(None if steady else (job >= 0) & (job < plan.total),
                None if parity is None else lax.rem(job, 2) == parity, *terms)


def when(ok):
    return (lambda f: f()) if ok is None else pl.when(ok)


def move(plan, flow, refs, job, cols, spot, step, lane, short=False):
    held, landing, side, result, send_sem, recv_sem = refs
    turn = job if flow.parity is None else lax.div(job, 2)
    rows = pl.ds(flow.row, flow.count)
    at = lambda first: pl.ds(first if isinstance(first, int) else pl.multiple_of(first, 128), flow.w)
    if not flow.summing:
        src = dst = result.at[job, rows, at(cols)]
    else:
        src = held.at[job, rows, at(cols)]
        if short or (flow.middle and flow.phase > 0):
            dst = side.at[job, pl.ds(0, flow.count), at(spot)]
        else:
            dst = landing.at[job, rows, at(spot)]

    def make(source):
        return pltpu.make_async_remote_copy(
            src_ref=source, dst_ref=dst, send_sem=send_sem.at[flow.stream + lane, lax.rem(turn, RING)],
            recv_sem=recv_sem.at[flow.arrival + lane * flow.turns + turn],
            device_id={"dp": plan.d + step}, device_id_type=MESH)

    def send(first_owner=False):
        copy = make(held.at[job, rows, at(cols)] if first_owner else src)
        @pl.when(turn >= RING)
        def _():
            copy.wait_send()
        copy.start()

    def receive():
        make(src).wait_recv()
        if flow.summing:
            place = (job, rows, at(cols))
            held[place] = held[place] + dst[...]

    def finish():
        @pl.when(turn >= flow.turns - RING)
        def _():
            make(src).wait_send()

    return send, receive, finish


def run_flow(plan, flow, tick, refs, steady, ending=False):
    n, c, w, left = flow.n, flow.c, flow.w, flow.left
    stride = plan.strides[flow.axis]
    from_held = not flow.summing and flow.phase == 2
    if n == 2:
        own, other = jnp.where(c == 1, w, 0), jnp.where(c == 1, 0, w)
        out, back = (other, own) if flow.summing else (own, other)
        step = jnp.where(c == 1, -stride, stride)
        job = tick - flow.lag
        send, _, finish = move(plan, flow, refs, job, left + out, flow.free + out, step, 0)
        @when(due(plan, job, steady, flow.parity))
        def _():
            finish() if ending else send(from_held)
        if not ending:
            job = job - 1
            _, receive, _ = move(plan, flow, refs, job, left + back, flow.free + back, step, 0)
            @when(due(plan, job, steady, flow.parity))
            def _():
                receive()
        return
    for up in (True, False):
        owner = flow.owners[int(up)]
        for below in (True, False):
            if (owner if below else n - 1 - owner) == 0:
                continue
            place = c <= owner if below else c >= owner
            if flow.summing:
                hops = c if below else n - 1 - c
                sends = c < owner if below else c > owner
                step = stride if below else -stride
            else:
                hops = owner - c if below else c - owner
                sends = c > 0 if below else c < n - 1
                step = -stride if below else stride
            job = tick - flow.lag - hops
            lower = w if up else 0
            short = flow.summing and flow.middle and flow.phase == 0 and up != below
            if short:
                spot = 0
            elif flow.middle and flow.phase == 0:
                spot = lower
            else:
                spot = flow.free + lower
            send, receive, finish = move(
                plan, flow, refs, job, left + lower, spot, step, 2 * int(up) + int(below) if flow.wide else int(up), short)
            @when(due(plan, job, steady, flow.parity, place, flow.active if flow.phase == 2 else None))
            def _():
                if ending:
                    pl.when(sends)(finish)
                    return
                pl.when(hops > 0)(receive)
                if from_held:
                    pl.when(sends & (hops == 0))(functools.partial(send, True))
                    pl.when(sends & (hops > 0))(send)
                else:
                    pl.when(sends)(send)


def own_copy(plan, own, refs, job, own_sem):
    turn = job if own.parity is None else lax.div(job, 2)
    part = (job, pl.ds(own.row, own.count), pl.ds(pl.multiple_of(own.left, 128), WIDTH >> 3))
    return pltpu.make_async_copy(refs[0].at[part], refs[3].at[part], own_sem.at[own.sem + turn])


def serve(plan, shares, tick, refs, own_sem, steady, ending=False):
    for k in shares:
        before, gate, inner, after = plan.shares[k]
        run_flow(plan, before, tick, refs, steady, ending)

        @when(gate)
        def _():
            for parity, flows, own in inner:
                for flow in flows:
                    if not flow.summing and not ending:
                        opens = flow.phase == 2
                        job = tick - (own.start if opens else own.end)
                        @when(due(plan, job, steady, parity, own.active))
                        def _():
                            copy = own_copy(plan, own, refs, job, own_sem)
                            copy.start() if opens else copy.wait()
                    run_flow(plan, flow, tick, refs, steady, ending)
        run_flow(plan, after, tick, refs, steady, ending)


def greet(plan):
    barrier = pltpu.get_barrier_semaphore()
    count = 0
    for n, c, s in zip(plan.dims, plan.coords, plan.strides):
        for inside, step in ((c > 0, -s), (c < n - 1, s)):
            @pl.when(inside)
            def _():
                pl.semaphore_signal(barrier, inc=1, device_id={"dp": plan.d + step}, device_id_type=MESH)
            count = count + inside.astype(jnp.int32)
    pl.semaphore_wait(barrier, count)


def weights_kernel(dims, tiles, total, left_ref, right_ref, extra_ref, result, held, landing, side,
                   left_buf, right_buf, load_sem, send_sem, recv_sem, own_sem):
    plan = Plan(dims, total)
    per = WIDTH // TILE
    greet(plan)

    def left_copy(s):
        job, part = lax.div(s, per), lax.rem(s, per)
        slab = jnp.where(job < 4, job, jnp.where(job < 8, 4, jnp.minimum(job - 3, 7)))
        return pltpu.make_async_copy(
            left_ref.at[:, pl.ds(pl.multiple_of(slab * WIDTH + part * TILE, TILE), TILE)],
            left_buf, load_sem.at[0])

    def right_copy(job):
        slab = jnp.where(job < 4, 0, job - 3)
        return pltpu.make_async_copy(
            right_ref.at[:, pl.ds(pl.multiple_of(slab * WIDTH, WIDTH), WIDTH)],
            right_buf, load_sem.at[1])

    def product(s):
        left_copy(s).wait()
        @pl.when(lax.rem(s, per) == 0)
        def _():
            right_copy(lax.div(s, per)).wait()
        held[s] = lax.dot_general(
            left_buf[...], right_buf[...], (((0,), (0,)), ((), ())),
            preferred_element_type=jnp.float32).astype(jnp.bfloat16)
        @pl.when(s + 1 < tiles)
        def _():
            left_copy(s + 1).start()
            @pl.when(lax.rem(s + 1, per) == 0)
            def _():
                right_copy(lax.div(s + 1, per)).start()

    extras = pltpu.make_async_copy(extra_ref, held.at[pl.ds(tiles, total - tiles)], load_sem.at[2])
    left_copy(0).start()
    right_copy(0).start()
    extras.start()
    product(0)
    extras.wait()
    refs = (held, landing, side, result, send_sem, recv_sem)

    def tick(steady, t, _):
        serve(plan, (0, 1), t, refs, own_sem, steady)
        @pl.when(t + 1 < tiles)
        def _():
            product(t + 1)
        serve(plan, (2, 3), t, refs, own_sem, steady)
        return 0

    lax.fori_loop(0, plan.depth, functools.partial(tick, False), 0)
    lax.fori_loop(plan.depth, total, functools.partial(tick, True), 0)
    lax.fori_loop(total, total + plan.depth, functools.partial(tick, False), 0)

    def finish(t, _):
        serve(plan, range(len(SHARES)), t, refs, own_sem, False, True)
        return 0

    lax.fori_loop(0, total + plan.depth, finish, 0)


def semaphores(dims, total):
    streams = arrivals = owns = 0
    for _, _, axis, orders, middle in SHARES:
        for parity, order in enumerate(orders):
            turns = total if len(orders) == 1 else (total + 1 - parity) // 2
            owns += turns
            for line in order:
                lanes = lanes_of(dims[line], False)
                streams, arrivals = streams + 2 * lanes, arrivals + 2 * lanes * turns
        lanes = lanes_of(dims[axis], middle and dims[axis] > 2)
        streams, arrivals = streams + 2 * lanes, arrivals + 2 * lanes * total
    return streams, arrivals, owns


def weight_sums(dims, lefts, rights, extras, cid):
    tiles = 12 * (WIDTH // TILE)
    total = tiles + extras.shape[0]
    rows = lefts.shape[0]
    streams, arrivals, owns = semaphores(dims, total)
    any_space = pl.BlockSpec(memory_space=pl.ANY)
    return pl.pallas_call(
        functools.partial(weights_kernel, dims, tiles, total),
        out_shape=jax.ShapeDtypeStruct((total, TILE, WIDTH), jnp.bfloat16),
        in_specs=[any_space] * 3,
        out_specs=any_space,
        scratch_shapes=[
            pltpu.VMEM((total, TILE, WIDTH), jnp.bfloat16),
            pltpu.VMEM((total, TILE, WIDTH), jnp.bfloat16),
            pltpu.VMEM((total, MIDDLE_ROWS, WIDTH), jnp.bfloat16),
            pltpu.VMEM((rows, TILE), jnp.bfloat16),
            pltpu.VMEM((rows, WIDTH), jnp.bfloat16),
            pltpu.SemaphoreType.DMA((3,)),
            pltpu.SemaphoreType.DMA((streams, RING)),
            pltpu.SemaphoreType.DMA((arrivals,)),
            pltpu.SemaphoreType.DMA((owns,)),
        ],
        compiler_params=pltpu.CompilerParams(collective_id=cid, has_side_effects=True, vmem_limit_bytes=63 * 2**20),
        cost_estimate=pl.CostEstimate(flops=2 * 12 * rows * WIDTH * WIDTH, bytes_accessed=100 * 2**20, transcendentals=0),
    )(lefts, rights, extras)


HEADS = 8
CHUNK = 1024
LOW = jnp.bfloat16
WIDE = jnp.float32
NN = (((1,), (0,)), ((), ()))
NT = (((1,), (1,)), ((), ()))
TN = (((0,), (0,)), ((), ()))


def dot(a, b, form):
    return lax.dot_general(a, b, form, preferred_element_type=WIDE)


def normalize(values):
    center = values - jnp.mean(values, -1, keepdims=True)
    inverse = lax.rsqrt(jnp.mean(center * center, -1, keepdims=True) + 1e-05)
    return center * inverse, inverse


def norm_back(upstream, gain, xhat, inverse):
    scaled = upstream * gain
    return inverse * (scaled - jnp.mean(scaled, -1, keepdims=True)
                      - xhat * jnp.mean(scaled * xhat, -1, keepdims=True))


def gelu_pair(u):
    c = 0.7978845608028654
    square = u * u
    t = jnp.tanh(u * (c + (c * 0.044715) * square))
    half = 0.5 * (1.0 + t)
    slope = half + (0.5 * u) * (1.0 - t * t) * (c + (3.0 * c * 0.044715) * square)
    return u * half, slope


def layers_kernel(groups, tokens, clip_frames, cotangent, embed, norm_params, w_qkv, w_out, w_up, w_down,
                  lefts, rights, sec_out, sec_grad, extras, sizes, params, g_params, g_embed,
                  qkv_w, out_w, up_w, down_w, emb, src, upstream, qkv, probs, slopes, xhat_f, stats,
                  keep, passed, acc, hid, u_buf,
                  w_sem, in_sem, left_sem, right_sem, wide_sem, send_sem, recv_sem):
    section = lax.axis_index("section")
    first = section == 0
    other = 1 - section
    slots, width = emb.shape
    units = up_w.shape[1]
    steps = units // CHUNK
    head = width // HEADS
    scale = head ** -0.5

    loads = [pltpu.make_async_copy(a, b, w_sem.at[k]) for k, (a, b) in enumerate(
        ((w_qkv, qkv_w), (w_out, out_w), (w_up, up_w), (w_down, down_w), (embed, emb), (norm_params, params)))]
    loads[4].start()
    loads[5].start()
    loads[0].start()

    def token_load(g):
        return pltpu.make_async_copy(tokens.at[g], src.at[g], in_sem.at[g])

    def cot_load(g):
        return pltpu.make_async_copy(cotangent.at[g], upstream.at[g], in_sem.at[groups + g])

    @pl.when(first)
    def _():
        for g in range(groups):
            token_load(g).start()
    for k in (1, 2, 3):
        loads[k].start()

    barrier = pltpu.get_barrier_semaphore()
    pl.semaphore_signal(barrier, inc=1, device_id={"section": other}, device_id_type=MESH)
    pl.semaphore_wait(barrier, 1)

    def relay(g):
        return pltpu.make_async_remote_copy(
            src_ref=passed, dst_ref=src.at[g], send_sem=send_sem.at[g], recv_sem=recv_sem.at[g],
            device_id={"section": other}, device_id_type=MESH)

    def relay_back(g):
        return pltpu.make_async_remote_copy(
            src_ref=passed, dst_ref=upstream.at[g], send_sem=send_sem.at[groups + g],
            recv_sem=recv_sem.at[groups + g], device_id={"section": other}, device_id_type=MESH)

    def rows_of(g):
        return pl.ds(pl.multiple_of(g * slots, slots), slots)

    def cols(i, w=CHUNK):
        return pl.ds(pl.multiple_of(i * w, w), w)

    def left_store(g, k):
        return pltpu.make_async_copy(
            keep.at[:, pl.ds((k - 1) * width, width)], lefts.at[rows_of(g), pl.ds(units + (k - 1) * width, width)], left_sem.at[k])

    def right_store(g, k):
        if k == 0:
            return pltpu.make_async_copy(upstream.at[g], rights.at[rows_of(g), pl.ds(0, width)], right_sem.at[0])
        return pltpu.make_async_copy(
            keep.at[:, pl.ds((k - 2) * width, width)],
            rights.at[rows_of(g), pl.ds(width + units + (k - 2) * width, width)], right_sem.at[k])

    def left_chunk(g, i):
        return pltpu.make_async_copy(
            upstream.at[i], lefts.at[rows_of(g), pl.ds(i * CHUNK, CHUNK)], left_sem.at[5 + i])

    def right_chunk(g, i):
        return pltpu.make_async_copy(
            slopes.at[g, :, pl.ds(i * CHUNK, CHUNK)],
            rights.at[rows_of(g), pl.ds(width + i * CHUNK, CHUNK)], right_sem.at[6 + i])

    def out_store(g):
        return pltpu.make_async_copy(acc, sec_out.at[g], wide_sem.at[0])

    def grad_store(g):
        return pltpu.make_async_copy(acc, sec_grad.at[g], wide_sem.at[1])

    def base_of(g):
        return jnp.where(first, 0.0, src[g].astype(WIDE)) + emb[...].astype(WIDE)

    stage = pl.when(section >= 0)

    def heads_of(g, h):
        return tuple(qkv[g, :, k * width + h * head:k * width + (h + 1) * head] for k in range(3))

    def forward(g):
        @pl.when(first)
        def _():
            token_load(g).wait()
        @pl.when(section == 1)
        def _():
            relay(g).wait_recv()

        @stage
        def _():
            @pl.when(g == 0)
            def _():
                loads[4].wait()
                loads[5].wait()

            @pl.when(g > 0)
            def _():
                for k in (3, 4):
                    left_store(g - 1, k).wait()
            source = src[g].astype(WIDE)
            xhat, inverse = normalize(source)
            stats[g, :, 0:1] = inverse
            stats[g, :, 3:4] = jnp.mean(source, -1, keepdims=True)
            keep[:, 3 * width:4 * width] = (xhat * params[2:3] + params[3:4]).astype(LOW)
            @pl.when(g == 0)
            def _():
                loads[0].wait()
            for k, rows in ((1, 3), (2, 3)):
                part = slice(k * width, (k + 1) * width)
                qkv[g, :, part] = dot(keep[:, rows * width:(rows + 1) * width], qkv_w[:, part], NN).astype(LOW)
            base = base_of(g)
            xhat, inverse = normalize(base)
            stats[g, :, 1:2] = inverse
            stats[g, :, 4:5] = jnp.mean(base, -1, keepdims=True)
            keep[:, 2 * width:3 * width] = (xhat * params[0:1] + params[1:2]).astype(LOW)
            qkv[g, :, 0:width] = dot(keep[:, 2 * width:3 * width], qkv_w[:, 0:width], NN).astype(LOW)
            left_store(g, 3).start()
            left_store(g, 4).start()

        @stage
        def _():
            @pl.when(g > 0)
            def _():
                for k in (1, 2):
                    left_store(g - 1, k).wait()
            limit = jnp.where(first, clip_frames[g] * (slots // 16), slots)
            seen = lax.broadcasted_iota(jnp.int32, (1, slots), 1) < limit
            for h in range(HEADS):
                q, k, v = heads_of(g, h)
                s = jnp.where(seen, dot(q, k, NT) * scale, -1e30)
                e = jnp.exp(s - jnp.max(s, -1, keepdims=True))
                p = (e / jnp.sum(e, -1, keepdims=True)).astype(LOW)
                probs[g, h] = p
                keep[:, width + h * head:width + (h + 1) * head] = dot(p, v, NN).astype(LOW)
            left_store(g, 2).start()
            @pl.when(g == 0)
            def _():
                loads[1].wait()

        @stage
        def _():
            hid[...] = dot(keep[:, width:2 * width], out_w[...], NN)
            hidden = base_of(g) + hid[...]
            hid[...] = hidden
            xhat, inverse = normalize(hidden)
            stats[g, :, 2:3] = inverse
            xhat_f[g] = xhat.astype(LOW)
            keep[:, 0:width] = (xhat * params[4:5] + params[5:6]).astype(LOW)
            left_store(g, 1).start()
            @pl.when(g == 0)
            def _():
                loads[2].wait()
                loads[3].wait()

            @pl.when(g > 0)
            def _():
                out_store(g - 1).wait()
                for i in range(steps):
                    left_chunk(g - 1, i).wait()

        @stage
        def _():
            chunks = [slice(i * CHUNK, (i + 1) * CHUNK) for i in range(steps)]
            u_buf[0] = dot(keep[:, 0:width], up_w[:, chunks[0]], NN)
            for i, part in enumerate(chunks):
                if i + 1 < steps:
                    u_buf[(i + 1) % 2] = dot(keep[:, 0:width], up_w[:, chunks[i + 1]], NN)
                value, slope = gelu_pair(u_buf[i % 2])
                slopes[g, :, part] = slope.astype(LOW)
                value = value.astype(LOW)
                upstream[i] = value
                term = dot(value, down_w[part, :], NN)
                if i == 0:
                    acc[...] = hid[...] + term
                else:
                    acc[...] += term
            for i in range(steps):
                left_chunk(g, i).start()
            out_store(g).start()

        @pl.when(first)
        def _():
            @pl.when(g > 0)
            def _():
                relay(g - 1).wait_send()
                @pl.when(g == groups - 1)
                def _():
                    for i in range(steps):
                        left_chunk(g, i).wait()
            passed[...] = acc[...].astype(LOW)
            relay(g).start()

    pl.loop(0, groups)(forward)

    for k in range(1, 5):
        left_store(groups - 1, k).wait()
    out_store(groups - 1).wait()

    @pl.when(first)
    def _():
        relay(groups - 1).wait_send()

    @pl.when(section == 1)
    def _():
        for i in range(steps):
            left_chunk(groups - 1, i).wait()
        for g in range(groups):
            cot_load(g).start()

    g_params[...] = jnp.zeros_like(g_params)
    g_embed[...] = jnp.zeros_like(g_embed)

    def gains(row, e, xhat):
        g_params[row:row + 1] += jnp.sum(e * xhat, axis=0, keepdims=True)
        g_params[row + 1:row + 2] += jnp.sum(e, axis=0, keepdims=True)

    def backward(g):
        @pl.when(first)
        def _():
            relay_back(g).wait_recv()
        @pl.when(section == 1)
        def _():
            cot_load(g).wait()

        @stage
        def _():
            @pl.when(g > 0)
            def _():
                for k in (2, 3, 4, 5):
                    right_store(g - 1, k).wait()
                right_store(g - 1, 0).wait()
                for i in range(steps):
                    right_chunk(g - 1, i).wait()
                grad_store(g - 1).wait()
            right_store(g, 0).start()
            chunks = [slice(i * CHUNK, (i + 1) * CHUNK) for i in range(steps)]
            u_buf[0] = dot(upstream[g], down_w[chunks[0], :], NT)
            for i, part in enumerate(chunks):
                if i + 1 < steps:
                    u_buf[(i + 1) % 2] = dot(upstream[g], down_w[chunks[i + 1], :], NT)
                value = (u_buf[i % 2] * slopes[g, :, part].astype(WIDE)).astype(LOW)
                slopes[g, :, part] = value
                term = dot(value, up_w[:, part], NT)
                if i == 0:
                    acc[...] = term
                else:
                    acc[...] += term

        @stage
        def _():
            for i in range(steps):
                right_chunk(g, i).start()
            e = acc[...]
            xhat = xhat_f[g].astype(WIDE)
            gains(4, e, xhat)
            grad_hidden = upstream[g].astype(WIDE) + norm_back(e, params[4:5], xhat, stats[g, :, 2:3])
            hid[...] = grad_hidden
            keep[:, 0:width] = grad_hidden.astype(LOW)
            xhat_f[g] = dot(keep[:, 0:width], out_w[...], NT).astype(LOW)

        @stage
        def _():
            for h in range(HEADS):
                q, k, v = heads_of(g, h)
                m = xhat_f[g, :, h * head:(h + 1) * head]
                low = probs[g, h]
                p = low.astype(WIDE)
                gp = dot(m, v, NT)
                ds = (p * (gp - jnp.sum(gp * p, -1, keepdims=True))).astype(LOW)
                keep[:, width + h * head:width + (h + 1) * head] = (dot(ds, k, NN) * scale).astype(LOW)
                keep[:, 2 * width + h * head:2 * width + (h + 1) * head] = (dot(ds, q, TN) * scale).astype(LOW)
                keep[:, 3 * width + h * head:3 * width + (h + 1) * head] = dot(low, m, TN).astype(LOW)
            for k in (2, 3, 4, 5):
                right_store(g, k).start()

        @stage
        def _():
            acc[...] = dot(keep[:, width:2 * width], qkv_w[:, 0:width], NT)
            u_buf[0] = dot(keep[:, 2 * width:4 * width], qkv_w[:, width:3 * width], NT)
            e = acc[...]
            xhat = (base_of(g) - stats[g, :, 4:5]) * stats[g, :, 1:2]
            gains(0, e, xhat)
            grad_base = hid[...] + norm_back(e, params[0:1], xhat, stats[g, :, 1:2])
            g_embed[...] += grad_base
            hid[...] = grad_base

        @stage
        def _():
            e = u_buf[0]
            xhat = (src[g].astype(WIDE) - stats[g, :, 3:4]) * stats[g, :, 0:1]
            gains(2, e, xhat)
            acc[...] = norm_back(e, params[2:3], xhat, stats[g, :, 0:1])

        @pl.when(section == 1)
        def _():
            @pl.when(g > 0)
            def _():
                relay_back(g - 1).wait_send()
            low = (acc[...] + hid[...]).astype(LOW)
            passed[...] = low
            relay_back(g).start()
            acc[...] = low.astype(WIDE)
        grad_store(g).start()
        total = acc[...]
        total = jnp.sum(jnp.sum(total * total, axis=0, keepdims=True), axis=1, keepdims=True)
        sizes[pl.ds(g, 1), :] = jnp.broadcast_to(
            jnp.sqrt(total / (slots * width) + 1e-06), (1, sizes.shape[1]))

    pl.loop(0, groups)(backward)

    for k in (0, 2, 3, 4, 5):
        right_store(groups - 1, k).wait()
    for i in range(steps):
        right_chunk(groups - 1, i).wait()
    grad_store(groups - 1).wait()

    g_params[6:7] = jnp.sum(sizes[:, 0:1], axis=0, keepdims=True) * spread_of(width)
    keep[:, 0:width] = g_embed[...].astype(LOW)
    keep[:, width:2 * width] = jnp.zeros((slots, width), LOW)
    keep[0:16, width:2 * width] = jnp.concatenate([g_params[...], jnp.zeros_like(g_params)]).astype(LOW)
    for k in range(2):
        pltpu.make_async_copy(keep.at[:, pl.ds(k * width, width)], extras.at[k], right_sem.at[k]).start()
    for k in range(2):
        pltpu.make_async_copy(keep.at[:, pl.ds(k * width, width)], extras.at[k], right_sem.at[k]).wait()

    @pl.when(section == 1)
    def _():
        relay_back(groups - 1).wait_send()


def spread_of(width):
    return 1.0 + lax.broadcasted_iota(jnp.int32, (1, width), 1).astype(WIDE) / width


def layers(tokens, clip_frames, cotangent, embed, norm_params, w_qkv, w_out, w_up, w_down, cid):
    groups, slots, width = tokens.shape
    units = w_up.shape[1]
    rows = groups * slots
    hbm = pl.BlockSpec(memory_space=pl.ANY)
    vmem = pl.BlockSpec(memory_space=pltpu.VMEM)
    shape = jax.ShapeDtypeStruct
    return pl.pallas_call(
        functools.partial(layers_kernel, groups),
        out_shape=(
            shape((rows, units + 4 * width), LOW),
            shape((rows, units + 5 * width), LOW),
            shape((groups, slots, width), WIDE),
            shape((groups, slots, width), WIDE),
            shape((2, slots, width), LOW),
            shape((groups, 128), WIDE),
        ),
        in_specs=[hbm, pl.BlockSpec(memory_space=pltpu.SMEM)] + [hbm] * 7,
        out_specs=(hbm, hbm, hbm, hbm, hbm, vmem),
        scratch_shapes=[
            pltpu.VMEM(norm_params.shape, WIDE),
            pltpu.VMEM((8, width), WIDE),
            pltpu.VMEM((slots, width), WIDE),
            pltpu.VMEM(w_qkv.shape, LOW),
            pltpu.VMEM(w_out.shape, LOW),
            pltpu.VMEM(w_up.shape, LOW),
            pltpu.VMEM(w_down.shape, LOW),
            pltpu.VMEM((slots, width), LOW),
            pltpu.VMEM((groups, slots, width), LOW),
            pltpu.VMEM((max(groups, units // CHUNK), slots, width), LOW),
            pltpu.VMEM((groups, slots, 3 * width), LOW),
            pltpu.VMEM((groups, HEADS, slots, slots), LOW),
            pltpu.VMEM((groups, slots, units), LOW),
            pltpu.VMEM((groups, slots, width), LOW),
            pltpu.VMEM((groups, slots, 128), WIDE),
            pltpu.VMEM((slots, 4 * width), LOW),
            pltpu.VMEM((slots, width), LOW),
            pltpu.VMEM((slots, width), WIDE),
            pltpu.VMEM((slots, width), WIDE),
            pltpu.VMEM((2, slots, CHUNK), WIDE),
            pltpu.SemaphoreType.DMA((6,)),
            pltpu.SemaphoreType.DMA((2 * groups,)),
            pltpu.SemaphoreType.DMA((5 + units // CHUNK,)),
            pltpu.SemaphoreType.DMA((6 + units // CHUNK,)),
            pltpu.SemaphoreType.DMA((2,)),
            pltpu.SemaphoreType.DMA((2 * groups,)),
            pltpu.SemaphoreType.DMA((2 * groups,)),
        ],
        compiler_params=pltpu.CompilerParams(
            collective_id=cid, has_side_effects=True, vmem_limit_bytes=63 * 2**20),
        cost_estimate=pl.CostEstimate(flops=54 * 10**9, bytes_accessed=120 * 2**20, transcendentals=10**7),
    )(tokens, clip_frames, cotangent, embed, norm_params, w_qkv, w_out, w_up, w_down)


def widen_kernel(ranges, count, block, sizes, *outs):
    step = pl.program_id(0)
    for (first, last), out in zip(ranges, outs):
        @pl.when((step >= first) & (step < last))
        def _():
            out[...] = block[...].reshape(out.shape).astype(out.dtype)

    @pl.when(step == ranges[-1][1])
    def _():
        embed, params, norms = outs[len(ranges):]
        embed[...] = block[0].astype(WIDE)
        params[...] = block[1, 0:8].astype(WIDE)[0:6]
        row = block[1, 0:8].astype(WIDE)[6:7]
        factors = spread_of(row.shape[1])
        mean = jnp.sum(row, axis=1, keepdims=True) / jnp.sum(factors, axis=1, keepdims=True) / count
        here = jnp.zeros(norms.shape, WIDE)
        for g in range(norms.shape[1]):
            lane = lax.broadcasted_iota(jnp.int32, norms.shape, 1) == g
            here = jnp.where(lane, sizes[g:g + 1, 0:1] / mean, here)
        norms[...] = here


def widen(sums, sizes, count, places):
    tile, width = sums.shape[1:]
    steps = sum(p[1] for p in places)

    def place(first, count, tall, wide):
        def index(step):
            k = jnp.clip(step - first, 0, count - 1)
            if wide == 1:
                return k, 0
            return lax.rem(k, tall), lax.div(k, tall)
        return pl.BlockSpec((2 * tile, width), index)

    shape = jax.ShapeDtypeStruct
    whole = lambda *dims: pl.BlockSpec(dims, lambda step: (0,) * len(dims))
    groups = sizes.shape[0]
    return pl.pallas_call(
        lambda *refs: widen_kernel(tuple((p[0], p[0] + p[1]) for p in places), count, *refs),
        grid=(steps + 1,),
        out_shape=tuple(shape((p[2] * 2 * tile, p[3] * width), WIDE) for p in places)
        + (shape((tile, width), WIDE), shape((6, width), WIDE), shape((1, groups), WIDE)),
        in_specs=[pl.BlockSpec((2, tile, width), lambda step: (step, 0, 0)), whole(*sizes.shape)],
        out_specs=tuple(place(*p) for p in places) + (whole(tile, width), whole(6, width), whole(1, groups)),
        compiler_params=pltpu.CompilerParams(vmem_limit_bytes=48 * 2**20),
        cost_estimate=pl.CostEstimate(flops=0, bytes_accessed=12 * steps * tile * width, transcendentals=0),
    )(sums, sizes)


def body(tokens, clip_frames, cotangent, embed, norm_params, w_qkv, w_out, w_up, w_down):
    groups = tokens.shape[0]
    devices = lax.axis_size("dp")
    lefts, rights, outcome, grad_inputs, extras, sizes = layers(
        tokens, clip_frames, cotangent, embed[0], norm_params[0], w_qkv[0], w_out[0], w_up[0], w_down[0], 2
    )
    sums = weight_sums(lines_of(devices), lefts, rights, extras, 1)
    down, up, out, qkv, g_embed, g_params, norms = widen(
        sums, sizes, groups * devices, ((0, 8, 8, 1), (8, 8, 2, 4), (16, 2, 2, 1), (18, 6, 2, 3))
    )
    return (
        outcome[None],
        grad_inputs[None],
        qkv[None],
        out[None],
        up[None],
        down[None],
        g_params[None],
        g_embed[None],
        norms,
    )


def solution(mesh):
    placed = (
        P("dp", None, None),
        P("dp"),
        P("dp", None, None),
        P("section", None, None),
        P("section", None, None),
        P("section", None, None),
        P("section", None, None),
        P("section", None, None),
        P("section", None, None),
    )
    return jax.shard_map(
        body,
        mesh=mesh,
        in_specs=placed,
        out_specs=(
            P("section", "dp", None, None),
            P("section", "dp", None, None),
            P("section", None, None),
            P("section", None, None),
            P("section", None, None),
            P("section", None, None),
            P("section", None, None),
            P("section", None, None),
            P("section", "dp"),
        ),
        check_vma=False,
    )
```

```python
import functools

import jax
import jax.numpy as jnp
from jax import lax
from jax.experimental import pallas as pl
from jax.experimental.pallas import tpu as pltpu
from jax.sharding import PartitionSpec as P

MESH = pl.DeviceIdType.MESH
TILE = 256
WIDTH = 1024
RING = 8
SHARES = (
    (0, 80, 2, ((1, 0),), False),
    (160, 48, 0, ((2, 1), (1, 2)), False),
    (208, 48, 0, ((1, 2), (2, 1)), True),
    (80, 80, 1, ((2, 0),), False),
)
MIDDLE_ROWS = 48


def lines_of(size):
    short = 1
    while 2 * short**3 < size:
        short += 1
    assert 2 * short**3 == size
    return (2 * short, short, short)


def both(*terms):
    out = None
    for t in terms:
        if t is not None:
            out = t if out is None else out & t
    return out


def lanes_of(n, wide):
    return 1 if n == 2 else 4 if wide else 2


class Flow:
    def __init__(self, row, count, middle, phase, axis, n, c, w, owners, left, free, active, parity, lag, summing):
        self.row, self.count, self.middle, self.phase, self.axis = row, count, middle, phase, axis
        self.n, self.c, self.w, self.owners, self.left, self.free = n, c, w, owners, left, free
        self.active, self.parity, self.lag, self.summing = active, parity, lag, summing


class Own:
    def __init__(self, row, count, left, active, parity, sem, turns):
        self.row, self.count, self.left, self.active = row, count, left, active
        self.parity, self.sem, self.turns = parity, sem, turns


class Plan:
    def __init__(self, dims, total):
        self.d = lax.axis_index("dp")
        self.dims = dims
        self.total = total
        self.strides = (dims[1] * dims[2], dims[2], 1)
        self.coords = tuple(lax.rem(lax.div(self.d, s), n) for s, n in zip(self.strides, dims))
        self.depth = self.streams = self.arrivals = self.owns = 0
        self.shares = [self.lay_out(*share) for share in SHARES]

    def flow(self, **fields):
        f = Flow(**fields)
        f.turns = self.total if f.parity is None else (self.total + 1 - f.parity) // 2
        f.wide = f.middle and f.phase == 0 and f.n > 2
        f.lanes = lanes_of(f.n, f.wide)
        f.stream, f.arrival = self.streams, self.arrivals
        self.streams += f.lanes
        self.arrivals += f.lanes * f.turns
        return f

    def lay_out(self, row, count, axis, orders, middle):
        share = dict(row=row, count=count, middle=middle)

        def phase(p, axis, lag, left, free, active, parity):
            n, c = self.dims[axis], self.coords[axis]
            w = WIDTH >> (p + 1)
            inner = middle and p == 0 and n > 2
            owners = (n // 2 - 1, n // 2) if inner else (0, n - 1)
            top = c == owners[1]
            half = jnp.where(top, w, 0)
            used = 0 if middle and p == 0 else w - half
            now = both(active, (c == owners[0]) | top) if n > 2 else active
            fields = dict(share, phase=p, axis=axis, n=n, c=c, w=w, owners=owners, left=left, free=free,
                          active=active, parity=parity)
            hops = (n // 2 if inner else n - 1, max(owners[1], n - 1 - owners[0]))
            return fields, hops, left + half, free + used, now

        free = 512 if middle else 0
        first, hops, left, free, gate = phase(0, axis, 0, 0, free, None, None)
        start = hops[0]
        inner = []
        for parity, order in enumerate(orders):
            key = None if len(orders) == 1 else parity
            lag = start
            second, hops2, left2, free2, gate2 = phase(1, order[0], lag, left, free, gate, key)
            third, hops3, left3, _, gate3 = phase(2, order[1], lag, left2, free2, gate2, key)
            own = Own(row=row, count=count, left=left3, active=gate3, parity=key, sem=self.owns,
                       turns=self.total if key is None else (self.total + 1 - key) // 2)
            self.owns += own.turns
            flows = [self.flow(**second, lag=lag, summing=True)]
            lag += hops2[0]
            flows.append(self.flow(**third, lag=lag, summing=True))
            lag += hops3[0]
            own.start = lag
            flows.append(self.flow(**third, lag=lag, summing=False))
            lag += hops3[1]
            own.end = lag
            flows.append(self.flow(**second, lag=lag, summing=False))
            lag += hops2[1]
            inner.append((key, flows, own))
        before = self.flow(**first, lag=0, summing=True)
        after = self.flow(**first, lag=lag, summing=False)
        self.depth = max(self.depth, lag + hops[1])
        return before, gate, inner, after


def due(plan, job, steady, parity, *terms):
    return both(None if steady else (job >= 0) & (job < plan.total),
                None if parity is None else lax.rem(job, 2) == parity, *terms)


def when(ok):
    return (lambda f: f()) if ok is None else pl.when(ok)


def move(plan, flow, refs, job, cols, spot, step, lane, short=False):
    held, landing, side, result, send_sem, recv_sem = refs
    turn = job if flow.parity is None else lax.div(job, 2)
    rows = pl.ds(flow.row, flow.count)
    at = lambda first: pl.ds(first if isinstance(first, int) else pl.multiple_of(first, 128), flow.w)
    if not flow.summing:
        src = dst = result.at[job, rows, at(cols)]
    else:
        src = held.at[job, rows, at(cols)]
        if short or (flow.middle and flow.phase > 0):
            dst = side.at[job, pl.ds(0, flow.count), at(spot)]
        else:
            dst = landing.at[job, rows, at(spot)]

    def make(source):
        return pltpu.make_async_remote_copy(
            src_ref=source, dst_ref=dst, send_sem=send_sem.at[flow.stream + lane, lax.rem(turn, RING)],
            recv_sem=recv_sem.at[flow.arrival + lane * flow.turns + turn],
            device_id={"dp": plan.d + step}, device_id_type=MESH)

    def send(first_owner=False):
        copy = make(held.at[job, rows, at(cols)] if first_owner else src)
        @pl.when(turn >= RING)
        def _():
            copy.wait_send()
        copy.start()

    def receive():
        make(src).wait_recv()
        if flow.summing:
            place = (job, rows, at(cols))
            held[place] = held[place] + dst[...]

    def finish():
        @pl.when(turn >= flow.turns - RING)
        def _():
            make(src).wait_send()

    return send, receive, finish


def run_flow(plan, flow, tick, refs, steady, ending=False):
    n, c, w, left = flow.n, flow.c, flow.w, flow.left
    stride = plan.strides[flow.axis]
    from_held = not flow.summing and flow.phase == 2
    if n == 2:
        own, other = jnp.where(c == 1, w, 0), jnp.where(c == 1, 0, w)
        out, back = (other, own) if flow.summing else (own, other)
        step = jnp.where(c == 1, -stride, stride)
        job = tick - flow.lag
        send, _, finish = move(plan, flow, refs, job, left + out, flow.free + out, step, 0)
        @when(due(plan, job, steady, flow.parity))
        def _():
            finish() if ending else send(from_held)
        if not ending:
            job = job - 1
            _, receive, _ = move(plan, flow, refs, job, left + back, flow.free + back, step, 0)
            @when(due(plan, job, steady, flow.parity))
            def _():
                receive()
        return
    for up in (True, False):
        owner = flow.owners[int(up)]
        for below in (True, False):
            if (owner if below else n - 1 - owner) == 0:
                continue
            place = c <= owner if below else c >= owner
            if flow.summing:
                hops = c if below else n - 1 - c
                sends = c < owner if below else c > owner
                step = stride if below else -stride
            else:
                hops = owner - c if below else c - owner
                sends = c > 0 if below else c < n - 1
                step = -stride if below else stride
            job = tick - flow.lag - hops
            lower = w if up else 0
            short = flow.summing and flow.middle and flow.phase == 0 and up != below
            if short:
                spot = 0
            elif flow.middle and flow.phase == 0:
                spot = lower
            else:
                spot = flow.free + lower
            send, receive, finish = move(
                plan, flow, refs, job, left + lower, spot, step, 2 * int(up) + int(below) if flow.wide else int(up), short)
            @when(due(plan, job, steady, flow.parity, place, flow.active if flow.phase == 2 else None))
            def _():
                if ending:
                    pl.when(sends)(finish)
                    return
                pl.when(hops > 0)(receive)
                if from_held:
                    pl.when(sends & (hops == 0))(functools.partial(send, True))
                    pl.when(sends & (hops > 0))(send)
                else:
                    pl.when(sends)(send)


def own_copy(plan, own, refs, job, own_sem):
    turn = job if own.parity is None else lax.div(job, 2)
    part = (job, pl.ds(own.row, own.count), pl.ds(pl.multiple_of(own.left, 128), WIDTH >> 3))
    return pltpu.make_async_copy(refs[0].at[part], refs[3].at[part], own_sem.at[own.sem + turn])


def serve(plan, shares, tick, refs, own_sem, steady, ending=False):
    for k in shares:
        before, gate, inner, after = plan.shares[k]
        run_flow(plan, before, tick, refs, steady, ending)

        @when(gate)
        def _():
            for parity, flows, own in inner:
                for flow in flows:
                    if not flow.summing and not ending:
                        opens = flow.phase == 2
                        job = tick - (own.start if opens else own.end)
                        @when(due(plan, job, steady, parity, own.active))
                        def _():
                            copy = own_copy(plan, own, refs, job, own_sem)
                            copy.start() if opens else copy.wait()
                    run_flow(plan, flow, tick, refs, steady, ending)
        run_flow(plan, after, tick, refs, steady, ending)


def greet(plan):
    barrier = pltpu.get_barrier_semaphore()
    count = 0
    for n, c, s in zip(plan.dims, plan.coords, plan.strides):
        for inside, step in ((c > 0, -s), (c < n - 1, s)):
            @pl.when(inside)
            def _():
                pl.semaphore_signal(barrier, inc=1, device_id={"dp": plan.d + step}, device_id_type=MESH)
            count = count + inside.astype(jnp.int32)
    pl.semaphore_wait(barrier, count)


class Small:
    def __init__(self, plan, partial, arriving, whole, sems):
        self.partial, self.whole = partial, whole
        self.steps, tick, active = [], 0, None
        for axis in (2, 1, 0):
            n, c = plan.dims[axis], plan.coords[axis]
            gather = pltpu.make_async_remote_copy(
                src_ref=partial, dst_ref=arriving.at[axis], send_sem=sems.at[axis], recv_sem=sems.at[3 + axis],
                device_id={"dp": plan.d + plan.strides[axis]}, device_id_type=MESH)
            spread = pltpu.make_async_remote_copy(
                src_ref=whole, dst_ref=whole, send_sem=sems.at[6 + axis], recv_sem=sems.at[9 + axis],
                device_id={"dp": plan.d - plan.strides[axis]}, device_id_type=MESH)
            self.steps.append((n, c, tick, active, gather, spread, arriving.at[axis]))
            tick += n - 1
            active = both(active, c == n - 1)
        self.last = (tick, active)

    def serve(self, t):
        for n, c, start, active, gather, _, arriving in self.steps:
            @when(both(t == start + c, active))
            def _():
                @pl.when(c > 0)
                def _():
                    gather.wait_recv()
                    self.partial[...] += arriving[...]
                pl.when(c < n - 1)(gather.start)
        tick, active = self.last

        @when(both(t == tick, active))
        def _():
            self.whole[...] = self.partial[...]
        for n, c, start, active, _, spread, _ in self.steps[::-1]:
            @when(both(t == 2 * tick - start - c, active))
            def _():
                pl.when(c < n - 1)(spread.wait_recv)
                pl.when(c > 0)(spread.start)

    def finish(self):
        for n, c, _, active, gather, spread, _ in self.steps:
            @when(active)
            def _():
                pl.when(c < n - 1)(gather.wait_send)
                pl.when(c > 0)(spread.wait_send)


def weights_kernel(dims, tiles, total, left_ref, right_ref, extra_ref, small_ref, result, small_sum, held, landing, side,
                   left_buf, right_buf, partial, arriving, whole, load_sem, send_sem, recv_sem, own_sem, small_sem):
    plan = Plan(dims, total)
    per = WIDTH // TILE
    greet(plan)

    def left_copy(s):
        job, part = lax.div(s, per), lax.rem(s, per)
        slab = jnp.where(job < 4, job, jnp.where(job < 8, 4, jnp.minimum(job - 3, 7)))
        return pltpu.make_async_copy(
            left_ref.at[:, pl.ds(pl.multiple_of(slab * WIDTH + part * TILE, TILE), TILE)],
            left_buf, load_sem.at[0])

    def right_copy(job):
        slab = jnp.where(job < 4, 0, job - 3)
        return pltpu.make_async_copy(
            right_ref.at[:, pl.ds(pl.multiple_of(slab * WIDTH, WIDTH), WIDTH)],
            right_buf, load_sem.at[1])

    def product(s):
        left_copy(s).wait()
        @pl.when(lax.rem(s, per) == 0)
        def _():
            right_copy(lax.div(s, per)).wait()
        held[s] = lax.dot_general(
            left_buf[...], right_buf[...], (((0,), (0,)), ((), ())),
            preferred_element_type=jnp.float32).astype(jnp.bfloat16)
        @pl.when(s + 1 < tiles)
        def _():
            left_copy(s + 1).start()
            @pl.when(lax.rem(s + 1, per) == 0)
            def _():
                right_copy(lax.div(s + 1, per)).start()

    extras = pltpu.make_async_copy(extra_ref, held.at[pl.ds(tiles, total - tiles)], load_sem.at[2])
    left_copy(0).start()
    right_copy(0).start()
    extras.start()
    product(0)
    extras.wait()
    refs = (held, landing, side, result, send_sem, recv_sem)

    def tick(steady, t, _):
        serve(plan, (1, 0, 2, 3), t, refs, own_sem, steady)
        @pl.when(t + 1 < tiles)
        def _():
            product(t + 1)
        return 0

    small = Small(plan, partial, arriving, whole, small_sem)
    partial[...] = small_ref[...]

    def first_tick(t, _):
        small.serve(t)
        return tick(False, t, 0)

    lax.fori_loop(0, plan.depth, first_tick, 0)
    small.serve(plan.depth)
    small.finish()
    small_sum[...] = whole[...]
    lax.fori_loop(plan.depth, total, functools.partial(tick, True), 0)
    lax.fori_loop(total, total + plan.depth, functools.partial(tick, False), 0)

    def finish(t, _):
        serve(plan, range(len(SHARES)), t, refs, own_sem, False, True)
        return 0

    lax.fori_loop(0, total + plan.depth, finish, 0)


def semaphores(dims, total):
    streams = arrivals = owns = 0
    for _, _, axis, orders, middle in SHARES:
        for parity, order in enumerate(orders):
            turns = total if len(orders) == 1 else (total + 1 - parity) // 2
            owns += turns
            for line in order:
                lanes = lanes_of(dims[line], False)
                streams, arrivals = streams + 2 * lanes, arrivals + 2 * lanes * turns
        lanes = lanes_of(dims[axis], middle and dims[axis] > 2)
        streams, arrivals = streams + 2 * lanes, arrivals + 2 * lanes * total
    return streams, arrivals, owns


def weight_sums(dims, lefts, rights, extras, small, cid):
    tiles = 12 * (WIDTH // TILE)
    total = tiles + extras.shape[0]
    rows = lefts.shape[0]
    streams, arrivals, owns = semaphores(dims, total)
    any_space = pl.BlockSpec(memory_space=pl.ANY)
    vmem = pl.BlockSpec(memory_space=pltpu.VMEM)
    return pl.pallas_call(
        functools.partial(weights_kernel, dims, tiles, total),
        out_shape=(jax.ShapeDtypeStruct((total, TILE, WIDTH), jnp.bfloat16),
                   jax.ShapeDtypeStruct(small.shape, jnp.float32)),
        in_specs=[any_space] * 3 + [vmem],
        out_specs=(any_space, vmem),
        scratch_shapes=[
            pltpu.VMEM((total, TILE, WIDTH), jnp.bfloat16),
            pltpu.VMEM((total, TILE, WIDTH), jnp.bfloat16),
            pltpu.VMEM((total, MIDDLE_ROWS, WIDTH), jnp.bfloat16),
            pltpu.VMEM((rows, TILE), jnp.bfloat16),
            pltpu.VMEM((rows, WIDTH), jnp.bfloat16),
            pltpu.VMEM(small.shape, jnp.float32),
            pltpu.VMEM((3,) + small.shape, jnp.float32),
            pltpu.VMEM(small.shape, jnp.float32),
            pltpu.SemaphoreType.DMA((3,)),
            pltpu.SemaphoreType.DMA((streams, RING)),
            pltpu.SemaphoreType.DMA((arrivals,)),
            pltpu.SemaphoreType.DMA((owns,)),
            pltpu.SemaphoreType.DMA((12,)),
        ],
        compiler_params=pltpu.CompilerParams(collective_id=cid, has_side_effects=True, vmem_limit_bytes=63 * 2**20),
        cost_estimate=pl.CostEstimate(flops=2 * 12 * rows * WIDTH * WIDTH, bytes_accessed=100 * 2**20, transcendentals=0),
    )(lefts, rights, extras, small)


HEADS = 8
CHUNK = 1024
LOW = jnp.bfloat16
WIDE = jnp.float32
NN = (((1,), (0,)), ((), ()))
NT = (((1,), (1,)), ((), ()))
TN = (((0,), (0,)), ((), ()))


def dot(a, b, form):
    return lax.dot_general(a, b, form, preferred_element_type=WIDE)


def normalize(values):
    center = values - jnp.mean(values, -1, keepdims=True)
    inverse = lax.rsqrt(jnp.mean(center * center, -1, keepdims=True) + 1e-05)
    return center * inverse, inverse


def norm_back(upstream, gain, xhat, inverse):
    scaled = upstream * gain
    return inverse * (scaled - jnp.mean(scaled, -1, keepdims=True)
                      - xhat * jnp.mean(scaled * xhat, -1, keepdims=True))


def gelu_pair(u):
    c = 0.7978845608028654
    square = u * u
    t = jnp.tanh(u * (c + (c * 0.044715) * square))
    half = 0.5 * (1.0 + t)
    slope = half + (0.5 * u) * (1.0 - t * t) * (c + (3.0 * c * 0.044715) * square)
    return u * half, slope


def layers_kernel(groups, tokens, clip_frames, cotangent, embed, norm_params, w_qkv, w_out, w_up, w_down,
                  lefts, rights, sec_out, sec_grad, extra, sizes, g_params, params, g_embed,
                  qkv_w, out_w, up_w, down_w, emb, src, upstream, qkv, probs, slopes, xhat_f, stats,
                  keep, passed, acc, hid, u_buf,
                  w_sem, in_sem, left_sem, right_sem, wide_sem, send_sem, recv_sem):
    section = lax.axis_index("section")
    first = section == 0
    other = 1 - section
    slots, width = emb.shape
    units = up_w.shape[1]
    steps = units // CHUNK
    head = width // HEADS
    scale = head ** -0.5

    loads = [pltpu.make_async_copy(a, b, w_sem.at[k]) for k, (a, b) in enumerate(
        ((w_qkv, qkv_w), (w_out, out_w), (w_up, up_w), (w_down, down_w), (embed, emb), (norm_params, params)))]
    loads[4].start()
    loads[5].start()
    loads[0].start()

    def token_load(g):
        return pltpu.make_async_copy(tokens.at[g], src.at[g], in_sem.at[g])

    def cot_load(g):
        return pltpu.make_async_copy(cotangent.at[g], upstream.at[g], in_sem.at[groups + g])

    @pl.when(first)
    def _():
        for g in range(groups):
            token_load(g).start()
    for k in (1, 2, 3):
        loads[k].start()

    barrier = pltpu.get_barrier_semaphore()
    pl.semaphore_signal(barrier, inc=1, device_id={"section": other}, device_id_type=MESH)
    pl.semaphore_wait(barrier, 1)

    def relay(g):
        return pltpu.make_async_remote_copy(
            src_ref=passed, dst_ref=src.at[g], send_sem=send_sem.at[g], recv_sem=recv_sem.at[g],
            device_id={"section": other}, device_id_type=MESH)

    def relay_back(g):
        return pltpu.make_async_remote_copy(
            src_ref=passed, dst_ref=upstream.at[g], send_sem=send_sem.at[groups + g],
            recv_sem=recv_sem.at[groups + g], device_id={"section": other}, device_id_type=MESH)

    def rows_of(g):
        return pl.ds(pl.multiple_of(g * slots, slots), slots)

    def cols(i, w=CHUNK):
        return pl.ds(pl.multiple_of(i * w, w), w)

    def left_store(g, k):
        return pltpu.make_async_copy(
            keep.at[:, pl.ds((k - 1) * width, width)], lefts.at[rows_of(g), pl.ds(units + (k - 1) * width, width)], left_sem.at[k])

    def right_store(g, k):
        if k == 0:
            return pltpu.make_async_copy(upstream.at[g], rights.at[rows_of(g), pl.ds(0, width)], right_sem.at[0])
        return pltpu.make_async_copy(
            keep.at[:, pl.ds((k - 2) * width, width)],
            rights.at[rows_of(g), pl.ds(width + units + (k - 2) * width, width)], right_sem.at[k])

    def left_chunk(g, i):
        return pltpu.make_async_copy(
            upstream.at[i], lefts.at[rows_of(g), pl.ds(i * CHUNK, CHUNK)], left_sem.at[5 + i])

    def right_chunk(g, i):
        return pltpu.make_async_copy(
            slopes.at[g, :, pl.ds(i * CHUNK, CHUNK)],
            rights.at[rows_of(g), pl.ds(width + i * CHUNK, CHUNK)], right_sem.at[6 + i])

    def out_store(g):
        return pltpu.make_async_copy(acc, sec_out.at[g], wide_sem.at[0])

    def grad_store(g):
        return pltpu.make_async_copy(acc, sec_grad.at[g], wide_sem.at[1])

    def base_of(g):
        return jnp.where(first, 0.0, src[g].astype(WIDE)) + emb[...].astype(WIDE)

    stage = pl.when(section >= 0)

    def heads_of(g, h):
        return tuple(qkv[g, :, k * width + h * head:k * width + (h + 1) * head] for k in range(3))

    def forward(g):
        @pl.when(first)
        def _():
            token_load(g).wait()
        @pl.when(section == 1)
        def _():
            relay(g).wait_recv()

        @stage
        def _():
            @pl.when(g == 0)
            def _():
                loads[4].wait()
                loads[5].wait()

            @pl.when(g > 0)
            def _():
                for k in (3, 4):
                    left_store(g - 1, k).wait()
            source = src[g].astype(WIDE)
            xhat, inverse = normalize(source)
            stats[g, :, 0:1] = inverse
            stats[g, :, 3:4] = jnp.mean(source, -1, keepdims=True)
            keep[:, 3 * width:4 * width] = (xhat * params[2:3] + params[3:4]).astype(LOW)
            @pl.when(g == 0)
            def _():
                loads[0].wait()
            for k, rows in ((1, 3), (2, 3)):
                part = slice(k * width, (k + 1) * width)
                qkv[g, :, part] = dot(keep[:, rows * width:(rows + 1) * width], qkv_w[:, part], NN).astype(LOW)
            base = base_of(g)
            xhat, inverse = normalize(base)
            stats[g, :, 1:2] = inverse
            stats[g, :, 4:5] = jnp.mean(base, -1, keepdims=True)
            keep[:, 2 * width:3 * width] = (xhat * params[0:1] + params[1:2]).astype(LOW)
            qkv[g, :, 0:width] = dot(keep[:, 2 * width:3 * width], qkv_w[:, 0:width], NN).astype(LOW)
            left_store(g, 3).start()
            left_store(g, 4).start()

        @stage
        def _():
            @pl.when(g > 0)
            def _():
                for k in (1, 2):
                    left_store(g - 1, k).wait()
            limit = jnp.where(first, clip_frames[g] * (slots // 16), slots)
            seen = lax.broadcasted_iota(jnp.int32, (1, slots), 1) < limit
            for h in range(HEADS):
                q, k, v = heads_of(g, h)
                s = jnp.where(seen, dot(q, k, NT) * scale, -1e30)
                e = jnp.exp(s - jnp.max(s, -1, keepdims=True))
                p = (e / jnp.sum(e, -1, keepdims=True)).astype(LOW)
                probs[g, h] = p
                keep[:, width + h * head:width + (h + 1) * head] = dot(p, v, NN).astype(LOW)
            left_store(g, 2).start()
            @pl.when(g == 0)
            def _():
                loads[1].wait()

        @stage
        def _():
            hid[...] = dot(keep[:, width:2 * width], out_w[...], NN)
            hidden = base_of(g) + hid[...]
            hid[...] = hidden
            xhat, inverse = normalize(hidden)
            stats[g, :, 2:3] = inverse
            xhat_f[g] = xhat.astype(LOW)
            keep[:, 0:width] = (xhat * params[4:5] + params[5:6]).astype(LOW)
            left_store(g, 1).start()
            @pl.when(g == 0)
            def _():
                loads[2].wait()
                loads[3].wait()

            @pl.when(g > 0)
            def _():
                out_store(g - 1).wait()
                for i in range(steps):
                    left_chunk(g - 1, i).wait()

        @stage
        def _():
            chunks = [slice(i * CHUNK, (i + 1) * CHUNK) for i in range(steps)]
            u_buf[0] = dot(keep[:, 0:width], up_w[:, chunks[0]], NN)
            for i, part in enumerate(chunks):
                if i + 1 < steps:
                    u_buf[(i + 1) % 2] = dot(keep[:, 0:width], up_w[:, chunks[i + 1]], NN)
                value, slope = gelu_pair(u_buf[i % 2])
                slopes[g, :, part] = slope.astype(LOW)
                value = value.astype(LOW)
                upstream[i] = value
                term = dot(value, down_w[part, :], NN)
                if i == 0:
                    acc[...] = hid[...] + term
                else:
                    acc[...] += term
            for i in range(steps):
                left_chunk(g, i).start()
            out_store(g).start()

        @pl.when(first)
        def _():
            @pl.when(g > 0)
            def _():
                relay(g - 1).wait_send()
                @pl.when(g == groups - 1)
                def _():
                    for i in range(steps):
                        left_chunk(g, i).wait()
            passed[...] = acc[...].astype(LOW)
            relay(g).start()

    pl.loop(0, groups)(forward)

    for k in range(1, 5):
        left_store(groups - 1, k).wait()
    out_store(groups - 1).wait()

    @pl.when(first)
    def _():
        relay(groups - 1).wait_send()

    @pl.when(section == 1)
    def _():
        for i in range(steps):
            left_chunk(groups - 1, i).wait()
        for g in range(groups):
            cot_load(g).start()

    g_params[...] = jnp.zeros_like(g_params)
    g_embed[...] = jnp.zeros_like(g_embed)

    def gains(row, e, xhat):
        g_params[row:row + 1] += jnp.sum(e * xhat, axis=0, keepdims=True)
        g_params[row + 1:row + 2] += jnp.sum(e, axis=0, keepdims=True)

    def backward(g):
        @pl.when(first)
        def _():
            relay_back(g).wait_recv()
        @pl.when(section == 1)
        def _():
            cot_load(g).wait()

        @stage
        def _():
            @pl.when(g > 0)
            def _():
                for k in (2, 3, 4, 5):
                    right_store(g - 1, k).wait()
                right_store(g - 1, 0).wait()
                for i in range(steps):
                    right_chunk(g - 1, i).wait()
                grad_store(g - 1).wait()
            right_store(g, 0).start()
            chunks = [slice(i * CHUNK, (i + 1) * CHUNK) for i in range(steps)]
            u_buf[0] = dot(upstream[g], down_w[chunks[0], :], NT)
            for i, part in enumerate(chunks):
                if i + 1 < steps:
                    u_buf[(i + 1) % 2] = dot(upstream[g], down_w[chunks[i + 1], :], NT)
                value = (u_buf[i % 2] * slopes[g, :, part].astype(WIDE)).astype(LOW)
                slopes[g, :, part] = value
                term = dot(value, up_w[:, part], NT)
                if i == 0:
                    acc[...] = term
                else:
                    acc[...] += term

        @stage
        def _():
            for i in range(steps):
                right_chunk(g, i).start()
            e = acc[...]
            xhat = xhat_f[g].astype(WIDE)
            gains(4, e, xhat)
            grad_hidden = upstream[g].astype(WIDE) + norm_back(e, params[4:5], xhat, stats[g, :, 2:3])
            hid[...] = grad_hidden
            keep[:, 0:width] = grad_hidden.astype(LOW)
            xhat_f[g] = dot(keep[:, 0:width], out_w[...], NT).astype(LOW)

        @stage
        def _():
            for h in range(HEADS):
                q, k, v = heads_of(g, h)
                m = xhat_f[g, :, h * head:(h + 1) * head]
                low = probs[g, h]
                p = low.astype(WIDE)
                gp = dot(m, v, NT)
                ds = (p * (gp - jnp.sum(gp * p, -1, keepdims=True))).astype(LOW)
                keep[:, width + h * head:width + (h + 1) * head] = (dot(ds, k, NN) * scale).astype(LOW)
                keep[:, 2 * width + h * head:2 * width + (h + 1) * head] = (dot(ds, q, TN) * scale).astype(LOW)
                keep[:, 3 * width + h * head:3 * width + (h + 1) * head] = dot(low, m, TN).astype(LOW)
            for k in (2, 3, 4, 5):
                right_store(g, k).start()

        @stage
        def _():
            acc[...] = dot(keep[:, width:2 * width], qkv_w[:, 0:width], NT)
            u_buf[0] = dot(keep[:, 2 * width:4 * width], qkv_w[:, width:3 * width], NT)
            e = acc[...]
            xhat = (base_of(g) - stats[g, :, 4:5]) * stats[g, :, 1:2]
            gains(0, e, xhat)
            grad_base = hid[...] + norm_back(e, params[0:1], xhat, stats[g, :, 1:2])
            g_embed[...] += grad_base
            hid[...] = grad_base

        @stage
        def _():
            e = u_buf[0]
            xhat = (src[g].astype(WIDE) - stats[g, :, 3:4]) * stats[g, :, 0:1]
            gains(2, e, xhat)
            acc[...] = norm_back(e, params[2:3], xhat, stats[g, :, 0:1])

        @pl.when(section == 1)
        def _():
            @pl.when(g > 0)
            def _():
                relay_back(g - 1).wait_send()
            low = (acc[...] + hid[...]).astype(LOW)
            passed[...] = low
            relay_back(g).start()
            acc[...] = low.astype(WIDE)
        grad_store(g).start()
        total = acc[...]
        total = jnp.sum(jnp.sum(total * total, axis=0, keepdims=True), axis=1, keepdims=True)
        sizes[pl.ds(g, 1), :] = jnp.broadcast_to(
            jnp.sqrt(total / (slots * width) + 1e-06), (1, sizes.shape[1]))

    pl.loop(0, groups)(backward)

    for k in (0, 2, 3, 4, 5):
        right_store(groups - 1, k).wait()
    for i in range(steps):
        right_chunk(groups - 1, i).wait()
    grad_store(groups - 1).wait()

    g_params[6:7] = jnp.broadcast_to(jnp.sum(sizes[:, 0:1], axis=0, keepdims=True), (1, width))
    keep[:, 0:width] = g_embed[...].astype(LOW)
    pltpu.make_async_copy(keep.at[:, pl.ds(0, width)], extra.at[0], right_sem.at[0]).start()
    pltpu.make_async_copy(keep.at[:, pl.ds(0, width)], extra.at[0], right_sem.at[0]).wait()

    @pl.when(section == 1)
    def _():
        relay_back(groups - 1).wait_send()


def layers(tokens, clip_frames, cotangent, embed, norm_params, w_qkv, w_out, w_up, w_down, cid):
    groups, slots, width = tokens.shape
    units = w_up.shape[1]
    rows = groups * slots
    hbm = pl.BlockSpec(memory_space=pl.ANY)
    vmem = pl.BlockSpec(memory_space=pltpu.VMEM)
    shape = jax.ShapeDtypeStruct
    return pl.pallas_call(
        functools.partial(layers_kernel, groups),
        out_shape=(
            shape((rows, units + 4 * width), LOW),
            shape((rows, units + 5 * width), LOW),
            shape((groups, slots, width), WIDE),
            shape((groups, slots, width), WIDE),
            shape((1, slots, width), LOW),
            shape((groups, 128), WIDE),
            shape((8, width), WIDE),
        ),
        in_specs=[hbm, pl.BlockSpec(memory_space=pltpu.SMEM)] + [hbm] * 7,
        out_specs=(hbm, hbm, hbm, hbm, hbm, vmem, vmem),
        scratch_shapes=[
            pltpu.VMEM(norm_params.shape, WIDE),
            pltpu.VMEM((slots, width), WIDE),
            pltpu.VMEM(w_qkv.shape, LOW),
            pltpu.VMEM(w_out.shape, LOW),
            pltpu.VMEM(w_up.shape, LOW),
            pltpu.VMEM(w_down.shape, LOW),
            pltpu.VMEM((slots, width), LOW),
            pltpu.VMEM((groups, slots, width), LOW),
            pltpu.VMEM((max(groups, units // CHUNK), slots, width), LOW),
            pltpu.VMEM((groups, slots, 3 * width), LOW),
            pltpu.VMEM((groups, HEADS, slots, slots), LOW),
            pltpu.VMEM((groups, slots, units), LOW),
            pltpu.VMEM((groups, slots, width), LOW),
            pltpu.VMEM((groups, slots, 128), WIDE),
            pltpu.VMEM((slots, 4 * width), LOW),
            pltpu.VMEM((slots, width), LOW),
            pltpu.VMEM((slots, width), WIDE),
            pltpu.VMEM((slots, width), WIDE),
            pltpu.VMEM((2, slots, CHUNK), WIDE),
            pltpu.SemaphoreType.DMA((6,)),
            pltpu.SemaphoreType.DMA((2 * groups,)),
            pltpu.SemaphoreType.DMA((5 + units // CHUNK,)),
            pltpu.SemaphoreType.DMA((6 + units // CHUNK,)),
            pltpu.SemaphoreType.DMA((2,)),
            pltpu.SemaphoreType.DMA((2 * groups,)),
            pltpu.SemaphoreType.DMA((2 * groups,)),
        ],
        compiler_params=pltpu.CompilerParams(
            collective_id=cid, has_side_effects=True, vmem_limit_bytes=63 * 2**20),
        cost_estimate=pl.CostEstimate(flops=54 * 10**9, bytes_accessed=120 * 2**20, transcendentals=10**7),
    )(tokens, clip_frames, cotangent, embed, norm_params, w_qkv, w_out, w_up, w_down)


DEEP = 4


def widen_kernel(places, count, sums, sizes, shared, *refs):
    outs, (embed, params, norms, narrow, wide, read_sem, write_sem) = refs[:len(places)], refs[len(places):]
    steps = places[-1][0] + places[-1][1]
    tall, width = wide.shape[1:]

    def read(i):
        slot = lax.rem(i, DEEP)
        return pltpu.make_async_copy(sums.at[pl.ds(2 * i, 2)], narrow.at[slot], read_sem.at[slot])

    for i in range(DEEP):
        read(i).start()

    for (first, number, down, across), out in zip(places, outs):
        def write(i):
            slot, k = lax.rem(i, DEEP), i - first
            rows = pl.ds(pl.multiple_of(lax.rem(k, down) * tall, tall), tall)
            cols = pl.ds(pl.multiple_of(lax.div(k, down) * width, width), width)
            return pltpu.make_async_copy(wide.at[slot], out.at[rows, cols], write_sem.at[slot])

        @pl.loop(first, first + number)
        def _(i):
            slot = lax.rem(i, DEEP)
            read(i).wait()
            @pl.when(i >= DEEP)
            def _():
                write(i).wait()
            wide[slot] = narrow[slot].reshape(tall, width).astype(WIDE)
            write(i).start()
            @pl.when(i + DEEP < steps)
            def _():
                read(i + DEEP).start()

    tail = pltpu.make_async_copy(sums.at[2 * steps], narrow.at[0, 0], read_sem.at[0])
    tail.start()
    params[...] = shared[0:6]
    mean = shared[6:7, 0:1] / count
    here = jnp.zeros(norms.shape, WIDE)
    for g in range(norms.shape[1]):
        lane = lax.broadcasted_iota(jnp.int32, norms.shape, 1) == g
        here = jnp.where(lane, sizes[g:g + 1, 0:1] / mean, here)
    norms[...] = here
    tail.wait()
    embed[...] = narrow[0, 0].astype(WIDE)
    for i in range(steps - DEEP, steps):
        write(i).wait()


def widen(sums, sizes, shared, count, places):
    tile, width = sums.shape[1:]
    steps = sum(p[1] for p in places)
    shape = jax.ShapeDtypeStruct
    hbm, vmem = pl.BlockSpec(memory_space=pl.ANY), pl.BlockSpec(memory_space=pltpu.VMEM)
    return pl.pallas_call(
        lambda *refs: widen_kernel(places, count, *refs),
        out_shape=tuple(shape((p[2] * 2 * tile, p[3] * width), WIDE) for p in places)
        + (shape((tile, width), WIDE), shape((6, width), WIDE), shape((1, sizes.shape[0]), WIDE)),
        in_specs=[hbm, vmem, vmem],
        out_specs=(hbm,) * len(places) + (vmem,) * 3,
        scratch_shapes=[
            pltpu.VMEM((DEEP, 2, tile, width), LOW),
            pltpu.VMEM((DEEP, 2 * tile, width), WIDE),
            pltpu.SemaphoreType.DMA((DEEP,)),
            pltpu.SemaphoreType.DMA((DEEP,)),
        ],
        compiler_params=pltpu.CompilerParams(vmem_limit_bytes=48 * 2**20),
        cost_estimate=pl.CostEstimate(flops=0, bytes_accessed=12 * steps * tile * width, transcendentals=0),
    )(sums, sizes, shared)


def body(tokens, clip_frames, cotangent, embed, norm_params, w_qkv, w_out, w_up, w_down):
    groups = tokens.shape[0]
    devices = lax.axis_size("dp")
    lefts, rights, outcome, grad_inputs, extra, sizes, g_params = layers(
        tokens, clip_frames, cotangent, embed[0], norm_params[0], w_qkv[0], w_out[0], w_up[0], w_down[0], 2
    )
    sums, shared = weight_sums(lines_of(devices), lefts, rights, extra, g_params, 1)
    down, up, out, qkv, g_embed, g_params, norms = widen(
        sums, sizes, shared, groups * devices, ((0, 8, 8, 1), (8, 8, 2, 4), (16, 2, 2, 1), (18, 6, 2, 3))
    )
    return (
        outcome[None],
        grad_inputs[None],
        qkv[None],
        out[None],
        up[None],
        down[None],
        g_params[None],
        g_embed[None],
        norms,
    )


def solution(mesh):
    placed = (
        P("dp", None, None),
        P("dp"),
        P("dp", None, None),
        P("section", None, None),
        P("section", None, None),
        P("section", None, None),
        P("section", None, None),
        P("section", None, None),
        P("section", None, None),
    )
    return jax.shard_map(
        body,
        mesh=mesh,
        in_specs=placed,
        out_specs=(
            P("section", "dp", None, None),
            P("section", "dp", None, None),
            P("section", None, None),
            P("section", None, None),
            P("section", None, None),
            P("section", None, None),
            P("section", None, None),
            P("section", None, None),
            P("section", "dp"),
        ),
        check_vma=False,
    )
```

```python
import functools

import jax
import jax.numpy as jnp
from jax import lax
from jax.experimental import pallas as pl
from jax.experimental.pallas import tpu as pltpu
from jax.sharding import PartitionSpec as P

MESH = pl.DeviceIdType.MESH
TILE = 256
WIDTH = 1024
RING = 8
SHARES = (
    (0, 80, 2, ((1, 0),), False),
    (160, 48, 0, ((2, 1), (1, 2)), False),
    (208, 48, 0, ((1, 2), (2, 1)), True),
    (80, 80, 1, ((2, 0),), False),
)
MIDDLE_ROWS = 48


def lines_of(size):
    short = 1
    while 2 * short**3 < size:
        short += 1
    assert 2 * short**3 == size
    return (2 * short, short, short)


def both(*terms):
    out = None
    for t in terms:
        if t is not None:
            out = t if out is None else out & t
    return out


def lanes_of(n, wide):
    return 1 if n == 2 else 4 if wide else 2


class Flow:
    def __init__(self, row, count, middle, phase, axis, n, c, w, owners, left, free, active, parity, lag, summing):
        self.row, self.count, self.middle, self.phase, self.axis = row, count, middle, phase, axis
        self.n, self.c, self.w, self.owners, self.left, self.free = n, c, w, owners, left, free
        self.active, self.parity, self.lag, self.summing = active, parity, lag, summing


class Own:
    def __init__(self, row, count, left, active, parity, sem, turns):
        self.row, self.count, self.left, self.active = row, count, left, active
        self.parity, self.sem, self.turns = parity, sem, turns


class Plan:
    def __init__(self, dims, total):
        self.d = lax.axis_index("dp")
        self.dims = dims
        self.total = total
        self.strides = (dims[1] * dims[2], dims[2], 1)
        self.coords = tuple(lax.rem(lax.div(self.d, s), n) for s, n in zip(self.strides, dims))
        self.depth = self.streams = self.arrivals = self.owns = 0
        self.shares = [self.lay_out(*share) for share in SHARES]

    def flow(self, **fields):
        f = Flow(**fields)
        f.turns = self.total if f.parity is None else (self.total + 1 - f.parity) // 2
        f.wide = f.middle and f.phase == 0 and f.n > 2
        f.lanes = lanes_of(f.n, f.wide)
        f.stream, f.arrival = self.streams, self.arrivals
        self.streams += f.lanes
        self.arrivals += f.lanes * f.turns
        return f

    def lay_out(self, row, count, axis, orders, middle):
        share = dict(row=row, count=count, middle=middle)

        def phase(p, axis, lag, left, free, active, parity):
            n, c = self.dims[axis], self.coords[axis]
            w = WIDTH >> (p + 1)
            inner = middle and p == 0 and n > 2
            owners = (n // 2 - 1, n // 2) if inner else (0, n - 1)
            top = c == owners[1]
            half = jnp.where(top, w, 0)
            used = 0 if middle and p == 0 else w - half
            now = both(active, (c == owners[0]) | top) if n > 2 else active
            fields = dict(share, phase=p, axis=axis, n=n, c=c, w=w, owners=owners, left=left, free=free,
                          active=active, parity=parity)
            hops = (n // 2 if inner else n - 1, max(owners[1], n - 1 - owners[0]))
            return fields, hops, left + half, free + used, now

        free = 512 if middle else 0
        first, hops, left, free, gate = phase(0, axis, 0, 0, free, None, None)
        start = hops[0]
        inner = []
        for parity, order in enumerate(orders):
            key = None if len(orders) == 1 else parity
            lag = start
            second, hops2, left2, free2, gate2 = phase(1, order[0], lag, left, free, gate, key)
            third, hops3, left3, _, gate3 = phase(2, order[1], lag, left2, free2, gate2, key)
            own = Own(row=row, count=count, left=left3, active=gate3, parity=key, sem=self.owns,
                       turns=self.total if key is None else (self.total + 1 - key) // 2)
            self.owns += own.turns
            flows = [self.flow(**second, lag=lag, summing=True)]
            lag += hops2[0]
            flows.append(self.flow(**third, lag=lag, summing=True))
            lag += hops3[0]
            own.start = lag
            flows.append(self.flow(**third, lag=lag, summing=False))
            lag += hops3[1]
            own.end = lag
            flows.append(self.flow(**second, lag=lag, summing=False))
            lag += hops2[1]
            inner.append((key, flows, own))
        before = self.flow(**first, lag=0, summing=True)
        after = self.flow(**first, lag=lag, summing=False)
        self.depth = max(self.depth, lag + hops[1])
        return before, gate, inner, after


def due(plan, job, steady, parity, *terms):
    return both(None if steady else (job >= 0) & (job < plan.total),
                None if parity is None else lax.rem(job, 2) == parity, *terms)


def when(ok):
    return (lambda f: f()) if ok is None else pl.when(ok)


def move(plan, flow, refs, job, cols, spot, step, lane, short=False):
    held, landing, side, result, send_sem, recv_sem = refs
    turn = job if flow.parity is None else lax.div(job, 2)
    rows = pl.ds(flow.row, flow.count)
    at = lambda first: pl.ds(first if isinstance(first, int) else pl.multiple_of(first, 128), flow.w)
    if not flow.summing:
        src = dst = result.at[job, rows, at(cols)]
    else:
        src = held.at[job, rows, at(cols)]
        if short or (flow.middle and flow.phase > 0):
            dst = side.at[job, pl.ds(0, flow.count), at(spot)]
        else:
            dst = landing.at[job, rows, at(spot)]

    def make(source):
        return pltpu.make_async_remote_copy(
            src_ref=source, dst_ref=dst, send_sem=send_sem.at[flow.stream + lane, lax.rem(turn, RING)],
            recv_sem=recv_sem.at[flow.arrival + lane * flow.turns + turn],
            device_id={"dp": plan.d + step}, device_id_type=MESH)

    def send(first_owner=False):
        copy = make(held.at[job, rows, at(cols)] if first_owner else src)
        @pl.when(turn >= RING)
        def _():
            copy.wait_send()
        copy.start()

    def receive():
        make(src).wait_recv()
        if flow.summing:
            place = (job, rows, at(cols))
            held[place] = held[place] + dst[...]

    def finish():
        @pl.when(turn >= flow.turns - RING)
        def _():
            make(src).wait_send()

    return send, receive, finish


def run_flow(plan, flow, tick, refs, steady, ending=False):
    n, c, w, left = flow.n, flow.c, flow.w, flow.left
    stride = plan.strides[flow.axis]
    from_held = not flow.summing and flow.phase == 2
    if n == 2:
        own, other = jnp.where(c == 1, w, 0), jnp.where(c == 1, 0, w)
        out, back = (other, own) if flow.summing else (own, other)
        step = jnp.where(c == 1, -stride, stride)
        job = tick - flow.lag
        send, _, finish = move(plan, flow, refs, job, left + out, flow.free + out, step, 0)
        @when(due(plan, job, steady, flow.parity))
        def _():
            finish() if ending else send(from_held)
        if not ending:
            job = job - 1
            _, receive, _ = move(plan, flow, refs, job, left + back, flow.free + back, step, 0)
            @when(due(plan, job, steady, flow.parity))
            def _():
                receive()
        return
    for up in (True, False):
        owner = flow.owners[int(up)]
        for below in (True, False):
            if (owner if below else n - 1 - owner) == 0:
                continue
            place = c <= owner if below else c >= owner
            if flow.summing:
                hops = c if below else n - 1 - c
                sends = c < owner if below else c > owner
                step = stride if below else -stride
            else:
                hops = owner - c if below else c - owner
                sends = c > 0 if below else c < n - 1
                step = -stride if below else stride
            job = tick - flow.lag - hops
            lower = w if up else 0
            short = flow.summing and flow.middle and flow.phase == 0 and up != below
            if short:
                spot = 0
            elif flow.middle and flow.phase == 0:
                spot = lower
            else:
                spot = flow.free + lower
            send, receive, finish = move(
                plan, flow, refs, job, left + lower, spot, step, 2 * int(up) + int(below) if flow.wide else int(up), short)
            @when(due(plan, job, steady, flow.parity, place, flow.active if flow.phase == 2 else None))
            def _():
                if ending:
                    pl.when(sends)(finish)
                    return
                pl.when(hops > 0)(receive)
                if from_held:
                    pl.when(sends & (hops == 0))(functools.partial(send, True))
                    pl.when(sends & (hops > 0))(send)
                else:
                    pl.when(sends)(send)


def own_copy(plan, own, refs, job, own_sem):
    turn = job if own.parity is None else lax.div(job, 2)
    part = (job, pl.ds(own.row, own.count), pl.ds(pl.multiple_of(own.left, 128), WIDTH >> 3))
    return pltpu.make_async_copy(refs[0].at[part], refs[3].at[part], own_sem.at[own.sem + turn])


def serve(plan, shares, tick, refs, own_sem, steady, ending=False):
    for k in shares:
        before, gate, inner, after = plan.shares[k]
        run_flow(plan, before, tick, refs, steady, ending)

        @when(gate)
        def _():
            for parity, flows, own in inner:
                for flow in flows:
                    if not flow.summing and not ending:
                        opens = flow.phase == 2
                        job = tick - (own.start if opens else own.end)
                        @when(due(plan, job, steady, parity, own.active))
                        def _():
                            copy = own_copy(plan, own, refs, job, own_sem)
                            copy.start() if opens else copy.wait()
                    run_flow(plan, flow, tick, refs, steady, ending)
        run_flow(plan, after, tick, refs, steady, ending)


def greet(plan):
    barrier = pltpu.get_barrier_semaphore()
    count = 0
    for n, c, s in zip(plan.dims, plan.coords, plan.strides):
        for inside, step in ((c > 0, -s), (c < n - 1, s)):
            @pl.when(inside)
            def _():
                pl.semaphore_signal(barrier, inc=1, device_id={"dp": plan.d + step}, device_id_type=MESH)
            count = count + inside.astype(jnp.int32)
    return lambda: pl.semaphore_wait(barrier, count)


class Small:
    def __init__(self, plan, partial, arriving, whole, sems):
        self.partial, self.whole = partial, whole
        self.steps, tick, active = [], 0, None
        for axis in (2, 1, 0):
            n, c = plan.dims[axis], plan.coords[axis]
            gather = pltpu.make_async_remote_copy(
                src_ref=partial, dst_ref=arriving.at[axis], send_sem=sems.at[axis], recv_sem=sems.at[3 + axis],
                device_id={"dp": plan.d + plan.strides[axis]}, device_id_type=MESH)
            spread = pltpu.make_async_remote_copy(
                src_ref=whole, dst_ref=whole, send_sem=sems.at[6 + axis], recv_sem=sems.at[9 + axis],
                device_id={"dp": plan.d - plan.strides[axis]}, device_id_type=MESH)
            self.steps.append((n, c, tick, active, gather, spread, arriving.at[axis]))
            tick += n - 1
            active = both(active, c == n - 1)
        self.last = (tick, active)

    def serve(self, t):
        for n, c, start, active, gather, _, arriving in self.steps:
            @when(both(t == start + c, active))
            def _():
                @pl.when(c > 0)
                def _():
                    gather.wait_recv()
                    self.partial[...] += arriving[...]
                pl.when(c < n - 1)(gather.start)
        tick, active = self.last

        @when(both(t == tick, active))
        def _():
            self.whole[...] = self.partial[...]
        for n, c, start, active, _, spread, _ in self.steps[::-1]:
            @when(both(t == 2 * tick - start - c, active))
            def _():
                pl.when(c < n - 1)(spread.wait_recv)
                pl.when(c > 0)(spread.start)

    def finish(self):
        for n, c, _, active, gather, spread, _ in self.steps:
            @when(active)
            def _():
                pl.when(c < n - 1)(gather.wait_send)
                pl.when(c > 0)(spread.wait_send)


def weights_kernel(dims, tiles, total, left_ref, right_ref, extra_ref, small_ref, result, small_sum, held, landing, side,
                   left_buf, right_buf, partial, arriving, whole, load_sem, send_sem, recv_sem, own_sem, small_sem):
    plan = Plan(dims, total)
    per = WIDTH // TILE
    met = greet(plan)

    def left_copy(s):
        job, part = lax.div(s, per), lax.rem(s, per)
        slab = jnp.where(job < 4, job, jnp.where(job < 8, 4, jnp.minimum(job - 3, 7)))
        return pltpu.make_async_copy(
            left_ref.at[:, pl.ds(pl.multiple_of(slab * WIDTH + part * TILE, TILE), TILE)],
            left_buf, load_sem.at[0])

    def right_copy(job):
        slab = jnp.where(job < 4, 0, job - 3)
        return pltpu.make_async_copy(
            right_ref.at[:, pl.ds(pl.multiple_of(slab * WIDTH, WIDTH), WIDTH)],
            right_buf, load_sem.at[1])

    def product(s):
        left_copy(s).wait()
        @pl.when(lax.rem(s, per) == 0)
        def _():
            right_copy(lax.div(s, per)).wait()
        held[s] = lax.dot_general(
            left_buf[...], right_buf[...], (((0,), (0,)), ((), ())),
            preferred_element_type=jnp.float32).astype(jnp.bfloat16)
        @pl.when(s + 1 < tiles)
        def _():
            left_copy(s + 1).start()
            @pl.when(lax.rem(s + 1, per) == 0)
            def _():
                right_copy(lax.div(s + 1, per)).start()

    extras = pltpu.make_async_copy(extra_ref, held.at[pl.ds(tiles, total - tiles)], load_sem.at[2])
    left_copy(0).start()
    right_copy(0).start()
    extras.start()
    product(0)
    met()
    extras.wait()
    refs = (held, landing, side, result, send_sem, recv_sem)

    def tick(steady, t, _):
        serve(plan, (1, 0, 2, 3), t, refs, own_sem, steady)
        @pl.when(t + 1 < tiles)
        def _():
            product(t + 1)
        return 0

    small = Small(plan, partial, arriving, whole, small_sem)
    partial[...] = small_ref[...]

    def first_tick(t, _):
        small.serve(t)
        return tick(False, t, 0)

    lax.fori_loop(0, plan.depth, first_tick, 0)
    small.serve(plan.depth)
    small.finish()
    small_sum[...] = whole[...]
    lax.fori_loop(plan.depth, total, functools.partial(tick, True), 0)
    lax.fori_loop(total, total + plan.depth, functools.partial(tick, False), 0)

    def finish(t, _):
        serve(plan, range(len(SHARES)), t, refs, own_sem, False, True)
        return 0

    lax.fori_loop(0, total + plan.depth, finish, 0)


def semaphores(dims, total):
    streams = arrivals = owns = 0
    for _, _, axis, orders, middle in SHARES:
        for parity, order in enumerate(orders):
            turns = total if len(orders) == 1 else (total + 1 - parity) // 2
            owns += turns
            for line in order:
                lanes = lanes_of(dims[line], False)
                streams, arrivals = streams + 2 * lanes, arrivals + 2 * lanes * turns
        lanes = lanes_of(dims[axis], middle and dims[axis] > 2)
        streams, arrivals = streams + 2 * lanes, arrivals + 2 * lanes * total
    return streams, arrivals, owns


def weight_sums(dims, lefts, rights, extras, small, cid):
    tiles = 12 * (WIDTH // TILE)
    total = tiles + extras.shape[0]
    rows = lefts.shape[0]
    streams, arrivals, owns = semaphores(dims, total)
    any_space = pl.BlockSpec(memory_space=pl.ANY)
    vmem = pl.BlockSpec(memory_space=pltpu.VMEM)
    return pl.pallas_call(
        functools.partial(weights_kernel, dims, tiles, total),
        out_shape=(jax.ShapeDtypeStruct((total, TILE, WIDTH), jnp.bfloat16),
                   jax.ShapeDtypeStruct(small.shape, jnp.float32)),
        in_specs=[any_space] * 3 + [vmem],
        out_specs=(any_space, vmem),
        scratch_shapes=[
            pltpu.VMEM((total, TILE, WIDTH), jnp.bfloat16),
            pltpu.VMEM((total, TILE, WIDTH), jnp.bfloat16),
            pltpu.VMEM((total, MIDDLE_ROWS, WIDTH), jnp.bfloat16),
            pltpu.VMEM((rows, TILE), jnp.bfloat16),
            pltpu.VMEM((rows, WIDTH), jnp.bfloat16),
            pltpu.VMEM(small.shape, jnp.float32),
            pltpu.VMEM((3,) + small.shape, jnp.float32),
            pltpu.VMEM(small.shape, jnp.float32),
            pltpu.SemaphoreType.DMA((3,)),
            pltpu.SemaphoreType.DMA((streams, RING)),
            pltpu.SemaphoreType.DMA((arrivals,)),
            pltpu.SemaphoreType.DMA((owns,)),
            pltpu.SemaphoreType.DMA((12,)),
        ],
        compiler_params=pltpu.CompilerParams(collective_id=cid, has_side_effects=True, vmem_limit_bytes=63 * 2**20),
        cost_estimate=pl.CostEstimate(flops=2 * 12 * rows * WIDTH * WIDTH, bytes_accessed=100 * 2**20, transcendentals=0),
    )(lefts, rights, extras, small)


HEADS = 8
CHUNK = 1024
LOW = jnp.bfloat16
WIDE = jnp.float32
NN = (((1,), (0,)), ((), ()))
NT = (((1,), (1,)), ((), ()))
TN = (((0,), (0,)), ((), ()))


def dot(a, b, form):
    return lax.dot_general(a, b, form, preferred_element_type=WIDE)


def normalize(values):
    center = values - jnp.mean(values, -1, keepdims=True)
    inverse = lax.rsqrt(jnp.mean(center * center, -1, keepdims=True) + 1e-05)
    return center * inverse, inverse


def norm_back(upstream, gain, xhat, inverse):
    scaled = upstream * gain
    return inverse * (scaled - jnp.mean(scaled, -1, keepdims=True)
                      - xhat * jnp.mean(scaled * xhat, -1, keepdims=True))


def gelu_pair(u):
    c = 0.7978845608028654
    square = u * u
    t = jnp.tanh(u * (c + (c * 0.044715) * square))
    half = 0.5 * (1.0 + t)
    slope = half + (0.5 * u) * (1.0 - t * t) * (c + (3.0 * c * 0.044715) * square)
    return u * half, slope


def layers_kernel(groups, tokens, clip_frames, cotangent, embed, norm_params, w_qkv, w_out, w_up, w_down,
                  lefts, rights, sec_out, sec_grad, extra, sizes, g_params, params, g_embed,
                  qkv_w, out_w, up_w, down_w, emb, src, upstream, qkv, probs, slopes, xhat_f, stats,
                  keep, passed, acc, hid, u_buf,
                  w_sem, in_sem, left_sem, right_sem, wide_sem, send_sem, recv_sem):
    section = lax.axis_index("section")
    first = section == 0
    other = 1 - section
    slots, width = emb.shape
    units = up_w.shape[1]
    steps = units // CHUNK
    head = width // HEADS
    scale = head ** -0.5

    loads = [pltpu.make_async_copy(a, b, w_sem.at[k]) for k, (a, b) in enumerate(
        ((w_qkv, qkv_w), (w_out, out_w), (w_up, up_w), (w_down, down_w), (embed, emb), (norm_params, params)))]
    loads[4].start()
    loads[5].start()
    loads[0].start()

    def token_load(g):
        return pltpu.make_async_copy(tokens.at[g], src.at[g], in_sem.at[g])

    def cot_load(g):
        return pltpu.make_async_copy(cotangent.at[g], upstream.at[g], in_sem.at[groups + g])

    @pl.when(first)
    def _():
        for g in range(groups):
            token_load(g).start()
    for k in (1, 2, 3):
        loads[k].start()

    barrier = pltpu.get_barrier_semaphore()
    pl.semaphore_signal(barrier, inc=1, device_id={"section": other}, device_id_type=MESH)
    pl.semaphore_wait(barrier, 1)

    def relay(g):
        return pltpu.make_async_remote_copy(
            src_ref=passed, dst_ref=src.at[g], send_sem=send_sem.at[g], recv_sem=recv_sem.at[g],
            device_id={"section": other}, device_id_type=MESH)

    def relay_back(g):
        return pltpu.make_async_remote_copy(
            src_ref=passed, dst_ref=upstream.at[g], send_sem=send_sem.at[groups + g],
            recv_sem=recv_sem.at[groups + g], device_id={"section": other}, device_id_type=MESH)

    def rows_of(g):
        return pl.ds(pl.multiple_of(g * slots, slots), slots)

    def cols(i, w=CHUNK):
        return pl.ds(pl.multiple_of(i * w, w), w)

    def left_store(g, k):
        return pltpu.make_async_copy(
            keep.at[:, pl.ds((k - 1) * width, width)], lefts.at[rows_of(g), pl.ds(units + (k - 1) * width, width)], left_sem.at[k])

    def right_store(g, k):
        if k == 0:
            return pltpu.make_async_copy(upstream.at[g], rights.at[rows_of(g), pl.ds(0, width)], right_sem.at[0])
        return pltpu.make_async_copy(
            keep.at[:, pl.ds((k - 2) * width, width)],
            rights.at[rows_of(g), pl.ds(width + units + (k - 2) * width, width)], right_sem.at[k])

    def left_chunk(g, i):
        return pltpu.make_async_copy(
            upstream.at[i], lefts.at[rows_of(g), pl.ds(i * CHUNK, CHUNK)], left_sem.at[5 + i])

    def right_chunk(g, i):
        return pltpu.make_async_copy(
            slopes.at[g, :, pl.ds(i * CHUNK, CHUNK)],
            rights.at[rows_of(g), pl.ds(width + i * CHUNK, CHUNK)], right_sem.at[6 + i])

    def out_store(g):
        return pltpu.make_async_copy(acc, sec_out.at[g], wide_sem.at[0])

    def grad_store(g):
        return pltpu.make_async_copy(acc, sec_grad.at[g], wide_sem.at[1])

    def base_of(g):
        return jnp.where(first, 0.0, src[g].astype(WIDE)) + emb[...].astype(WIDE)

    stage = pl.when(section >= 0)

    def heads_of(g, h):
        return tuple(qkv[g, :, k * width + h * head:k * width + (h + 1) * head] for k in range(3))

    def forward(g):
        @pl.when(first)
        def _():
            token_load(g).wait()
        @pl.when(section == 1)
        def _():
            relay(g).wait_recv()

        @stage
        def _():
            @pl.when(g == 0)
            def _():
                loads[4].wait()
                loads[5].wait()

            @pl.when(g > 0)
            def _():
                for k in (3, 4):
                    left_store(g - 1, k).wait()
            source = src[g].astype(WIDE)
            xhat, inverse = normalize(source)
            stats[g, :, 0:1] = inverse
            stats[g, :, 3:4] = jnp.mean(source, -1, keepdims=True)
            keep[:, 3 * width:4 * width] = (xhat * params[2:3] + params[3:4]).astype(LOW)
            @pl.when(g == 0)
            def _():
                loads[0].wait()
            for k, rows in ((1, 3), (2, 3)):
                part = slice(k * width, (k + 1) * width)
                qkv[g, :, part] = dot(keep[:, rows * width:(rows + 1) * width], qkv_w[:, part], NN).astype(LOW)
            base = base_of(g)
            xhat, inverse = normalize(base)
            stats[g, :, 1:2] = inverse
            stats[g, :, 4:5] = jnp.mean(base, -1, keepdims=True)
            keep[:, 2 * width:3 * width] = (xhat * params[0:1] + params[1:2]).astype(LOW)
            qkv[g, :, 0:width] = dot(keep[:, 2 * width:3 * width], qkv_w[:, 0:width], NN).astype(LOW)
            left_store(g, 3).start()
            left_store(g, 4).start()

        @stage
        def _():
            @pl.when(g > 0)
            def _():
                for k in (1, 2):
                    left_store(g - 1, k).wait()
            limit = jnp.where(first, clip_frames[g] * (slots // 16), slots)
            seen = lax.broadcasted_iota(jnp.int32, (1, slots), 1) < limit
            for h in range(HEADS):
                q, k, v = heads_of(g, h)
                s = jnp.where(seen, dot(q, k, NT) * scale, -1e30)
                e = jnp.exp(s - jnp.max(s, -1, keepdims=True))
                p = (e / jnp.sum(e, -1, keepdims=True)).astype(LOW)
                probs[g, h] = p
                keep[:, width + h * head:width + (h + 1) * head] = dot(p, v, NN).astype(LOW)
            left_store(g, 2).start()
            @pl.when(g == 0)
            def _():
                loads[1].wait()

        @stage
        def _():
            hid[...] = dot(keep[:, width:2 * width], out_w[...], NN)
            hidden = base_of(g) + hid[...]
            hid[...] = hidden
            xhat, inverse = normalize(hidden)
            stats[g, :, 2:3] = inverse
            xhat_f[g] = xhat.astype(LOW)
            keep[:, 0:width] = (xhat * params[4:5] + params[5:6]).astype(LOW)
            left_store(g, 1).start()
            @pl.when(g == 0)
            def _():
                loads[2].wait()
                loads[3].wait()

            @pl.when(g > 0)
            def _():
                out_store(g - 1).wait()
                for i in range(steps):
                    left_chunk(g - 1, i).wait()

        @stage
        def _():
            chunks = [slice(i * CHUNK, (i + 1) * CHUNK) for i in range(steps)]
            u_buf[0] = dot(keep[:, 0:width], up_w[:, chunks[0]], NN)
            for i, part in enumerate(chunks):
                if i + 1 < steps:
                    u_buf[(i + 1) % 2] = dot(keep[:, 0:width], up_w[:, chunks[i + 1]], NN)
                value, slope = gelu_pair(u_buf[i % 2])
                slopes[g, :, part] = slope.astype(LOW)
                value = value.astype(LOW)
                upstream[i] = value
                term = dot(value, down_w[part, :], NN)
                if i == 0:
                    acc[...] = hid[...] + term
                else:
                    acc[...] += term
            for i in range(steps):
                left_chunk(g, i).start()
            out_store(g).start()

        @pl.when(first)
        def _():
            @pl.when(g > 0)
            def _():
                relay(g - 1).wait_send()
                @pl.when(g == groups - 1)
                def _():
                    for i in range(steps):
                        left_chunk(g, i).wait()
            passed[...] = acc[...].astype(LOW)
            relay(g).start()

    pl.loop(0, groups)(forward)

    for k in range(1, 5):
        left_store(groups - 1, k).wait()
    out_store(groups - 1).wait()

    @pl.when(first)
    def _():
        relay(groups - 1).wait_send()

    @pl.when(section == 1)
    def _():
        for i in range(steps):
            left_chunk(groups - 1, i).wait()
        for g in range(groups):
            cot_load(g).start()

    g_params[...] = jnp.zeros_like(g_params)
    g_embed[...] = jnp.zeros_like(g_embed)

    def gains(row, e, xhat):
        g_params[row:row + 1] += jnp.sum(e * xhat, axis=0, keepdims=True)
        g_params[row + 1:row + 2] += jnp.sum(e, axis=0, keepdims=True)

    def backward(g):
        @pl.when(first)
        def _():
            relay_back(g).wait_recv()
        @pl.when(section == 1)
        def _():
            cot_load(g).wait()

        @stage
        def _():
            @pl.when(g > 0)
            def _():
                for k in (2, 3, 4, 5):
                    right_store(g - 1, k).wait()
                right_store(g - 1, 0).wait()
                for i in range(steps):
                    right_chunk(g - 1, i).wait()
                grad_store(g - 1).wait()
            right_store(g, 0).start()
            chunks = [slice(i * CHUNK, (i + 1) * CHUNK) for i in range(steps)]
            u_buf[0] = dot(upstream[g], down_w[chunks[0], :], NT)
            for i, part in enumerate(chunks):
                if i + 1 < steps:
                    u_buf[(i + 1) % 2] = dot(upstream[g], down_w[chunks[i + 1], :], NT)
                value = (u_buf[i % 2] * slopes[g, :, part].astype(WIDE)).astype(LOW)
                slopes[g, :, part] = value
                term = dot(value, up_w[:, part], NT)
                if i == 0:
                    acc[...] = term
                else:
                    acc[...] += term

        @stage
        def _():
            for i in range(steps):
                right_chunk(g, i).start()
            e = acc[...]
            xhat = xhat_f[g].astype(WIDE)
            gains(4, e, xhat)
            grad_hidden = upstream[g].astype(WIDE) + norm_back(e, params[4:5], xhat, stats[g, :, 2:3])
            hid[...] = grad_hidden
            keep[:, 0:width] = grad_hidden.astype(LOW)
            xhat_f[g] = dot(keep[:, 0:width], out_w[...], NT).astype(LOW)

        @stage
        def _():
            for h in range(HEADS):
                q, k, v = heads_of(g, h)
                m = xhat_f[g, :, h * head:(h + 1) * head]
                low = probs[g, h]
                p = low.astype(WIDE)
                gp = dot(m, v, NT)
                ds = (p * (gp - jnp.sum(gp * p, -1, keepdims=True))).astype(LOW)
                keep[:, width + h * head:width + (h + 1) * head] = (dot(ds, k, NN) * scale).astype(LOW)
                keep[:, 2 * width + h * head:2 * width + (h + 1) * head] = (dot(ds, q, TN) * scale).astype(LOW)
                keep[:, 3 * width + h * head:3 * width + (h + 1) * head] = dot(low, m, TN).astype(LOW)
            for k in (2, 3, 4, 5):
                right_store(g, k).start()

        @stage
        def _():
            acc[...] = dot(keep[:, width:2 * width], qkv_w[:, 0:width], NT)
            u_buf[0] = dot(keep[:, 2 * width:4 * width], qkv_w[:, width:3 * width], NT)
            e = acc[...]
            xhat = (base_of(g) - stats[g, :, 4:5]) * stats[g, :, 1:2]
            gains(0, e, xhat)
            grad_base = hid[...] + norm_back(e, params[0:1], xhat, stats[g, :, 1:2])
            g_embed[...] += grad_base
            hid[...] = grad_base

        @stage
        def _():
            e = u_buf[0]
            xhat = (src[g].astype(WIDE) - stats[g, :, 3:4]) * stats[g, :, 0:1]
            gains(2, e, xhat)
            acc[...] = norm_back(e, params[2:3], xhat, stats[g, :, 0:1])

        @pl.when(section == 1)
        def _():
            @pl.when(g > 0)
            def _():
                relay_back(g - 1).wait_send()
            low = (acc[...] + hid[...]).astype(LOW)
            passed[...] = low
            relay_back(g).start()
            acc[...] = low.astype(WIDE)
        grad_store(g).start()
        total = acc[...]
        total = jnp.sum(jnp.sum(total * total, axis=0, keepdims=True), axis=1, keepdims=True)
        sizes[pl.ds(g, 1), :] = jnp.broadcast_to(
            jnp.sqrt(total / (slots * width) + 1e-06), (1, sizes.shape[1]))

    pl.loop(0, groups)(backward)

    for k in (0, 2, 3, 4, 5):
        right_store(groups - 1, k).wait()
    for i in range(steps):
        right_chunk(groups - 1, i).wait()
    grad_store(groups - 1).wait()

    g_params[6:7] = jnp.broadcast_to(jnp.sum(sizes[:, 0:1], axis=0, keepdims=True), (1, width))
    keep[:, 0:width] = g_embed[...].astype(LOW)
    pltpu.make_async_copy(keep.at[:, pl.ds(0, width)], extra.at[0], right_sem.at[0]).start()
    pltpu.make_async_copy(keep.at[:, pl.ds(0, width)], extra.at[0], right_sem.at[0]).wait()

    @pl.when(section == 1)
    def _():
        relay_back(groups - 1).wait_send()


def layers(tokens, clip_frames, cotangent, embed, norm_params, w_qkv, w_out, w_up, w_down, cid):
    groups, slots, width = tokens.shape
    units = w_up.shape[1]
    rows = groups * slots
    hbm = pl.BlockSpec(memory_space=pl.ANY)
    vmem = pl.BlockSpec(memory_space=pltpu.VMEM)
    shape = jax.ShapeDtypeStruct
    return pl.pallas_call(
        functools.partial(layers_kernel, groups),
        out_shape=(
            shape((rows, units + 4 * width), LOW),
            shape((rows, units + 5 * width), LOW),
            shape((groups, slots, width), WIDE),
            shape((groups, slots, width), WIDE),
            shape((1, slots, width), LOW),
            shape((groups, 128), WIDE),
            shape((8, width), WIDE),
        ),
        in_specs=[hbm, pl.BlockSpec(memory_space=pltpu.SMEM)] + [hbm] * 7,
        out_specs=(hbm, hbm, hbm, hbm, hbm, vmem, vmem),
        scratch_shapes=[
            pltpu.VMEM(norm_params.shape, WIDE),
            pltpu.VMEM((slots, width), WIDE),
            pltpu.VMEM(w_qkv.shape, LOW),
            pltpu.VMEM(w_out.shape, LOW),
            pltpu.VMEM(w_up.shape, LOW),
            pltpu.VMEM(w_down.shape, LOW),
            pltpu.VMEM((slots, width), LOW),
            pltpu.VMEM((groups, slots, width), LOW),
            pltpu.VMEM((max(groups, units // CHUNK), slots, width), LOW),
            pltpu.VMEM((groups, slots, 3 * width), LOW),
            pltpu.VMEM((groups, HEADS, slots, slots), LOW),
            pltpu.VMEM((groups, slots, units), LOW),
            pltpu.VMEM((groups, slots, width), LOW),
            pltpu.VMEM((groups, slots, 128), WIDE),
            pltpu.VMEM((slots, 4 * width), LOW),
            pltpu.VMEM((slots, width), LOW),
            pltpu.VMEM((slots, width), WIDE),
            pltpu.VMEM((slots, width), WIDE),
            pltpu.VMEM((2, slots, CHUNK), WIDE),
            pltpu.SemaphoreType.DMA((6,)),
            pltpu.SemaphoreType.DMA((2 * groups,)),
            pltpu.SemaphoreType.DMA((5 + units // CHUNK,)),
            pltpu.SemaphoreType.DMA((6 + units // CHUNK,)),
            pltpu.SemaphoreType.DMA((2,)),
            pltpu.SemaphoreType.DMA((2 * groups,)),
            pltpu.SemaphoreType.DMA((2 * groups,)),
        ],
        compiler_params=pltpu.CompilerParams(
            collective_id=cid, has_side_effects=True, vmem_limit_bytes=63 * 2**20),
        cost_estimate=pl.CostEstimate(flops=54 * 10**9, bytes_accessed=120 * 2**20, transcendentals=10**7),
    )(tokens, clip_frames, cotangent, embed, norm_params, w_qkv, w_out, w_up, w_down)


DEEP = 4


def widen_kernel(places, count, sums, sizes, shared, first, second, *refs):
    outs, (embed, params, norms, first_out, second_out, narrow, wide, held, read_sem, write_sem, pass_sem) = (
        refs[:len(places)], refs[len(places):])
    coming = [pltpu.make_async_copy(a, held.at[k], pass_sem.at[k]) for k, a in enumerate((first, second))]
    going = [pltpu.make_async_copy(held.at[k], a, pass_sem.at[2 + k]) for k, a in enumerate((first_out, second_out))]
    steps = places[-1][0] + places[-1][1]
    tall, width = wide.shape[1:]

    def read(i):
        slot = lax.rem(i, DEEP)
        return pltpu.make_async_copy(sums.at[pl.ds(2 * i, 2)], narrow.at[slot], read_sem.at[slot])

    for i in range(DEEP):
        read(i).start()
    for copy in coming:
        copy.start()

    for (start, number, down, across), out in zip(places, outs):
        def write(i):
            slot, k = lax.rem(i, DEEP), i - start
            rows = pl.ds(pl.multiple_of(lax.rem(k, down) * tall, tall), tall)
            cols = pl.ds(pl.multiple_of(lax.div(k, down) * width, width), width)
            return pltpu.make_async_copy(wide.at[slot], out.at[rows, cols], write_sem.at[slot])

        if start == places[1][0]:
            for copy in coming:
                copy.wait()
            for copy in going:
                copy.start()

        @pl.loop(start, start + number)
        def _(i):
            slot = lax.rem(i, DEEP)
            read(i).wait()
            @pl.when(i >= DEEP)
            def _():
                write(i).wait()
            wide[slot] = narrow[slot].reshape(tall, width).astype(WIDE)
            write(i).start()
            @pl.when(i + DEEP < steps)
            def _():
                read(i + DEEP).start()

    tail = pltpu.make_async_copy(sums.at[2 * steps], narrow.at[0, 0], read_sem.at[0])
    tail.start()
    params[...] = shared[0:6]
    mean = shared[6:7, 0:1] / count
    here = jnp.zeros(norms.shape, WIDE)
    for g in range(norms.shape[1]):
        lane = lax.broadcasted_iota(jnp.int32, norms.shape, 1) == g
        here = jnp.where(lane, sizes[g:g + 1, 0:1] / mean, here)
    norms[...] = here
    tail.wait()
    embed[...] = narrow[0, 0].astype(WIDE)
    for i in range(steps - DEEP, steps):
        write(i).wait()
    for copy in going:
        copy.wait()


def widen(sums, sizes, shared, first, second, count, places):
    tile, width = sums.shape[1:]
    steps = sum(p[1] for p in places)
    shape = jax.ShapeDtypeStruct
    hbm, vmem = pl.BlockSpec(memory_space=pl.ANY), pl.BlockSpec(memory_space=pltpu.VMEM)
    return pl.pallas_call(
        lambda *refs: widen_kernel(places, count, *refs),
        out_shape=tuple(shape((p[2] * 2 * tile, p[3] * width), WIDE) for p in places)
        + (shape((tile, width), WIDE), shape((6, width), WIDE), shape((1, sizes.shape[0]), WIDE),
           shape(first.shape, WIDE), shape(second.shape, WIDE)),
        in_specs=[hbm, vmem, vmem, hbm, hbm],
        out_specs=(hbm,) * len(places) + (vmem,) * 3 + (hbm,) * 2,
        scratch_shapes=[
            pltpu.VMEM((DEEP, 2, tile, width), LOW),
            pltpu.VMEM((DEEP, 2 * tile, width), WIDE),
            pltpu.VMEM((2,) + first.shape, WIDE),
            pltpu.SemaphoreType.DMA((DEEP,)),
            pltpu.SemaphoreType.DMA((DEEP,)),
            pltpu.SemaphoreType.DMA((4,)),
        ],
        compiler_params=pltpu.CompilerParams(vmem_limit_bytes=62 * 2**20),
        cost_estimate=pl.CostEstimate(flops=0, bytes_accessed=12 * steps * tile * width, transcendentals=0),
    )(sums, sizes, shared, first, second)


def body(tokens, clip_frames, cotangent, embed, norm_params, w_qkv, w_out, w_up, w_down):
    groups = tokens.shape[0]
    devices = lax.axis_size("dp")
    lefts, rights, outcome, grad_inputs, extra, sizes, g_params = layers(
        tokens, clip_frames, cotangent, embed[0], norm_params[0], w_qkv[0], w_out[0], w_up[0], w_down[0], 2
    )
    sums, shared = weight_sums(lines_of(devices), lefts, rights, extra, g_params, 1)
    down, up, out, qkv, g_embed, g_params, norms, outcome, grad_inputs = widen(
        sums, sizes, shared, outcome, grad_inputs, groups * devices, ((0, 8, 8, 1), (8, 8, 2, 4), (16, 2, 2, 1), (18, 6, 2, 3))
    )
    return (
        outcome[None],
        grad_inputs[None],
        qkv[None],
        out[None],
        up[None],
        down[None],
        g_params[None],
        g_embed[None],
        norms,
    )


def solution(mesh):
    placed = (
        P("dp", None, None),
        P("dp"),
        P("dp", None, None),
        P("section", None, None),
        P("section", None, None),
        P("section", None, None),
        P("section", None, None),
        P("section", None, None),
        P("section", None, None),
    )
    return jax.shard_map(
        body,
        mesh=mesh,
        in_specs=placed,
        out_specs=(
            P("section", "dp", None, None),
            P("section", "dp", None, None),
            P("section", None, None),
            P("section", None, None),
            P("section", None, None),
            P("section", None, None),
            P("section", None, None),
            P("section", None, None),
            P("section", "dp"),
        ),
        check_vma=False,
    )
```
